32 devices in a mesh: dp: 16 (over z, y, x), tensor: 2 (over core).
Axes of the slice: x: 2, y: 2, z: 4, core: 2. Of those that a mesh axis runs over, the one named last changes fastest.
Arguments:
- tokens: bfloat16 [4096, 2048], P(('dp', 'tensor')), may hold values from -6 to 6
- norm1_gain: bfloat16 [2048], P('dp'), may hold values from 0.099609375 to 1.8984375
- qkv_weight: bfloat16 [2048, 3, 2048], P('dp', None, 'tensor'), may hold values from -0.125 to 0.125
- out_weight: bfloat16 [2048, 2048], P('dp', 'tensor'), may hold values from -0.5 to 0.5
- norm2_gain: bfloat16 [2048], P('dp'), may hold values from 0.099609375 to 1.8984375
- gate_up_weight: bfloat16 [2048, 2, 5632], P('dp', None, 'tensor'), may hold values from -0.125 to 0.125
- down_weight: bfloat16 [2048, 5632], P('dp', 'tensor'), may hold values from -0.078125 to 0.078125
- doc_lengths: int32 [16, 8], P('dp'), may hold values from 1 to 128, 256 in all within a row
- cotangent: bfloat16 [4096, 2048], P(('dp', 'tensor')), may hold values from -6 to 6
Outputs:
- output: bfloat16 [4096, 2048], P(('dp', 'tensor'))
- input_grad: bfloat16 [4096, 2048], P(('dp', 'tensor'))
- norm1_gain_grad: float32 [2048], P('dp')
- qkv_grad: float32 [2048, 3, 2048], P('dp', None, 'tensor')
- out_grad: float32 [2048, 2048], P('dp', 'tensor')
- norm2_gain_grad: float32 [2048], P('dp')
- gate_up_grad: float32 [2048, 2, 5632], P('dp', None, 'tensor')
- down_grad: float32 [2048, 5632], P('dp', 'tensor')
The draws below stay inside these ranges and needn't reach their ends.
Inputs may be any that keep to these rules, and one draw needn't show every extreme that they name: `doc_lengths`: in every packed row the 8 lengths sum to 256, and the longest is 128.
All inputs are finite; a program needn't handle non-finite values.
Results may differ from the reference program's by a relative error of at most 0.014.
Values may be sent and summed in bfloat16 or wider, within the bound.
No kernel may reach another device: no remote copies, remote signals or barrier semaphores. Data moves between devices by JAX's collectives and lax.ppermute only.
A program may use at most 256 MiB of HBM per device.

```python
import math
import jax
import jax.numpy as jnp
import numpy as np
from jax import lax

D = 2048
HEADS = 16
HEAD_DIM = 128
FF = 5632
DOCS = 8
ROW = 256
MOST = 128
TOKENS = 4096
N_DP = 16


def spiked(result, key, source, target, parts, factor):
    def block_of(position):
        return (jnp.arange(result.shape[position]) // (result.shape[position] // parts)).reshape((-1,) + (1,) * (result.ndim - 1 - position))

    near = jax.random.permutation(key, parts)[block_of(target)]
    second = (block_of(target) + parts // 2) % parts
    return jnp.where((block_of(source) == near) | (block_of(source) == second), factor * result, result)


def block_scale(own_key, shape, cuts, least, largest):
    loudness, own = 1.0, jax.random.fold_in(own_key, 6)
    for position, parts in cuts:
        draws = jnp.exp(jax.random.uniform(jax.random.fold_in(own, position), (parts,), jnp.float32, least / len(cuts), largest / len(cuts)))
        loudness = loudness * jnp.repeat(draws, shape[position] // parts).reshape([-1 if axis == position else 1 for axis in range(len(shape))])
    return loudness


def split_up(number_of, total, limit, lean):
    weights = [(1 << 20) // math.isqrt(grade ** lean) + 1 for grade in range(2, number_of + 1)]
    surplus, holding = total - limit - (number_of - 1), [1] * (number_of - 1)
    while surplus > 0:
        free = [i for i in range(number_of - 1) if holding[i] < limit]
        whole, remaining = sum([weights[i] for i in free]), surplus
        for i in free:
            more = min(limit - holding[i], max(1, remaining * weights[i] // whole), surplus)
            holding[i] = holding[i] + more
            surplus = surplus - more
    return np.array([limit] + holding)


def uneven(rng, count, total, bound, lean):
    if count == 2:
        one = jax.random.randint(rng, (), max(1, total - bound), min(bound, total - 1) + 1)
        return jnp.stack([one, total - one])
    tallies = jnp.asarray(split_up(count, total, bound, lean), jnp.int32)
    couples = (count - 1) // 2
    donor, receiver = tallies[1:1 + 2 * couples:2], tallies[2:2 + 2 * couples:2]
    room = jnp.minimum(donor - 1, bound - receiver)
    shifted = jax.random.randint(jax.random.fold_in(rng, 1), (couples,), 0, 1 << 20) % (room + 1)
    tallies = tallies.at[1:1 + 2 * couples:2].set(donor - shifted).at[2:2 + 2 * couples:2].set(receiver + shifted)
    return tallies[jax.random.permutation(jax.random.fold_in(rng, 2), count)]


def normal_values(key, extent, scale, bound, cuts=(), kind=jnp.bfloat16):
    result = scale * jax.random.normal(key, extent, jnp.float32)
    if cuts:
        result = result * block_scale(key, extent, cuts, -0.22, 0.18)
    return jnp.clip(result, -bound, bound).astype(kind)


def bell_draw_with(stream_key, dims, width, bound, cuts, heavy, kind=jnp.bfloat16):
    values = width * jax.random.normal(stream_key, dims, jnp.float32)
    if cuts:
        values = values * block_scale(stream_key, dims, cuts, -0.22, 0.18)
    return jnp.clip(spiked(values, jax.random.fold_in(stream_key, 3), *heavy), -bound, bound).astype(kind)


def setup_inputs(seed: int = 0) -> dict:
    key_list = jax.random.split(jax.random.key(seed), 10)
    return {
        "tokens": bell_draw_with(key_list[0], (TOKENS, D), 1.0, 6.0, ((0, 32),), (0, 1, 32, 2.75)),
        "norm1_gain": jnp.clip(1.0 + 0.18 * jax.random.normal(key_list[1], (D,), jnp.float32), 0.099609375, 1.8984375).astype(jnp.bfloat16),
        "qkv_weight": normal_values(key_list[2], (D, 3, D), D ** -0.5, 0.125, ((0, 16), (2, 2))),
        "out_weight": normal_values(key_list[3], (D, D), (D // 16) ** -0.5, 0.5, ((0, 16), (1, 2))),
        "norm2_gain": jnp.clip(1.0 + 0.18 * jax.random.normal(key_list[4], (D,), jnp.float32), 0.099609375, 1.8984375).astype(jnp.bfloat16),
        "gate_up_weight": normal_values(key_list[5], (D, 2, FF), D ** -0.5, 0.125, ((0, 16), (2, 2))),
        "down_weight": normal_values(key_list[6], (D, FF), FF ** -0.5, 0.078125, ((0, 16), (1, 2))),
        "doc_lengths": jax.vmap(lambda own: uneven(own, DOCS, ROW, MOST, 2))(jax.random.split(key_list[7], N_DP)).reshape((N_DP, DOCS)).astype(jnp.int32),
        "cotangent": bell_draw_with(key_list[8], (TOKENS, D), 1.0, 6.0, ((0, 32),), (0, 1, 32, 2.75)),
    }


@jax.custom_vjp
def low(v):
    return lax.optimization_barrier(v.astype(jnp.bfloat16)).astype(jnp.float32)

@jax.custom_vjp
def low_back(v):
    return v

def low_keep(v):
    return (low(v), None)

def low_pass(kept, grad):
    return (grad,)

def back_keep(v):
    return (v, None)

def back_low(kept, grad):
    return (low(grad),)
low.defvjp(low_keep, low_pass)
low_back.defvjp(back_keep, back_low)
EPS_NORM = 1e-05
MASKED_SCORE = -1e+30
HIGH = lax.Precision.HIGHEST

def doc_layout(lengths_row, row_count):
    ends_at = jnp.cumsum(lengths_row, dtype=jnp.int32)
    positions = jnp.arange(row_count, dtype=jnp.int32)
    passed = positions[:, None] >= ends_at[None, :]
    segment = lax.optimization_barrier(jnp.sum(passed.astype(jnp.int32), axis=1, dtype=jnp.int32))
    doc_start = lax.optimization_barrier(jnp.sum(jnp.where(passed, lengths_row[None, :], 0), axis=1, dtype=jnp.int32))
    offset = (positions - doc_start).astype(jnp.float32)
    allowed = (segment[:, None] == segment[None, :]) & (positions[:, None] >= positions[None, :])
    half_dim = HEAD_DIM // 2
    inverse = jnp.exp(jnp.arange(half_dim, dtype=jnp.float32) * (-2.0 * math.log(10000.0) / HEAD_DIM))
    angles = offset[:, None] * inverse[None, :]
    return (allowed, jnp.cos(angles), jnp.sin(angles))

def rotate(values, cosine, sine_part, sign):
    half_dim = values.shape[-1] // 2
    first_half = values[..., :half_dim]
    second = values[..., half_dim:]
    cos_wide = cosine[:, None, :]
    sin_wide = sign * sine_part[:, None, :]
    return jnp.concatenate([first_half * cos_wide - second * sin_wide, second * cos_wide + first_half * sin_wide], axis=-1)

def rms_scale(values):
    return lax.rsqrt(lax.optimization_barrier(jnp.mean(values * values, axis=-1, keepdims=True)) + EPS_NORM)

def forward(params_in, tokens_in, lengths_row):
    gain_one, qkv_w, out_w, gain_two, gate_up_w, down_w = params_in
    allowed, cosine, sine_part = doc_layout(lengths_row, ROW)
    shape3 = (ROW, HEADS, HEAD_DIM)
    normed_one = low(tokens_in * rms_scale(tokens_in) * gain_one)
    queries = low_back(jnp.dot(normed_one, qkv_w[:, 0, :], precision=HIGH))
    queries = low(rotate(queries.reshape(shape3), cosine, sine_part, 1.0))
    keys_rot = low_back(jnp.dot(normed_one, qkv_w[:, 1, :], precision=HIGH))
    keys_rot = low(rotate(keys_rot.reshape(shape3), cosine, sine_part, 1.0))
    values_in = low(low_back(jnp.dot(normed_one, qkv_w[:, 2, :], precision=HIGH))).reshape(shape3)
    scores = low_back(jnp.einsum('qhd,khd->hqk', queries, keys_rot, precision=HIGH)) * HEAD_DIM ** (-0.5)
    scores = jnp.where(allowed[None, :, :], scores, MASKED_SCORE)
    weights = low(jax.nn.softmax(scores, axis=-1))
    mixed = jnp.einsum('hqk,khd->qhd', weights, values_in, precision=HIGH).reshape(ROW, D)
    mixed = low_back(low(mixed))
    attn = low_back(jnp.dot(mixed, out_w.T, precision=HIGH))
    stream = tokens_in + attn
    normed_two = low(stream * rms_scale(stream) * gain_two)
    gate = low_back(jnp.dot(normed_two, gate_up_w[:, 0, :], precision=HIGH))
    upper = low_back(jnp.dot(normed_two, gate_up_w[:, 1, :], precision=HIGH))
    hidden = low(jax.nn.silu(gate) * upper)
    return stream + jnp.dot(hidden, down_w.T, precision=HIGH)

def reference(tokens, norm1_gain, qkv_weight, out_weight, norm2_gain, gate_up_weight, down_weight, doc_lengths, cotangent):
    params = tuple((arr.astype(jnp.float32) for arr in (norm1_gain, qkv_weight, out_weight, norm2_gain, gate_up_weight, down_weight)))
    rows_in = tokens.astype(jnp.float32).reshape(N_DP, ROW, D)
    rows_cot = cotangent.astype(jnp.float32).reshape(N_DP, ROW, D)

    def one_row(totals, pieces):
        row_in, cot_row, lengths_row = pieces
        out_row, pullback = jax.vjp(lambda params_in, tokens_in: forward(params_in, tokens_in, lengths_row), params, row_in)
        grads, dx_row = pullback(cot_row)
        totals = tuple((acc + grad for acc, grad in zip(totals, grads)))
        return (totals, (out_row.astype(jnp.bfloat16), dx_row.astype(jnp.bfloat16)))
    zero_sums = tuple((jnp.zeros_like(arr) for arr in params))
    totals, (out_rows, dx_rows) = lax.scan(one_row, zero_sums, (rows_in, rows_cot, doc_lengths))
    return (out_rows.reshape(TOKENS, D), dx_rows.reshape(TOKENS, D), totals[0], totals[1], totals[2], totals[3], totals[4], totals[5])
```

```python
import math

import jax
import jax.numpy as jnp
from jax import lax
from jax.sharding import PartitionSpec as P

HEAD_DIM = 128


EPS_NORM = 1e-05
MASKED_SCORE = -1e30


def doc_layout(lengths_row, row_count):
    docs = jnp.arange(lengths_row.shape[0], dtype=jnp.int32)
    ends_at = jnp.sum(
        jnp.where(docs[None, :] <= docs[:, None], lengths_row[None, :], 0), axis=1, dtype=jnp.int32
    )
    positions = jnp.arange(row_count, dtype=jnp.int32)
    passed = positions[:, None] >= ends_at[None, :]
    segment = jnp.sum(passed.astype(jnp.int32), axis=1, dtype=jnp.int32)
    doc_start = jnp.sum(jnp.where(passed, lengths_row[None, :], 0), axis=1, dtype=jnp.int32)
    offset = (positions - doc_start).astype(jnp.float32)
    allowed = (segment[:, None] == segment[None, :]) & (positions[:, None] >= positions[None, :])
    half_dim = HEAD_DIM // 2
    inverse = jnp.exp(
        jnp.arange(half_dim, dtype=jnp.float32) * (-2.0 * math.log(10000.0) / HEAD_DIM)
    )
    angles = offset[:, None] * inverse[None, :]
    return (allowed, jnp.cos(angles), jnp.sin(angles))


def rotate(values, cosine, sine_part, sign):
    half_dim = values.shape[-1] // 2
    first_half = values[..., :half_dim]
    second = values[..., half_dim:]
    cos_wide = cosine[:, None, :]
    sin_wide = sign * sine_part[:, None, :]
    return jnp.concatenate(
        [first_half * cos_wide - second * sin_wide, second * cos_wide + first_half * sin_wide],
        axis=-1,
    )


def rms_scale(values):
    return lax.rsqrt(jnp.mean(values * values, axis=-1, keepdims=True) + EPS_NORM)


def norm_back(grad_in, normed, scaling, gain_f32):
    gain_part = jnp.sum(grad_in * normed, axis=0)
    grad_normed = grad_in * gain_f32
    return (
        scaling * (grad_normed - normed * jnp.mean(grad_normed * normed, axis=-1, keepdims=True)),
        gain_part,
    )


def contract_rows(left, right):
    return lax.dot_general(
        left, right, (((0,), (0,)), ((), ())), preferred_element_type=jnp.float32
    )


def contract_last(left, right):
    return lax.dot_general(
        left, right, (((1,), (1,)), ((), ())), preferred_element_type=jnp.float32
    )


def head_scores(queries, keys_head, allowed, scaling):
    scores = contract_last(queries, keys_head) * scaling
    return jnp.where(allowed, scores, MASKED_SCORE)


def head_forward(pieces, allowed, scaling):
    queries, keys_head, values_head = pieces
    scores = head_scores(queries, keys_head, allowed, scaling)
    row_max = jnp.max(scores, axis=1, keepdims=True)
    exp_scores = jnp.exp(scores - row_max)
    row_total = jnp.sum(exp_scores, axis=1, keepdims=True)
    weights = (exp_scores / row_total).astype(jnp.bfloat16)
    mixed = jnp.dot(weights, values_head, preferred_element_type=jnp.float32).astype(jnp.bfloat16)
    return (mixed, (row_max + jnp.log(row_total))[:, 0])


def head_backward(pieces, allowed, scaling):
    queries, keys_head, values_head, grad_mixed, log_total = pieces
    scores = head_scores(queries, keys_head, allowed, scaling)
    probs = jnp.exp(scores - log_total[:, None])
    grad_values = contract_rows(probs.astype(jnp.bfloat16), grad_mixed).astype(jnp.bfloat16)
    grad_probs = contract_last(grad_mixed, values_head)
    delta_sum = jnp.sum(probs * grad_probs, axis=1, keepdims=True)
    grad_scores = (probs * (grad_probs - delta_sum) * scaling).astype(jnp.bfloat16)
    grad_queries = jnp.dot(grad_scores, keys_head, preferred_element_type=jnp.float32)
    grad_keys = contract_rows(grad_scores, queries)
    return (grad_queries, grad_keys, grad_values)


def shards(
    tokens,
    norm1_gain,
    qkv_weight,
    out_weight,
    norm2_gain,
    gate_up_weight,
    down_weight,
    doc_lengths,
    cotangent,
):
    row_dev = tokens.shape[0]
    row_count = row_dev * lax.axis_size("tensor")
    local_width = qkv_weight.shape[2]
    hidden_width = gate_up_weight.shape[2]
    heads_here = local_width // HEAD_DIM
    scaling = HEAD_DIM ** (-0.5)
    shape3 = (row_count, heads_here, HEAD_DIM)
    qkv_full, out_full, gain_one = (
        lax.all_gather(qkv_weight, "dp", axis=0, tiled=True),
        lax.all_gather(out_weight, "dp", axis=0, tiled=True),
        lax.all_gather(norm1_gain, "dp", axis=0, tiled=True),
    )
    gate_up_full, down_full, gain_two = (
        lax.all_gather(gate_up_weight, "dp", axis=0, tiled=True),
        lax.all_gather(down_weight, "dp", axis=0, tiled=True),
        lax.all_gather(norm2_gain, "dp", axis=0, tiled=True),
    )
    qkv_mat = qkv_full.reshape(qkv_full.shape[0], 3 * local_width)
    gate_up_mat = gate_up_full.reshape(gate_up_full.shape[0], 2 * hidden_width)
    gain_one = gain_one.astype(jnp.float32)
    gain_two = gain_two.astype(jnp.float32)
    allowed, cosine, sine_part = doc_layout(doc_lengths[0], row_count)
    residual = tokens.astype(jnp.float32)
    scale_one = rms_scale(residual)
    normed_one = residual * scale_one
    norm_out_one = (normed_one * gain_one).astype(jnp.bfloat16)
    rows_one = lax.all_gather(norm_out_one, "tensor", axis=0, tiled=True)
    projected = jnp.dot(rows_one, qkv_mat, preferred_element_type=jnp.float32)
    queries = rotate(projected[:, :local_width].reshape(shape3), cosine, sine_part, 1.0).astype(
        jnp.bfloat16
    )
    keys_rot = rotate(
        projected[:, local_width : 2 * local_width].reshape(shape3), cosine, sine_part, 1.0
    ).astype(jnp.bfloat16)
    values_all = projected[:, 2 * local_width :].reshape(shape3).astype(jnp.bfloat16)
    query_heads = jnp.swapaxes(queries, 0, 1)
    key_heads = jnp.swapaxes(keys_rot, 0, 1)
    value_heads = jnp.swapaxes(values_all, 0, 1)
    mixed_heads, log_totals = lax.map(
        lambda pieces: head_forward(pieces, allowed, scaling), (query_heads, key_heads, value_heads)
    )
    mixed_flat = jnp.swapaxes(mixed_heads, 0, 1).reshape(row_count, local_width)
    attn = lax.psum_scatter(
        contract_last(mixed_flat, out_full), "tensor", scatter_dimension=0, tiled=True
    )
    stream = residual + attn
    scale_two = rms_scale(stream)
    normed_two = stream * scale_two
    norm_out_two = (normed_two * gain_two).astype(jnp.bfloat16)
    rows_two = lax.all_gather(norm_out_two, "tensor", axis=0, tiled=True)
    gate_up = jnp.dot(rows_two, gate_up_mat, preferred_element_type=jnp.float32)
    gate = gate_up[:, :hidden_width]
    upper = gate_up[:, hidden_width:]
    sigma = jax.nn.sigmoid(gate)
    silu_gate = gate * sigma
    hidden = (silu_gate * upper).astype(jnp.bfloat16)
    mlp_out = lax.psum_scatter(
        contract_last(hidden, down_full).astype(jnp.bfloat16),
        "tensor",
        scatter_dimension=0,
        tiled=True,
    ).astype(jnp.float32)
    output = (stream + mlp_out).astype(jnp.bfloat16)
    cot_rows = lax.all_gather(cotangent, "tensor", axis=0, tiled=True)
    down_part = contract_rows(cot_rows, hidden)
    grad_hidden = jnp.dot(cot_rows, down_full, preferred_element_type=jnp.float32)
    grad_gate = (grad_hidden * upper * (sigma * (1.0 + gate * (1.0 - sigma)))).astype(jnp.bfloat16)
    grad_upper = (grad_hidden * silu_gate).astype(jnp.bfloat16)
    grad_gate_up = jnp.concatenate([grad_gate, grad_upper], axis=1)
    gate_up_part = contract_rows(rows_two, grad_gate_up)
    grad_norm_two = lax.psum_scatter(
        contract_last(grad_gate_up, gate_up_mat), "tensor", scatter_dimension=0, tiled=True
    )
    grad_from_two, gain_two_part = norm_back(grad_norm_two, normed_two, scale_two, gain_two)
    grad_stream = cotangent.astype(jnp.float32) + grad_from_two
    stream_rows = lax.all_gather(grad_stream.astype(jnp.bfloat16), "tensor", axis=0, tiled=True)
    out_part = contract_rows(stream_rows, mixed_flat)
    grad_mixed = jnp.dot(stream_rows, out_full, preferred_element_type=jnp.float32).astype(
        jnp.bfloat16
    )
    grad_mixed_heads = jnp.swapaxes(grad_mixed.reshape(shape3), 0, 1)
    grad_q_heads, grad_k_heads, grad_v_heads = lax.map(
        lambda pieces: head_backward(pieces, allowed, scaling),
        (query_heads, key_heads, value_heads, grad_mixed_heads, log_totals),
    )
    grad_queries = (
        rotate(jnp.swapaxes(grad_q_heads, 0, 1), cosine, sine_part, -1.0)
        .reshape(row_count, local_width)
        .astype(jnp.bfloat16)
    )
    grad_keys = (
        rotate(jnp.swapaxes(grad_k_heads, 0, 1), cosine, sine_part, -1.0)
        .reshape(row_count, local_width)
        .astype(jnp.bfloat16)
    )
    grad_values = jnp.swapaxes(grad_v_heads, 0, 1).reshape(row_count, local_width)
    grad_qkv = jnp.concatenate([grad_queries, grad_keys, grad_values], axis=1)
    qkv_part = contract_rows(rows_one, grad_qkv)
    grad_norm_one = lax.psum_scatter(
        contract_last(grad_qkv, qkv_mat), "tensor", scatter_dimension=0, tiled=True
    )
    grad_from_one, gain_one_part = norm_back(grad_norm_one, normed_one, scale_one, gain_one)
    input_grad = (grad_stream + grad_from_one).astype(jnp.bfloat16)
    qkv_flat, out_grad, gain_one_sum, gate_up_flat, down_grad, gain_two_sum = (
        lax.psum_scatter(qkv_part, "dp", scatter_dimension=0, tiled=True),
        lax.psum_scatter(out_part, "dp", scatter_dimension=0, tiled=True),
        lax.psum_scatter(gain_one_part, "dp", scatter_dimension=0, tiled=True),
        lax.psum_scatter(gate_up_part, "dp", scatter_dimension=0, tiled=True),
        lax.psum_scatter(down_part, "dp", scatter_dimension=0, tiled=True),
        lax.psum_scatter(gain_two_part, "dp", scatter_dimension=0, tiled=True),
    )
    qkv_grad = qkv_flat.reshape(qkv_flat.shape[0], 3, local_width)
    gate_up_grad = gate_up_flat.reshape(gate_up_flat.shape[0], 2, hidden_width)
    gain_one_grad, gain_two_grad = lax.psum((gain_one_sum, gain_two_sum), "tensor")
    return (
        output,
        input_grad,
        gain_one_grad,
        qkv_grad,
        out_grad,
        gain_two_grad,
        gate_up_grad,
        down_grad,
    )


def solution(mesh):
    placed = (
        P(("dp", "tensor"), None),
        P("dp"),
        P("dp", None, "tensor"),
        P("dp", "tensor"),
        P("dp"),
        P("dp", None, "tensor"),
        P("dp", "tensor"),
        P("dp", None),
        P(("dp", "tensor"), None),
    )
    return jax.shard_map(
        shards,
        mesh=mesh,
        in_specs=placed,
        out_specs=(
            P(("dp", "tensor"), None),
            P(("dp", "tensor"), None),
            P("dp"),
            P("dp", None, "tensor"),
            P("dp", "tensor"),
            P("dp"),
            P("dp", None, "tensor"),
            P("dp", "tensor"),
        ),
        check_vma=False,
    )
```

```python
import math

import jax
import jax.numpy as jnp
from jax import lax
from jax.sharding import PartitionSpec as P

HEAD_DIM = 128
EPS_NORM = 1e-05
MASKED_SCORE = -1e30
GROUP = 8
THIRDS = (0, 48, 88, 128)
BF = jnp.bfloat16
F32 = jnp.float32


def over_dp(x, bit):
    size = lax.axis_size("dp")
    return lax.ppermute(x, "dp", [(i, i ^ bit) for i in range(size)])


def over_cores(x):
    return lax.ppermute(x, "tensor", [(0, 1), (1, 0)])


def third_cuts(rows):
    return [0, rows * 3 // 8, rows * 11 // 16, rows]


def gather_cube(own):
    cuts = third_cuts(own.shape[0])
    x, y, z = over_dp(own, 1), over_dp(own, 2), over_dp(own, 4)
    xy, yz, zx = over_dp(x, 2), over_dp(y, 4), over_dp(z, 1)
    last = [
        over_dp(xy[: cuts[1]], 4),
        over_dp(yz[cuts[1] : cuts[2]], 1),
        over_dp(zx[cuts[2] :], 2),
    ]
    return [[own], [x], [y], [xy], [z], [zx], [yz], last]


def gather_tokens(own):
    out = []
    for pieces in gather_cube(own):
        out += pieces + [over_cores(piece) for piece in pieces]
    return jnp.concatenate(out, axis=0)


def reduce_tokens(partial):
    cuts = third_cuts(partial.shape[2])
    both = (partial[:, 0].astype(F32) + over_cores(partial[:, 1]).astype(F32)).astype(BF)
    far = both[7]
    parts = [
        over_dp(far[: cuts[1]], 4),
        over_dp(far[cuts[1] : cuts[2]], 1),
        over_dp(far[cuts[2] :], 2),
    ]

    def added(base, index):
        low, high = cuts[index], cuts[index + 1]
        middle = (base[low:high].astype(F32) + parts[index].astype(F32)).astype(BF)
        return jnp.concatenate([base[:low], middle, base[high:]], axis=0)

    xy, yz, zx = added(both[3], 0), added(both[6], 1), added(both[5], 2)

    def plus(base, more):
        return (base.astype(F32) + more.astype(F32)).astype(BF)

    x = plus(both[1], over_dp(xy, 2))
    y = plus(both[2], over_dp(yz, 4))
    z = plus(both[4], over_dp(zx, 1))
    return (
        both[0].astype(F32)
        + over_dp(x, 1).astype(F32)
        + over_dp(y, 2).astype(F32)
        + over_dp(z, 4).astype(F32)
    )


def flip_blocks(x, axis, count, index):
    shape = x.shape
    bit = 1
    while bit < count:
        view = x.reshape(
            shape[:axis] + (count // (2 * bit), 2, bit * (shape[axis] // count)) + shape[axis + 1 :]
        )
        turned = jnp.concatenate(
            [
                lax.slice_in_dim(view, 1, 2, axis=axis + 1),
                lax.slice_in_dim(view, 0, 1, axis=axis + 1),
            ],
            axis=axis + 1,
        )
        x = jnp.where((index & bit) != 0, turned, view).reshape(shape)
        bit *= 2
    return x


def outer_gather(x):
    bit = GROUP
    while bit < lax.axis_size("dp"):
        x = jnp.concatenate([x, over_dp(x, bit)], axis=0)
        bit *= 2
    return x


def outer_reduce(x):
    bit = lax.axis_size("dp") // 2
    while bit >= GROUP:
        half = x.shape[0] // 2
        x = x[:half] + over_dp(x[half:].astype(BF), bit).astype(F32)
        bit //= 2
    return x.astype(BF)


def swap_members(x):
    size = lax.axis_size("dp")
    groups = [list(range(first, first + GROUP)) for first in range(0, size, GROUP)]
    return lax.all_to_all(
        x, "dp", split_axis=0, concat_axis=0, tiled=True, axis_index_groups=groups
    )


def spread_weight(weight):
    rows, which, columns = weight.shape
    own = columns // GROUP
    blocks = jnp.transpose(weight.reshape(rows, which, GROUP, own), (2, 0, 1, 3))
    moved = swap_members(blocks.reshape(GROUP, rows, which * own))
    return outer_gather(moved.reshape(GROUP * rows, which * own))


def return_grad(grad, which):
    summed = outer_reduce(grad)
    rows, own = summed.shape[0] // GROUP, summed.shape[1] // which
    back = swap_members(summed.reshape(GROUP, rows, which * own))
    back = back.reshape(GROUP, rows, which, own).astype(F32)
    return jnp.transpose(back, (1, 2, 0, 3)).reshape(rows, which, GROUP * own)


def doc_layout(lengths, positions):
    docs = jnp.arange(lengths.shape[1], dtype=jnp.int32)
    ends_at = jnp.sum(
        jnp.where(docs[None, None, :] <= docs[None, :, None], lengths[:, None, :], 0),
        axis=2,
        dtype=jnp.int32,
    )
    passed = positions[None, :, None] >= ends_at[:, None, :]
    segment = jnp.sum(passed.astype(jnp.int32), axis=2, dtype=jnp.int32)
    doc_start = jnp.sum(jnp.where(passed, lengths[:, None, :], 0), axis=2, dtype=jnp.int32)
    offset = (positions[None, :] - doc_start).astype(F32)
    allowed = (segment[:, :, None] == segment[:, None, :]) & (
        positions[None, :, None] >= positions[None, None, :]
    )
    half_dim = HEAD_DIM // 2
    inverse = jnp.exp(
        jnp.arange(half_dim, dtype=F32) * (-2.0 * math.log(10000.0) / HEAD_DIM)
    )
    angles = offset[:, :, None] * inverse
    return (allowed, jnp.cos(angles), jnp.sin(angles))


def rotate(values, cosine, sine_part):
    half_dim = HEAD_DIM // 2
    first, second = values[..., :half_dim], values[..., half_dim:]
    return jnp.concatenate(
        [first * cosine - second * sine_part, second * cosine + first * sine_part], axis=-1
    )


def rms_scale(values):
    return lax.rsqrt(jnp.mean(values * values, axis=-1, keepdims=True) + EPS_NORM)


def dot(left, right, contract, batch=((), ())):
    return lax.dot_general(left, right, (contract, batch), preferred_element_type=F32)


NN = ((1,), (0,))
NT = ((1,), (1,))
TN = ((0,), (0,))
ROWS = ((0,), (0,))
B_NN = ((2,), (1,))
B_NT = ((2,), (2,))
B_TN = ((1,), (1,))


def heads_to_tokens(mixed, member):
    rows = mixed.shape[1] // 2
    pair = jnp.concatenate([mixed[:, :rows], over_cores(mixed[:, rows:])], axis=2)
    got = jnp.stack([pair[0]] + [over_dp(pair[k], k) for k in range(1, GROUP)], axis=0)
    got = flip_blocks(got, 0, GROUP, member)
    width = mixed.shape[2]
    return [
        jnp.transpose(part, (1, 0, 2)).reshape(rows, GROUP * width)
        for part in (got[:, :, :width], got[:, :, width:])
    ]


def tokens_to_heads(own, other, member):
    rows, width = own.shape[0], own.shape[1] // GROUP
    halves = [part.reshape(rows, GROUP, width) for part in (own, other)]
    pair = jnp.transpose(jnp.concatenate(halves, axis=2), (1, 0, 2))
    pair = flip_blocks(pair, 0, GROUP, member)
    got = jnp.stack([pair[0]] + [over_dp(pair[k], k) for k in range(1, GROUP)], axis=0)
    return jnp.concatenate([got[:, :, :width], over_cores(got[:, :, width:])], axis=1)


def shards(
    tokens,
    norm1_gain,
    qkv_weight,
    out_weight,
    norm2_gain,
    gate_up_weight,
    down_weight,
    doc_lengths,
    cotangent,
):
    rows, width = tokens.shape
    place = lax.axis_index("dp")
    core = lax.axis_index("tensor")
    member, group = place % GROUP, place // GROUP
    outer = lax.axis_size("dp") // GROUP
    row_count = 2 * rows
    local_width = qkv_weight.shape[2]
    own_width = local_width // GROUP
    heads = own_width // HEAD_DIM
    own_hidden = gate_up_weight.shape[2] // GROUP
    scaling = HEAD_DIM ** (-0.5)

    def rolled(x):
        return flip_blocks(x, 1, outer, group)

    gain_one = norm1_gain.astype(F32)[:, None, None]
    gain_two = norm2_gain.astype(F32)[:, None, None]
    qkv_mat = spread_weight((qkv_weight.astype(F32) * gain_one).astype(BF))
    residual = rolled(tokens).astype(F32)
    scale_one = rms_scale(residual)
    normed_one = residual * scale_one
    rows_one = gather_tokens(normed_one.astype(BF))
    lengths = doc_lengths
    for bit in (1, 2, 4):
        lengths = jnp.concatenate([lengths, over_dp(lengths, bit)], axis=0)
    positions = (jnp.arange(row_count, dtype=jnp.int32) + rows * core) % row_count
    allowed, cosine, sine_part = doc_layout(lengths, positions)
    out_blocks = gather_cube(outer_gather(out_weight))
    out_own = jnp.concatenate([p for block in out_blocks for p in block], axis=0)
    out_other = over_cores(out_own)
    gate_up_mat = spread_weight((gate_up_weight.astype(F32) * gain_two).astype(BF))
    down_mat = spread_weight(down_weight[:, None, :])

    def member_order(x):
        shaped = x.reshape(x.shape[0], outer, GROUP, -1)
        shaped = flip_blocks(shaped, 2, GROUP, member)
        return jnp.swapaxes(shaped, 1, 2).reshape(x.shape)

    def feature_order(x):
        shaped = jnp.swapaxes(x.reshape(x.shape[0], GROUP, outer, -1), 1, 2)
        return flip_blocks(shaped, 2, GROUP, member).reshape(x.shape)

    projected = dot(rows_one, qkv_mat, NN).reshape(GROUP, row_count, 3, heads, HEAD_DIM)
    projected = jnp.moveaxis(projected, 3, 1).reshape(GROUP * heads, row_count, 3, HEAD_DIM)
    if heads > 1:
        allowed, cosine, sine_part = (
            jnp.repeat(part, heads, axis=0) for part in (allowed, cosine, sine_part)
        )
    queries = rotate(projected[:, :, 0], cosine, sine_part).astype(BF)
    keys = rotate(projected[:, :, 1], cosine, sine_part).astype(BF)
    values = projected[:, :, 2].astype(BF)
    scores = dot(queries, keys, B_NT, ROWS) * scaling
    scores = jnp.where(allowed, scores, MASKED_SCORE)
    row_max = jnp.max(scores, axis=2, keepdims=True)
    exp_scores = jnp.exp(scores - row_max)
    row_total = jnp.sum(exp_scores, axis=2, keepdims=True)
    probs = exp_scores / row_total
    weights = probs.astype(BF)
    mixed = dot(weights, values, B_NN, ROWS).astype(BF)
    mixed = jnp.moveaxis(mixed.reshape(GROUP, heads, row_count, HEAD_DIM), 1, 2)
    mixed = mixed.reshape(GROUP, row_count, own_width)
    mixed_own, mixed_other = heads_to_tokens(mixed, member)
    attn = feature_order(dot(mixed_own, out_own, NT) + dot(mixed_other, out_other, NT))
    stream = residual + attn
    scale_two = rms_scale(stream)
    normed_two = stream * scale_two
    rows_two = gather_tokens(normed_two.astype(BF))

    gate_up = dot(rows_two, gate_up_mat, NN)
    gate, upper = gate_up[:, :own_hidden], gate_up[:, own_hidden:]
    sigma = jax.nn.sigmoid(gate)
    silu_gate = gate * sigma
    hidden = (silu_gate * upper).astype(BF)
    cot_own = rolled(cotangent)
    cot_rows = gather_tokens(cot_own)
    grad_hidden = dot(cot_rows, down_mat, NN)
    grad_gate = (grad_hidden * upper * (sigma * (1.0 + gate * (1.0 - sigma)))).astype(BF)
    grad_upper = (grad_hidden * silu_gate).astype(BF)
    grad_gate_up = jnp.concatenate([grad_gate, grad_upper], axis=1)
    part_shape = (GROUP, 2, rows, width)
    back_two = reduce_tokens(dot(grad_gate_up, gate_up_mat, NT).astype(BF).reshape(part_shape))
    down_grad = return_grad(dot(cot_rows, hidden, TN), 1)[:, 0]
    gate_up_plain = return_grad(dot(rows_two, grad_gate_up, TN), 2)
    mlp_out = reduce_tokens(dot(hidden, down_mat, NT).astype(BF).reshape(part_shape))
    output = rolled((stream + mlp_out).astype(BF))

    def norm_back(grad_normed, normed, scale):
        return scale * (
            grad_normed - normed * jnp.mean(grad_normed * normed, axis=-1, keepdims=True)
        )

    grad_stream = cot_own.astype(F32) + norm_back(back_two, normed_two, scale_two)
    grad_low = grad_stream.astype(BF)

    grad_moved = member_order(grad_low)
    mixed_grad = tokens_to_heads(
        dot(grad_moved, out_own, NN).astype(BF), dot(grad_moved, out_other, NN).astype(BF), member
    )
    mixed_grad = jnp.moveaxis(mixed_grad.reshape(GROUP, row_count, heads, HEAD_DIM), 2, 1)
    mixed_grad = mixed_grad.reshape(GROUP * heads, row_count, HEAD_DIM)
    grad_values = dot(weights, mixed_grad, B_TN, ROWS)
    grad_probs = dot(mixed_grad, values, B_NT, ROWS)
    delta_sum = jnp.sum(probs * grad_probs, axis=2, keepdims=True)
    grad_scores = (probs * (grad_probs - delta_sum) * scaling).astype(BF)
    grad_queries = rotate(dot(grad_scores, keys, B_NN, ROWS), cosine, -sine_part)
    grad_keys = rotate(dot(grad_scores, queries, B_TN, ROWS), cosine, -sine_part)
    grad_qkv = jnp.stack([grad_queries, grad_keys, grad_values], axis=2).astype(BF)
    grad_qkv = grad_qkv.reshape(GROUP, heads, row_count, 3, HEAD_DIM)
    grad_qkv = jnp.moveaxis(grad_qkv, 1, 3).reshape(GROUP * row_count, 3 * own_width)
    back_one = reduce_tokens(dot(grad_qkv, qkv_mat, NT).astype(BF).reshape(part_shape))
    qkv_plain = return_grad(dot(rows_one, grad_qkv, TN), 3)
    grad_rows = gather_tokens(grad_low)
    out_grad = return_grad(dot(grad_rows, mixed.reshape(GROUP * row_count, own_width), TN), 1)[:, 0]
    input_grad = rolled((grad_stream + norm_back(back_one, normed_one, scale_one)).astype(BF))

    gains = jnp.stack(
        [
            jnp.sum(qkv_weight.astype(F32) * qkv_plain, axis=(1, 2)),
            jnp.sum(gate_up_weight.astype(F32) * gate_up_plain, axis=(1, 2)),
        ]
    )
    gains = gains + over_cores(gains)
    return (
        output,
        input_grad,
        gains[0],
        qkv_plain * gain_one,
        out_grad,
        gains[1],
        gate_up_plain * gain_two,
        down_grad,
    )


def solution(mesh):
    placed = (
        P(("dp", "tensor"), None),
        P("dp"),
        P("dp", None, "tensor"),
        P("dp", "tensor"),
        P("dp"),
        P("dp", None, "tensor"),
        P("dp", "tensor"),
        P("dp", None),
        P(("dp", "tensor"), None),
    )
    return jax.shard_map(
        shards,
        mesh=mesh,
        in_specs=placed,
        out_specs=(
            P(("dp", "tensor"), None),
            P(("dp", "tensor"), None),
            P("dp"),
            P("dp", None, "tensor"),
            P("dp", "tensor"),
            P("dp"),
            P("dp", None, "tensor"),
            P("dp", "tensor"),
        ),
        check_vma=False,
    )
```

```python
import functools
import math

import jax
import jax.numpy as jnp
from jax import lax
from jax.experimental import pallas as pl
from jax.experimental.pallas import tpu as pltpu
from jax.sharding import PartitionSpec as P

HEAD_DIM = 128
EPS_NORM = 1e-05
MASKED_SCORE = -1e30
GROUP = 8
X, Y, Z = 1, 2, 8
NEXT = 4
ORDER = (0, 1, 2, 4, 3, 6, 5, 7)
BF = jnp.bfloat16
F32 = jnp.float32
VMEM_LIMIT = 60 * 2**20


def over_dp(x, bit):
    size = lax.axis_size("dp")
    return lax.ppermute(x, "dp", [(i, i ^ bit) for i in range(size)])


def over_cores(x):
    return lax.ppermute(x, "tensor", [(0, 1), (1, 0)])


def outer_bits():
    size = lax.axis_size("dp")
    return [NEXT] + [1 << i for i in range(4, 12) if 1 << i < size]


def groups():
    size = lax.axis_size("dp")
    members = [x + y + z for z in (0, Z) for y in (0, Y) for x in (0, X)]
    firsts = [i for i in range(size) if not i & (X | Y | Z)]
    return [[first + member for member in members] for first in firsts]


def flip_blocks(x, axis, count, index):
    shape = x.shape
    bit = 1
    while bit < count:
        view = x.reshape(
            shape[:axis] + (count // (2 * bit), 2, bit * (shape[axis] // count)) + shape[axis + 1 :]
        )
        turned = jnp.concatenate(
            [
                lax.slice_in_dim(view, 1, 2, axis=axis + 1),
                lax.slice_in_dim(view, 0, 1, axis=axis + 1),
            ],
            axis=axis + 1,
        )
        x = jnp.where((index & bit) != 0, turned, view).reshape(shape)
        bit *= 2
    return x


def after(x, *others):
    return lax.optimization_barrier((x, *others))[0]


def after_all(arrays, *others):
    return list(lax.optimization_barrier((*arrays, *others)))[: len(arrays)]


def with_other_core(blocks):
    return [array for block in blocks for array in (block, over_cores(block))]


def part_of(pieces, first, rows):
    moves = [(i, first, i // 2, (i % 2) * rows, rows) for i in range(len(pieces))]
    return pieces, tuple(moves)


def gather(own):
    x, y, z = over_dp(own, X), over_dp(own, Y), over_dp(own, Z)
    xy, zx, yz = over_dp(x, Y), over_dp(z, X), over_dp(z, Y)
    far = over_dp(yz, X)
    return [own, x, y, z, xy, yz, zx, far]


def plus(base, more):
    return (base.astype(F32) + more.astype(F32)).astype(BF)


def both_cores(own, other):
    other = over_cores(other)
    return [plus(own[step], other[step]) for step in range(GROUP)]


def reduce_first(blocks):
    own, x, y, z, xy, yz, zx, far = blocks
    return [own, plus(x, over_dp(xy, Y)), y, plus(z, over_dp(zx, X)), plus(yz, over_dp(far, X))]


def reduce_second(blocks):
    own, x, y, z, yz = blocks
    return [own, x, y, plus(z, over_dp(yz, Y))]


def reduce_last(own, x, y, z):
    terms = [own, over_dp(x, X), over_dp(y, Y), over_dp(z, Z)]
    return sum(term.astype(F32) for term in terms)


def swap_members(blocks):
    return lax.all_to_all(
        blocks, "dp", split_axis=0, concat_axis=0, tiled=True, axis_index_groups=groups()
    )


def outer_gather(block):
    blocks = [block]
    for bit in outer_bits():
        blocks += [over_dp(one, bit) for one in blocks]
    return blocks


def outer_reduce(part):
    size = lax.axis_size("dp")
    across = [[i for i in range(size) if i & (X | Y | Z) == low] for low in range(size) if not low & ~(X | Y | Z)]
    outer = len(across[0])
    got = lax.all_to_all(
        part.reshape(outer, GROUP, *part.shape[1:]),
        "dp",
        split_axis=0,
        concat_axis=0,
        tiled=True,
        axis_index_groups=across,
    )
    return jnp.sum(got.astype(F32), axis=0).astype(BF)


def dot(left, right, left_dim, right_dim):
    return lax.dot_general(
        left, right, (((left_dim,), (right_dim,)), ((), ())), preferred_element_type=F32
    )


def moves_of(moves, piece_refs, held, sems):
    return [
        (
            step,
            pltpu.make_async_copy(
                piece_refs[index].at[pl.ds(source, rows)],
                held.at[step, pl.ds(row, rows)],
                sems.at[index],
            ),
        )
        for index, source, step, row, rows in moves
    ]


def fetch(moves, piece_refs, held, sems, step):
    copies = moves_of(moves, piece_refs, held, sems)

    @pl.when(step == 0)
    def _():
        for _, copy in copies:
            copy.start()

    for index in range(GROUP):

        @pl.when(step == index)
        def _():
            for at, copy in copies:
                if at == index:
                    copy.wait()


def turned(values, cosine, sine):
    return values * cosine + pltpu.roll(values, HEAD_DIM // 2, 1) * sine


def probabilities(queries, keys, mask):
    scores = dot(queries, keys, 1, 1) * (HEAD_DIM**-0.5)
    scores = jnp.where(mask > 0, scores, MASKED_SCORE)
    exps = jnp.exp(scores - jnp.max(scores, axis=1, keepdims=True))
    return exps / jnp.sum(exps, axis=1, keepdims=True)


def params():
    return pltpu.CompilerParams(
        dimension_semantics=("arbitrary",), vmem_limit_bytes=VMEM_LIMIT
    )


def whole(array):
    return pl.BlockSpec(array.shape, lambda step, places: (0,) * array.ndim)


def stepped(*block):
    return pl.BlockSpec((1, *block), lambda step, places: (step,) + (0,) * len(block))


ANYWHERE = pl.BlockSpec(memory_space=pl.ANY)


def fetch_weights(refs, held, sems, step):
    blocks = refs[0].shape[0]
    copies = [
        pltpu.make_async_copy(ref, held.at[pl.ds(i * blocks, blocks)], sems.at[i])
        for i, ref in enumerate(refs)
    ]

    @pl.when(step == 0)
    def _():
        for copy in copies:
            copy.start()

    def wait():
        @pl.when(step == 0)
        def _():
            for copy in copies:
                copy.wait()

    return wait


def head_weights(held, rows):
    owners = held.shape[0]
    cut = 3 * HEAD_DIM
    return (
        held[:, :rows, :cut].reshape(owners * rows, cut),
        held[:, :rows, cut:].reshape(owners * rows, HEAD_DIM),
    )


def attend_kernel(moves, shard_rows, outer, places, cosine, sine, mask, *refs):
    weights, refs = refs[:outer], refs[outer:]
    count = len(moves)
    pieces, refs = refs[:count], refs[count:]
    a_own, a_other, mixed_ref, q_ref, k_ref, v_ref, held, weight, sems, weight_sems = refs
    step = pl.program_id(0)
    wait = fetch_weights(weights, weight, weight_sems, step)
    fetch(moves, pieces, held, sems, step)
    wait()
    qkv_w, out_w = head_weights(weight, shard_rows)
    projected = dot(held[step], qkv_w, 1, 0)
    width = HEAD_DIM
    queries = turned(projected[:, :width], cosine[0], sine[0]).astype(BF)
    keys = turned(projected[:, width : 2 * width], cosine[0], sine[0]).astype(BF)
    values = projected[:, 2 * width :].astype(BF)
    q_ref[0], k_ref[0], v_ref[0] = queries, keys, values
    probs = probabilities(queries, keys, mask[0]).astype(BF)
    mixed = dot(probs, values, 1, 0).astype(BF)
    mixed_ref[0] = mixed
    attn = dot(mixed, out_w, 1, 1).astype(BF)
    half = attn.shape[0] // 2
    a_own[0], a_other[0] = attn[:half], attn[half:]


def row_specs(tokens):
    return [stepped(tokens, HEAD_DIM), stepped(tokens, HEAD_DIM), stepped(tokens, tokens)]


def attend(places, rows_one, weights, shard_rows, cosine, sine, mask):
    arrays, moves = rows_one
    tokens, width = mask.shape[1], arrays[0].shape[1]
    half = tokens // 2
    outer = len(weights)
    made = [jax.ShapeDtypeStruct((GROUP, half, width), BF)] * 2
    made += [jax.ShapeDtypeStruct((GROUP, tokens, HEAD_DIM), BF)] * 4
    return pl.pallas_call(
        functools.partial(attend_kernel, moves, shard_rows, outer),
        grid_spec=pltpu.PrefetchScalarGridSpec(
            num_scalar_prefetch=1,
            grid=(GROUP,),
            in_specs=row_specs(tokens) + [ANYWHERE] * (outer + len(arrays)),
            out_specs=[stepped(half, width)] * 2 + [stepped(tokens, HEAD_DIM)] * 4,
            scratch_shapes=[
                pltpu.VMEM((GROUP, tokens, width), BF),
                pltpu.VMEM((outer * GROUP, *weights[0].shape[1:]), BF),
                pltpu.SemaphoreType.DMA((len(arrays),)),
                pltpu.SemaphoreType.DMA((outer,)),
            ],
        ),
        out_shape=made,
        compiler_params=params(),
        cost_estimate=pl.CostEstimate(
            flops=2 * GROUP * tokens * (width * 4 + 2 * tokens) * HEAD_DIM,
            bytes_accessed=4 * GROUP * tokens * width,
            transcendentals=GROUP * tokens * tokens,
        ),
        name="attend",
    )(places, cosine, sine, mask, *weights, *arrays)


def feed_kernel(moves, cot_moves, outer, places, *refs):
    weights, refs = refs[:outer], refs[outer:]
    count, cot_count = len(moves), len(cot_moves)
    pieces, cots, refs = refs[:count], refs[count : count + cot_count], refs[count + cot_count :]
    m_own, m_other, hidden_ref, gate_ref, upper_ref, *refs = refs
    held, held_cot, weight, sems, cot_sems, weight_sems = refs
    step = pl.program_id(0)
    wait = fetch_weights(weights, weight, weight_sems, step)
    fetch(moves, pieces, held, sems, step)
    fetch(cot_moves, cots, held_cot, cot_sems, step)
    wait()
    width = held.shape[2]
    own = weight.shape[3]
    rows = held[step]
    half = rows.shape[0] // 2
    gate_w = weight[:, 0].reshape(width, own)
    upper_w = weight[:, 1].reshape(width, own)
    down_w = weight[:, 2].reshape(width, own)
    gate = dot(rows, gate_w, 1, 0)
    upper = dot(rows, upper_w, 1, 0)
    grad_hidden = dot(held_cot[step], down_w, 1, 0)
    sigma = 1.0 / (1.0 + jnp.exp(-gate))
    silu = gate * sigma
    hidden = (silu * upper).astype(BF)
    grad_gate = (grad_hidden * upper * (sigma * (1.0 + gate * (1.0 - sigma)))).astype(BF)
    grad_upper = (grad_hidden * silu).astype(BF)
    hidden_ref[0], gate_ref[0], upper_ref[0] = hidden, grad_gate, grad_upper
    back = (dot(grad_gate, gate_w, 1, 1) + dot(grad_upper, upper_w, 1, 1)).astype(BF)
    m_own[0, :half], m_other[0, :half] = back[:half], back[half:]
    out = dot(hidden, down_w, 1, 1).astype(BF)
    m_own[0, half:], m_other[0, half:] = out[:half], out[half:]


def feed(places, weights, rows_two, rows_cot, rows):
    (arrays, moves), (cot_arrays, cot_moves) = rows_two, rows_cot
    half, width = rows, arrays[0].shape[1]
    outer = len(weights)
    tokens, own = 2 * half, weights[0].shape[3]
    made = [jax.ShapeDtypeStruct((GROUP, tokens, width), BF)] * 2
    made += [jax.ShapeDtypeStruct((GROUP, tokens, own), BF)] * 3
    return pl.pallas_call(
        functools.partial(feed_kernel, moves, cot_moves, outer),
        grid_spec=pltpu.PrefetchScalarGridSpec(
            num_scalar_prefetch=1,
            grid=(GROUP,),
            in_specs=[ANYWHERE] * (outer + len(arrays) + len(cot_arrays)),
            out_specs=[stepped(tokens, width)] * 2 + [stepped(tokens, own)] * 3,
            scratch_shapes=[
                pltpu.VMEM((GROUP, tokens, width), BF),
                pltpu.VMEM((GROUP, tokens, width), BF),
                pltpu.VMEM((outer * GROUP, *weights[0].shape[1:]), BF),
                pltpu.SemaphoreType.DMA((len(arrays),)),
                pltpu.SemaphoreType.DMA((len(cot_arrays),)),
                pltpu.SemaphoreType.DMA((outer,)),
            ],
        ),
        out_shape=made,
        compiler_params=params(),
        cost_estimate=pl.CostEstimate(
            flops=12 * GROUP * tokens * width * own,
            bytes_accessed=8 * GROUP * tokens * width,
            transcendentals=GROUP * tokens * own,
        ),
        name="feed",
    )(places, *weights, *arrays, *cot_arrays)


def grads_kernel(layout, count_rights, places, *refs):
    count = len(layout)
    pieces, refs = refs[:count], refs[count:]
    rights, (*_, out, held, sems) = refs[:count_rights], refs[count_rights:]
    step, which = pl.program_id(0), pl.program_id(1)

    @pl.when((step == 0) & (which == 0))
    def _():
        copies = moves_of(layout, pieces, held, sems)
        for _, copy in copies:
            copy.start()
        for _, copy in copies:
            copy.wait()

    shards, _, rows, own = out.shape
    tile = shards * rows
    tokens = held.shape[0] * held.shape[1]
    for i, right in enumerate(rights):

        @pl.when(which == i)
        def _():
            left = held[:, :, pl.ds(pl.multiple_of(step * tile, 128), tile)].reshape(tokens, tile)
            product = dot(left, right[...].reshape(tokens, own), 0, 0)
            out[:, 0] = product.astype(BF).reshape(shards, rows, own)


def by_group(step, places):
    return 2 * ((step // 2) ^ places[GROUP]) + step % 2


def by_place(step, places):
    group = (step // 2) ^ places[GROUP]
    return 4 * (group // 2) + 2 * (step % 2) + group % 2


def weight_grads(places, pieces, rights, shard_rows, order, shape, at, into=None):
    arrays, layout = pieces
    _, tokens, own = rights[0].shape
    width = arrays[0].shape[1]
    tile = GROUP * shard_rows // 2
    kept = [] if into is None else [into]
    made = jax.ShapeDtypeStruct((width // shard_rows, shape[0], shard_rows, shape[1]), BF)
    return pl.pallas_call(
        functools.partial(grads_kernel, layout, len(rights)),
        grid_spec=pltpu.PrefetchScalarGridSpec(
            num_scalar_prefetch=1,
            grid=(width // tile, len(rights)),
            in_specs=[ANYWHERE] * len(arrays)
            + [
                pl.BlockSpec(right.shape, lambda step, which, places: (0, 0, 0))
                for right in rights
            ]
            + [ANYWHERE] * len(kept),
            out_specs=pl.BlockSpec(
                (tile // shard_rows, 1, shard_rows, own),
                lambda step, which, places: (order(step, places), at[0] + which, 0, at[1]),
            ),
            scratch_shapes=[
                pltpu.VMEM((GROUP, tokens, width), BF),
                pltpu.SemaphoreType.DMA((len(arrays),)),
            ],
        ),
        out_shape=made,
        input_output_aliases={1 + len(arrays) + len(rights): 0} if kept else {},
        compiler_params=pltpu.CompilerParams(
            dimension_semantics=("arbitrary", "arbitrary"), vmem_limit_bytes=VMEM_LIMIT
        ),
        cost_estimate=pl.CostEstimate(
            flops=2 * GROUP * tokens * width * own * len(rights),
            bytes_accessed=2 * GROUP * tokens * width,
            transcendentals=0,
        ),
        name="weight_grads",
    )(places, *arrays, *rights, *kept)


def pack_heads_kernel(qkv, out_weight, gain, note, packed):
    rows, columns = out_weight.shape
    for member in range(GROUP):
        for which in range(3):
            first = which * columns + member * HEAD_DIM
            part = qkv[:, first : first + HEAD_DIM].astype(F32) * gain[...]
            packed[member, :rows, which * HEAD_DIM : (which + 1) * HEAD_DIM] = part.astype(BF)
        first = member * HEAD_DIM
        packed[member, :rows, 3 * HEAD_DIM :] = out_weight[:, first : first + HEAD_DIM]
        packed[member, rows:, :] = note[...]


def pack_feed_kernel(gate_up, down, gain, packed):
    own = packed.shape[3]
    for which in range(3):
        for member in range(GROUP):
            if which < 2:
                first = (which * GROUP + member) * own
                part = (gate_up[:, first : first + own].astype(F32) * gain[...]).astype(BF)
            else:
                part = down[:, member * own : (member + 1) * own]
            packed[member, which] = part


def gained(gain_ref, sums):
    total = sum(jnp.sum(part, axis=1, keepdims=True) for part in sums)
    gain_ref[...] = jnp.broadcast_to(total, gain_ref.shape)


def unpack_heads_kernel(sources, got, qkv, gain, qkv_ref, out_ref, gain_ref):
    columns = out_ref.shape[1]
    sums = []
    for member in range(GROUP):
        total = sum(got[source].astype(F32) for source in sources[member])
        for which in range(3):
            first = which * columns + member * HEAD_DIM
            part = total[:, which * HEAD_DIM : (which + 1) * HEAD_DIM]
            sums.append(qkv[:, first : first + HEAD_DIM].astype(F32) * part)
            qkv_ref[:, first : first + HEAD_DIM] = part * gain[...]
        out_ref[:, member * HEAD_DIM : (member + 1) * HEAD_DIM] = total[:, 3 * HEAD_DIM :]
    gained(gain_ref, sums)


def unpack_feed_kernel(got, gate_up, gain, gate_up_ref, down_ref, gain_ref):
    own = got.shape[3]
    sums = []
    for which in range(3):
        for member in range(GROUP):
            part = got[member, which].astype(F32)
            if which < 2:
                first = (which * GROUP + member) * own
                sums.append(gate_up[:, first : first + own].astype(F32) * part)
                gate_up_ref[:, first : first + own] = part * gain[...]
            else:
                down_ref[:, member * own : (member + 1) * own] = part
    gained(gain_ref, sums)


def plain_call(kernel, name, arrays, made):
    in_vmem = pl.BlockSpec(memory_space=pltpu.VMEM)
    return pl.pallas_call(
        kernel,
        in_specs=[in_vmem] * len(arrays),
        out_specs=jax.tree.map(lambda _: in_vmem, made),
        out_shape=made,
        compiler_params=pltpu.CompilerParams(vmem_limit_bytes=VMEM_LIMIT),
        name=name,
    )(*arrays)


def attend_back_kernel(
    moves, shard_rows, outer, places, cosine, sine, mask, q_ref, k_ref, v_ref, *refs
):
    weights, refs = refs[:outer], refs[outer:]
    count = len(moves)
    pieces, refs = refs[:count], refs[count:]
    grad_ref, m_own, m_other, held, weight, sems, weight_sems = refs
    step = pl.program_id(0)
    wait = fetch_weights(weights, weight, weight_sems, step)
    fetch(moves, pieces, held, sems, step)
    wait()
    qkv_w, out_w = head_weights(weight, shard_rows)
    queries, keys, values = q_ref[0], k_ref[0], v_ref[0]
    grad_mixed = dot(held[step], out_w, 1, 0).astype(BF)
    probs = probabilities(queries, keys, mask[0])
    grad_values = dot(probs.astype(BF), grad_mixed, 0, 0)
    grad_probs = dot(grad_mixed, values, 1, 1)
    delta = jnp.sum(probs * grad_probs, axis=1, keepdims=True)
    grad_scores = (probs * (grad_probs - delta) * (HEAD_DIM**-0.5)).astype(BF)
    grad_queries = turned(dot(grad_scores, keys, 1, 0), cosine[0], -sine[0])
    grad_keys = turned(dot(grad_scores, queries, 0, 0), cosine[0], -sine[0])
    grads = jnp.concatenate([grad_queries, grad_keys, grad_values], axis=1).astype(BF)
    grad_ref[0] = grads
    back = dot(grads, qkv_w, 1, 1).astype(BF)
    half = back.shape[0] // 2
    m_own[0], m_other[0] = back[:half], back[half:]


def attend_back(places, rows_grad, weights, shard_rows, cosine, sine, mask, queries, keys, values):
    arrays, moves = rows_grad
    tokens, width = mask.shape[1], arrays[0].shape[1]
    half = tokens // 2
    outer = len(weights)
    made = [jax.ShapeDtypeStruct((GROUP, tokens, 3 * HEAD_DIM), BF)]
    made += [jax.ShapeDtypeStruct((GROUP, half, width), BF)] * 2
    return pl.pallas_call(
        functools.partial(attend_back_kernel, moves, shard_rows, outer),
        grid_spec=pltpu.PrefetchScalarGridSpec(
            num_scalar_prefetch=1,
            grid=(GROUP,),
            in_specs=row_specs(tokens)
            + [stepped(tokens, HEAD_DIM)] * 3
            + [ANYWHERE] * (outer + len(arrays)),
            out_specs=[stepped(tokens, 3 * HEAD_DIM)] + [stepped(half, width)] * 2,
            scratch_shapes=[
                pltpu.VMEM((GROUP, tokens, width), BF),
                pltpu.VMEM((outer * GROUP, *weights[0].shape[1:]), BF),
                pltpu.SemaphoreType.DMA((len(arrays),)),
                pltpu.SemaphoreType.DMA((outer,)),
            ],
        ),
        out_shape=made,
        compiler_params=params(),
        cost_estimate=pl.CostEstimate(
            flops=2 * GROUP * tokens * (width * 4 + 5 * tokens) * HEAD_DIM,
            bytes_accessed=4 * GROUP * tokens * width,
            transcendentals=GROUP * tokens * tokens,
        ),
        name="attend_back",
    )(places, cosine, sine, mask, queries, keys, values, *weights, *arrays)


def doc_layout(lengths, positions):
    docs = jnp.arange(lengths.shape[1], dtype=jnp.int32)
    ends_at = jnp.sum(
        jnp.where(docs[None, None, :] <= docs[None, :, None], lengths[:, None, :], 0),
        axis=2,
        dtype=jnp.int32,
    )
    passed = positions[None, :, None] >= ends_at[:, None, :]
    segment = jnp.sum(passed.astype(jnp.int32), axis=2, dtype=jnp.int32)
    doc_start = jnp.sum(jnp.where(passed, lengths[:, None, :], 0), axis=2, dtype=jnp.int32)
    offset = (positions[None, :] - doc_start).astype(F32)
    allowed = (segment[:, :, None] == segment[:, None, :]) & (
        positions[None, :, None] >= positions[None, None, :]
    )
    half_dim = HEAD_DIM // 2
    inverse = jnp.exp(
        jnp.arange(half_dim, dtype=F32) * (-2.0 * math.log(10000.0) / HEAD_DIM)
    )
    angles = offset[:, :, None] * inverse
    cosine, sine = jnp.cos(angles), jnp.sin(angles)
    return (
        allowed.astype(BF),
        jnp.concatenate([cosine, cosine], axis=2),
        jnp.concatenate([-sine, sine], axis=2),
    )


def rms_scale(values):
    return lax.rsqrt(jnp.mean(values * values, axis=-1, keepdims=True) + EPS_NORM)


def norm_back(grad_normed, normed, scale):
    return scale * (
        grad_normed - normed * jnp.mean(grad_normed * normed, axis=-1, keepdims=True)
    )


def shards(
    tokens,
    norm1_gain,
    qkv_weight,
    out_weight,
    norm2_gain,
    gate_up_weight,
    down_weight,
    doc_lengths,
    cotangent,
):
    rows, width = tokens.shape
    place = lax.axis_index("dp")
    core = lax.axis_index("tensor")
    member = place % NEXT + NEXT * ((place // Z) % 2)
    group = (place // NEXT) % 2 + 2 * (place // (2 * Z))
    outer = lax.axis_size("dp") // GROUP
    row_count = 2 * rows
    shard_rows, _, local_width = qkv_weight.shape
    own_hidden = gate_up_weight.shape[2] // GROUP
    assert local_width == GROUP * HEAD_DIM
    places = jnp.concatenate(
        [jnp.array(ORDER, jnp.int32) ^ member, jnp.reshape(group, (1,)).astype(jnp.int32)]
    )

    def rolled(x):
        shaped = x.reshape(rows, outer // 2, 2, 2, NEXT * shard_rows)
        return flip_blocks(jnp.swapaxes(shaped, 2, 3).reshape(x.shape), 1, outer, group)

    def unrolled(x):
        shaped = flip_blocks(x, 1, outer, group).reshape(rows, outer // 2, 2, 2, NEXT * shard_rows)
        return jnp.swapaxes(shaped, 2, 3).reshape(x.shape)

    gain_one = norm1_gain.astype(F32)[:, None]
    gain_two = norm2_gain.astype(F32)[:, None]

    residual = rolled(tokens).astype(F32)
    scale_one = rms_scale(residual)
    normed_one = residual * scale_one
    blocks_one = gather(normed_one.astype(BF))
    rows_one = part_of(with_other_core(blocks_one), 0, rows)
    qkv_flat = qkv_weight.reshape(shard_rows, 3 * local_width)
    docs = doc_lengths.shape[1]
    note = jnp.pad(doc_lengths.astype(BF), ((0, 15), (0, 4 * HEAD_DIM - docs)))
    head_own = swap_members(
        plain_call(
            pack_heads_kernel,
            "pack_heads",
            [qkv_flat, out_weight, gain_one, note],
            jax.ShapeDtypeStruct((GROUP, shard_rows + 16, 4 * HEAD_DIM), BF),
        )
    )
    head_mats = outer_gather(head_own)
    chosen = (jnp.arange(GROUP, dtype=jnp.int32)[None, :] == places[:GROUP, None])[:, :, None]
    lengths = jnp.sum(
        jnp.where(chosen, head_own[:, shard_rows, :docs].astype(F32)[None], 0.0), axis=1
    ).astype(jnp.int32)
    positions = (jnp.arange(row_count, dtype=jnp.int32) + rows * core) % row_count
    mask, cosine, sine = doc_layout(lengths, positions)

    gate_up_flat = gate_up_weight.reshape(shard_rows, 2 * GROUP * own_hidden)
    feed_packed = plain_call(
        pack_feed_kernel,
        "pack_feed",
        [gate_up_flat, down_weight, gain_two],
        jax.ShapeDtypeStruct((GROUP, 3, shard_rows, own_hidden), BF),
    )
    feed_mats = outer_gather(swap_members(after(feed_packed, blocks_one[1])))
    cot_own = rolled(cotangent)
    blocks_cot = gather(after(cot_own, *blocks_one[4:]))
    rows_cot = part_of(with_other_core(blocks_cot), 0, rows)

    a_own, a_other, mixed, queries, keys, values = attend(
        places, rows_one, head_mats, shard_rows, cosine, sine, mask
    )
    attn_blocks = after_all(both_cores(a_own, a_other), *blocks_cot[1:3])
    attn = reduce_last(*reduce_second(reduce_first(attn_blocks)))
    stream = residual + attn
    scale_two = rms_scale(stream)
    normed_two = stream * scale_two
    blocks_two = gather(after(normed_two.astype(BF), *blocks_cot[4:]))
    rows_two = part_of(with_other_core(blocks_two), 0, rows)

    m_own, m_other, hidden, grad_gate, grad_upper = feed(
        places, feed_mats, rows_two, rows_cot, rows
    )
    feed_shape = (3, own_hidden)
    feed_part = weight_grads(
        places, rows_cot, [hidden], shard_rows, by_group, feed_shape, (2, 0)
    )
    ends = both_cores(m_own, m_other)
    first = reduce_first(ends)
    second = reduce_second(after_all(first, feed_part))
    feed_part = weight_grads(
        places,
        rows_two,
        after_all([grad_gate, grad_upper], *first),
        shard_rows,
        by_group,
        feed_shape,
        (0, 0),
        feed_part,
    )
    both = reduce_last(*after_all(second, feed_part))
    back_two, mlp_out = both[:rows], both[rows:]
    feed_sum = outer_reduce(feed_part)
    feed_got = swap_members(feed_sum)
    grad_stream = cot_own.astype(F32) + norm_back(back_two, normed_two, scale_two)

    grad_low = grad_stream.astype(BF)
    rows_grad = part_of(with_other_core(gather(grad_low)), 0, rows)
    grad_qkv, m_own, m_other = attend_back(
        places,
        rows_grad,
        head_mats,
        shard_rows,
        cosine,
        sine,
        after(mask, feed_sum),
        queries,
        keys,
        values,
    )
    head_shape = (1, 4 * HEAD_DIM)
    head_part = weight_grads(
        places, rows_grad, [mixed], shard_rows, by_place, head_shape, (0, 3)
    )
    head_part = weight_grads(
        places, rows_one, [grad_qkv], shard_rows, by_place, head_shape, (0, 0), head_part
    )
    head_got = lax.all_to_all(head_part[:, 0], "dp", split_axis=0, concat_axis=0, tiled=True)
    ends = after_all(both_cores(m_own, m_other), head_part)
    back_one = reduce_last(*reduce_second(reduce_first(ends)))

    output = unrolled((stream + mlp_out).astype(BF))
    input_grad = unrolled((grad_stream + norm_back(back_one, normed_one, scale_one)).astype(BF))
    gate_up_grad, down_grad, gain_two_part = plain_call(
        unpack_feed_kernel,
        "unpack_feed",
        [feed_got, gate_up_flat, gain_two],
        [
            jax.ShapeDtypeStruct(gate_up_flat.shape, F32),
            jax.ShapeDtypeStruct(down_weight.shape, F32),
            jax.ShapeDtypeStruct((shard_rows, 128), F32),
        ],
    )
    sources = [
        [
            16 * (other // 2) + Z * (one // NEXT) + NEXT * (other % 2) + one % NEXT
            for other in range(outer)
        ]
        for one in range(GROUP)
    ]
    qkv_grad, out_grad, gain_one_part = plain_call(
        functools.partial(unpack_heads_kernel, sources),
        "unpack_heads",
        [head_got, qkv_flat, gain_one],
        [
            jax.ShapeDtypeStruct(qkv_flat.shape, F32),
            jax.ShapeDtypeStruct(out_weight.shape, F32),
            jax.ShapeDtypeStruct((shard_rows, 128), F32),
        ],
    )
    gain_two_part, gain_one_part = gain_two_part[:, 0], gain_one_part[:, 0]
    return (
        output,
        input_grad,
        gain_one_part + over_cores(gain_one_part),
        qkv_grad.reshape(qkv_weight.shape),
        out_grad,
        gain_two_part + over_cores(gain_two_part),
        gate_up_grad.reshape(gate_up_weight.shape),
        down_grad,
    )


def solution(mesh):
    placed = (
        P(("dp", "tensor"), None),
        P("dp"),
        P("dp", None, "tensor"),
        P("dp", "tensor"),
        P("dp"),
        P("dp", None, "tensor"),
        P("dp", "tensor"),
        P("dp", None),
        P(("dp", "tensor"), None),
    )
    return jax.shard_map(
        shards,
        mesh=mesh,
        in_specs=placed,
        out_specs=(
            P(("dp", "tensor"), None),
            P(("dp", "tensor"), None),
            P("dp"),
            P("dp", None, "tensor"),
            P("dp", "tensor"),
            P("dp"),
            P("dp", None, "tensor"),
            P("dp", "tensor"),
        ),
        check_vma=False,
    )
```

```python
import functools
import math

import jax
import jax.numpy as jnp
from jax import lax
from jax.experimental import pallas as pl
from jax.experimental.pallas import tpu as pltpu
from jax.sharding import PartitionSpec as P

HEAD_DIM = 128
EPS_NORM = 1e-05
MASKED_SCORE = -1e30
GROUP = 4
X, Y = 1, 2
BF = jnp.bfloat16
F32 = jnp.float32
VMEM_LIMIT = 60 * 2**20


def over_dp(x, bit):
    size = lax.axis_size("dp")
    return lax.ppermute(x, "dp", [(i, i ^ bit) for i in range(size)])


def over_cores(x):
    return lax.ppermute(x, "tensor", [(0, 1), (1, 0)])


def groups():
    size = lax.axis_size("dp")
    return [list(range(first, first + GROUP)) for first in range(0, size, GROUP)]


def ring():
    count = lax.axis_size("dp") // GROUP
    return [*range(0, count, 2)][:1] + [*range(1, count, 2)] + [*range(2, count, 2)][::-1]


def over_ring(x):
    order = ring()
    pairs = zip(order, order[1:] + order[:1])
    return lax.ppermute(
        x, "dp", [(GROUP * a + i, GROUP * b + i) for a, b in pairs for i in range(GROUP)]
    )


def after(x, *others):
    return lax.optimization_barrier((x, *others))[0]


def after_all(arrays, *others):
    return list(lax.optimization_barrier((*arrays, *others)))[: len(arrays)]


def with_other_core(blocks):
    return [array for block in blocks for array in (block, over_cores(block))]


def part_of(pieces, first, rows):
    moves = [(i, first, i // 2, (i % 2) * rows, rows) for i in range(len(pieces))]
    return pieces, tuple(moves)


def gather(own):
    x, y = over_dp(own, X), over_dp(own, Y)
    return [own, x, y, over_dp(x, Y)]


def plus(base, more):
    return (base.astype(F32) + more.astype(F32)).astype(BF)


def both_cores(own, other):
    other = over_cores(other)
    return [plus(own[step], other[step]) for step in range(GROUP)]


def reduce_first(blocks):
    own, x, y, xy = blocks
    return [own, plus(x, over_dp(xy, Y)), y]


def reduce_last(own, x, y):
    terms = [own, over_dp(x, X), over_dp(y, Y)]
    return sum(term.astype(F32) for term in terms)


def swap_members(blocks):
    return lax.all_to_all(
        blocks, "dp", split_axis=0, concat_axis=0, tiled=True, axis_index_groups=groups()
    )


def outer_gather(block):
    blocks = [block]
    for _ in ring()[1:]:
        blocks.append(over_ring(blocks[-1]))
    return blocks


def outer_reduce(part):
    chunks = part.reshape(-1, GROUP, *part.shape[1:])
    sums = [over_ring(chunks[1])]
    for k in range(2, chunks.shape[0]):
        sums.append(over_ring(plus(sums[-1], chunks[k])))
    sums.append(plus(sums[-1], chunks[0]))
    return sums


def dot(left, right, left_dim, right_dim):
    return lax.dot_general(
        left, right, (((left_dim,), (right_dim,)), ((), ())), preferred_element_type=F32
    )


def moves_of(moves, piece_refs, held, sems):
    return [
        (
            step,
            pltpu.make_async_copy(
                piece_refs[index].at[pl.ds(source, rows)],
                held.at[step, pl.ds(row, rows)],
                sems.at[index],
            ),
        )
        for index, source, step, row, rows in moves
    ]


def fetch(moves, piece_refs, held, sems, step):
    copies = moves_of(moves, piece_refs, held, sems)

    @pl.when(step == 0)
    def _():
        for _, copy in copies:
            copy.start()

    for index in range(GROUP):

        @pl.when(step == index)
        def _():
            for at, copy in copies:
                if at == index:
                    copy.wait()


def turned(values, cosine, sine):
    return values * cosine + pltpu.roll(values, HEAD_DIM // 2, 1) * sine


def probabilities(queries, keys, mask):
    scores = dot(queries, keys, 1, 1) * (HEAD_DIM**-0.5)
    scores = jnp.where(mask > 0, scores, MASKED_SCORE)
    exps = jnp.exp(scores - jnp.max(scores, axis=1, keepdims=True))
    return exps / jnp.sum(exps, axis=1, keepdims=True)


def params():
    return pltpu.CompilerParams(
        dimension_semantics=("arbitrary",), vmem_limit_bytes=VMEM_LIMIT
    )


def whole(array):
    return pl.BlockSpec(array.shape, lambda step, places: (0,) * array.ndim)


def stepped(*block):
    return pl.BlockSpec((1, *block), lambda step, places: (step,) + (0,) * len(block))


ANYWHERE = pl.BlockSpec(memory_space=pl.ANY)


def up_to_lanes(columns):
    return -(-columns // 128) * 128


def fetch_weights(refs, held, sems, step):
    blocks = refs[0].shape[0]
    copies = [
        pltpu.make_async_copy(ref, held.at[pl.ds(i * blocks, blocks)], sems.at[i])
        for i, ref in enumerate(refs)
    ]

    @pl.when(step == 0)
    def _():
        for copy in copies:
            copy.start()

    def wait():
        @pl.when(step == 0)
        def _():
            for copy in copies:
                copy.wait()

    return wait


def head_weights(held, rows):
    owners, _, columns = held.shape
    cut = columns // 4 * 3
    return (
        held[:, :rows, :cut].reshape(owners * rows, cut),
        held[:, :rows, cut:].reshape(owners * rows, columns - cut),
    )


def heads_of(width):
    return [(i, i + HEAD_DIM) for i in range(0, width, HEAD_DIM)]


def attend_kernel(moves, shard_rows, outer, places, cosine, sine, mask, *refs):
    weights, refs = refs[:outer], refs[outer:]
    count = len(moves)
    pieces, refs = refs[:count], refs[count:]
    a_own, a_other, mixed_ref, q_ref, k_ref, v_ref, held, weight, sems, weight_sems = refs
    step = pl.program_id(0)
    wait = fetch_weights(weights, weight, weight_sems, step)
    fetch(moves, pieces, held, sems, step)
    wait()
    qkv_w, out_w = head_weights(weight, shard_rows)
    projected = dot(held[step], qkv_w, 1, 0)
    width = out_w.shape[1]
    for low, high in heads_of(width):
        queries = turned(projected[:, low:high], cosine[0], sine[0]).astype(BF)
        keys = turned(projected[:, width + low : width + high], cosine[0], sine[0]).astype(BF)
        values = projected[:, 2 * width + low : 2 * width + high].astype(BF)
        q_ref[0, :, low:high], k_ref[0, :, low:high], v_ref[0, :, low:high] = queries, keys, values
        probs = probabilities(queries, keys, mask[0]).astype(BF)
        mixed_ref[0, :, low:high] = dot(probs, values, 1, 0).astype(BF)
    mixed = mixed_ref[0]
    attn = dot(mixed, out_w, 1, 1).astype(BF)
    half = attn.shape[0] // 2
    a_own[0], a_other[0] = attn[:half], attn[half:]


def row_specs(tokens):
    return [stepped(tokens, HEAD_DIM), stepped(tokens, HEAD_DIM), stepped(tokens, tokens)]


def attend(places, rows_one, weights, shard_rows, cosine, sine, mask):
    arrays, moves = rows_one
    tokens, width = mask.shape[1], arrays[0].shape[1]
    half = tokens // 2
    outer = len(weights)
    made = [jax.ShapeDtypeStruct((GROUP, half, width), BF)] * 2
    own = weights[0].shape[2] // 4
    made += [jax.ShapeDtypeStruct((GROUP, tokens, own), BF)] * 4
    return pl.pallas_call(
        functools.partial(attend_kernel, moves, shard_rows, outer),
        grid_spec=pltpu.PrefetchScalarGridSpec(
            num_scalar_prefetch=1,
            grid=(GROUP,),
            in_specs=row_specs(tokens) + [ANYWHERE] * (outer + len(arrays)),
            out_specs=[stepped(half, width)] * 2 + [stepped(tokens, own)] * 4,
            scratch_shapes=[
                pltpu.VMEM((GROUP, tokens, width), BF),
                pltpu.VMEM((outer * GROUP, *weights[0].shape[1:]), BF),
                pltpu.SemaphoreType.DMA((len(arrays),)),
                pltpu.SemaphoreType.DMA((outer,)),
            ],
        ),
        out_shape=made,
        compiler_params=params(),
        cost_estimate=pl.CostEstimate(
            flops=2 * GROUP * tokens * (width * 4 + 2 * tokens) * own,
            bytes_accessed=4 * GROUP * tokens * width,
            transcendentals=GROUP * tokens * tokens,
        ),
        name="attend",
    )(places, cosine, sine, mask, *weights, *arrays)


def feed_kernel(moves, cot_moves, outer, places, *refs):
    weights, refs = refs[:outer], refs[outer:]
    count, cot_count = len(moves), len(cot_moves)
    pieces, cots, refs = refs[:count], refs[count : count + cot_count], refs[count + cot_count :]
    m_own, m_other, hidden_ref, grads_ref, *refs = refs
    held, held_cot, weight, sems, cot_sems, weight_sems = refs
    step = pl.program_id(0)
    wait = fetch_weights(weights, weight, weight_sems, step)
    fetch(moves, pieces, held, sems, step)
    fetch(cot_moves, cots, held_cot, cot_sems, step)
    wait()
    width = held.shape[2]
    own = grads_ref.shape[2] // 2
    pair_w = weight[:, :, : 2 * own].reshape(width, 2 * own)
    down_w = weight[:, :, 2 * own : 3 * own].reshape(width, own)
    rows = held[step]
    half = rows.shape[0] // 2
    both = dot(rows, pair_w, 1, 0)
    gate, upper = both[:, :own], both[:, own:]
    grad_hidden = dot(held_cot[step], down_w, 1, 0)
    sigma = 1.0 / (1.0 + jnp.exp(-gate))
    silu = gate * sigma
    hidden = (silu * upper).astype(BF)
    grad_gate = grad_hidden * upper * (sigma * (1.0 + gate * (1.0 - sigma)))
    grads = jnp.concatenate([grad_gate, grad_hidden * silu], axis=1).astype(BF)
    hidden_ref[0, :, :own], grads_ref[0] = hidden, grads
    hidden_ref[0, :, own:] = jnp.zeros((2 * half, hidden_ref.shape[2] - own), BF)
    back = dot(grads, pair_w, 1, 1).astype(BF)
    m_own[0, :half], m_other[0, :half] = back[:half], back[half:]
    out = dot(hidden, down_w, 1, 1).astype(BF)
    m_own[0, half:], m_other[0, half:] = out[:half], out[half:]


def feed(places, weights, rows_two, rows_cot, rows, own):
    (arrays, moves), (cot_arrays, cot_moves) = rows_two, rows_cot
    half, width = rows, arrays[0].shape[1]
    outer = len(weights)
    tokens = 2 * half
    made = [jax.ShapeDtypeStruct((GROUP, tokens, width), BF)] * 2
    kept = [up_to_lanes(own), 2 * own]
    made += [jax.ShapeDtypeStruct((GROUP, tokens, one), BF) for one in kept]
    return pl.pallas_call(
        functools.partial(feed_kernel, moves, cot_moves, outer),
        grid_spec=pltpu.PrefetchScalarGridSpec(
            num_scalar_prefetch=1,
            grid=(GROUP,),
            in_specs=[ANYWHERE] * (outer + len(arrays) + len(cot_arrays)),
            out_specs=[stepped(tokens, width)] * 2 + [stepped(tokens, one) for one in kept],
            scratch_shapes=[
                pltpu.VMEM((GROUP, tokens, width), BF),
                pltpu.VMEM((GROUP, tokens, width), BF),
                pltpu.VMEM((outer * GROUP, *weights[0].shape[1:]), BF),
                pltpu.SemaphoreType.DMA((len(arrays),)),
                pltpu.SemaphoreType.DMA((len(cot_arrays),)),
                pltpu.SemaphoreType.DMA((outer,)),
            ],
        ),
        out_shape=made,
        compiler_params=params(),
        cost_estimate=pl.CostEstimate(
            flops=12 * GROUP * tokens * width * own,
            bytes_accessed=8 * GROUP * tokens * width,
            transcendentals=GROUP * tokens * own,
        ),
        name="feed",
    )(places, *weights, *arrays, *cot_arrays)


def grads_kernel(layout, places, *refs):
    count = len(layout)
    pieces, (right, *_, out, held, sems) = refs[:count], refs[count:]
    step = pl.program_id(0)

    @pl.when(step == 0)
    def _():
        copies = moves_of(layout, pieces, held, sems)
        for _, copy in copies:
            copy.start()
        for _, copy in copies:
            copy.wait()

    shards, rows, own = out.shape
    tile = shards * rows
    tokens = held.shape[0] * held.shape[1]
    left = held[:, :, pl.ds(pl.multiple_of(step * tile, 128), tile)].reshape(tokens, tile)
    product = dot(left, right[...].reshape(tokens, own), 0, 0)
    out[...] = product.astype(BF).reshape(shards, rows, own)


def weight_grads(places, pieces, right, shard_rows, columns, at=0, into=None):
    arrays, layout = pieces
    _, tokens, own = right.shape
    width = arrays[0].shape[1]
    tile = 512
    kept = [] if into is None else [into]
    return pl.pallas_call(
        functools.partial(grads_kernel, layout),
        grid_spec=pltpu.PrefetchScalarGridSpec(
            num_scalar_prefetch=1,
            grid=(width // tile,),
            in_specs=[ANYWHERE] * len(arrays) + [whole(right)] + [ANYWHERE] * len(kept),
            out_specs=pl.BlockSpec(
                (tile // shard_rows, shard_rows, own), lambda step, places: (step, 0, at)
            ),
            scratch_shapes=[
                pltpu.VMEM((GROUP, tokens, width), BF),
                pltpu.SemaphoreType.DMA((len(arrays),)),
            ],
        ),
        out_shape=jax.ShapeDtypeStruct((width // shard_rows, shard_rows, columns), BF),
        input_output_aliases={2 + len(arrays): 0} if kept else {},
        compiler_params=params(),
        cost_estimate=pl.CostEstimate(
            flops=2 * GROUP * tokens * width * own,
            bytes_accessed=2 * GROUP * tokens * width,
            transcendentals=0,
        ),
        name="weight_grads",
    )(places, *arrays, right, *kept)


def pack_heads_kernel(qkv, out_weight, gain, note, packed):
    rows, columns = out_weight.shape
    own = columns // GROUP
    for member in range(GROUP):
        for which in range(3):
            first = which * columns + member * own
            part = qkv[:, first : first + own].astype(F32) * gain[...]
            packed[member, :rows, which * own : (which + 1) * own] = part.astype(BF)
        packed[member, :rows, 3 * own :] = out_weight[:, member * own : (member + 1) * own]
        packed[member, rows:, :] = note[...]


def pack_feed_kernel(gate_up, down, gain, packed):
    rows, columns = down.shape
    own = columns // GROUP
    for member in range(GROUP):
        for which in range(2):
            first = which * columns + member * own
            part = (gate_up[:, first : first + own].astype(F32) * gain[...]).astype(BF)
            packed[member, :, which * own : (which + 1) * own] = part
        packed[member, :, 2 * own : 3 * own] = down[:, member * own : (member + 1) * own]
        packed[member, :, 3 * own :] = jnp.zeros((rows, packed.shape[2] - 3 * own), BF)


def gained(gain_ref, sums):
    gain_ref[...] = jnp.broadcast_to(sum(sums), gain_ref.shape)


def unpack_heads_kernel(got, qkv, gain, qkv_ref, out_ref, gain_ref):
    columns = out_ref.shape[1]
    own = columns // GROUP
    sums = []
    for member in range(GROUP):
        total = got[member].astype(F32)
        for which in range(3):
            first = which * columns + member * own
            part = total[:, which * own : (which + 1) * own]
            sums.append(jnp.sum(qkv[:, first : first + own].astype(F32) * part, axis=1, keepdims=True))
            qkv_ref[:, first : first + own] = part * gain[...]
        out_ref[:, member * own : (member + 1) * own] = total[:, 3 * own :]
    gained(gain_ref, sums)


def unpack_feed_kernel(got, got_down, gate_up, gain, gate_up_ref, down_ref, gain_ref):
    columns = down_ref.shape[1]
    own = columns // GROUP
    sums = []
    for member in range(GROUP):
        total = got[member].astype(F32)
        for which in range(2):
            first = which * columns + member * own
            part = total[:, which * own : (which + 1) * own]
            old = gate_up[:, first : first + own].astype(F32)
            sums.append(jnp.sum(old * part, axis=1, keepdims=True))
            gate_up_ref[:, first : first + own] = part * gain[...]
        down_ref[:, member * own : (member + 1) * own] = got_down[member, :, :own].astype(F32)
    gained(gain_ref, sums)


def plain_call(kernel, name, arrays, made):
    in_vmem = pl.BlockSpec(memory_space=pltpu.VMEM)
    return pl.pallas_call(
        kernel,
        in_specs=[in_vmem] * len(arrays),
        out_specs=jax.tree.map(lambda _: in_vmem, made),
        out_shape=made,
        compiler_params=pltpu.CompilerParams(vmem_limit_bytes=VMEM_LIMIT),
        name=name,
    )(*arrays)


def attend_back_kernel(
    moves, shard_rows, outer, places, cosine, sine, mask, q_ref, k_ref, v_ref, *refs
):
    weights, refs = refs[:outer], refs[outer:]
    count = len(moves)
    pieces, refs = refs[:count], refs[count:]
    grad_ref, m_own, m_other, held, weight, sems, weight_sems = refs
    step = pl.program_id(0)
    wait = fetch_weights(weights, weight, weight_sems, step)
    fetch(moves, pieces, held, sems, step)
    wait()
    qkv_w, out_w = head_weights(weight, shard_rows)
    width = out_w.shape[1]
    all_mixed = dot(held[step], out_w, 1, 0).astype(BF)
    made = [[], [], []]
    for low, high in heads_of(width):
        queries, keys, values = (ref[0, :, low:high] for ref in (q_ref, k_ref, v_ref))
        grad_mixed = all_mixed[:, low:high]
        probs = probabilities(queries, keys, mask[0])
        made[2].append(dot(probs.astype(BF), grad_mixed, 0, 0))
        grad_probs = dot(grad_mixed, values, 1, 1)
        delta = jnp.sum(probs * grad_probs, axis=1, keepdims=True)
        grad_scores = (probs * (grad_probs - delta) * (HEAD_DIM**-0.5)).astype(BF)
        made[0].append(turned(dot(grad_scores, keys, 1, 0), cosine[0], -sine[0]))
        made[1].append(turned(dot(grad_scores, queries, 0, 0), cosine[0], -sine[0]))
    grads = jnp.concatenate([part for parts in made for part in parts], axis=1).astype(BF)
    grad_ref[0] = grads
    back = dot(grads, qkv_w, 1, 1).astype(BF)
    half = back.shape[0] // 2
    m_own[0], m_other[0] = back[:half], back[half:]


def attend_back(places, rows_grad, weights, shard_rows, cosine, sine, mask, queries, keys, values):
    arrays, moves = rows_grad
    tokens, width = mask.shape[1], arrays[0].shape[1]
    half = tokens // 2
    outer = len(weights)
    own = weights[0].shape[2] // 4
    made = [jax.ShapeDtypeStruct((GROUP, tokens, 3 * own), BF)]
    made += [jax.ShapeDtypeStruct((GROUP, half, width), BF)] * 2
    return pl.pallas_call(
        functools.partial(attend_back_kernel, moves, shard_rows, outer),
        grid_spec=pltpu.PrefetchScalarGridSpec(
            num_scalar_prefetch=1,
            grid=(GROUP,),
            in_specs=row_specs(tokens)
            + [stepped(tokens, own)] * 3
            + [ANYWHERE] * (outer + len(arrays)),
            out_specs=[stepped(tokens, 3 * own)] + [stepped(half, width)] * 2,
            scratch_shapes=[
                pltpu.VMEM((GROUP, tokens, width), BF),
                pltpu.VMEM((outer * GROUP, *weights[0].shape[1:]), BF),
                pltpu.SemaphoreType.DMA((len(arrays),)),
                pltpu.SemaphoreType.DMA((outer,)),
            ],
        ),
        out_shape=made,
        compiler_params=params(),
        cost_estimate=pl.CostEstimate(
            flops=2 * GROUP * tokens * (width * 4 + 5 * tokens) * own,
            bytes_accessed=4 * GROUP * tokens * width,
            transcendentals=GROUP * tokens * tokens,
        ),
        name="attend_back",
    )(places, cosine, sine, mask, queries, keys, values, *weights, *arrays)


def doc_layout(lengths, positions):
    docs = jnp.arange(lengths.shape[1], dtype=jnp.int32)
    ends_at = jnp.sum(
        jnp.where(docs[None, None, :] <= docs[None, :, None], lengths[:, None, :], 0),
        axis=2,
        dtype=jnp.int32,
    )
    passed = positions[None, :, None] >= ends_at[:, None, :]
    segment = jnp.sum(passed.astype(jnp.int32), axis=2, dtype=jnp.int32)
    doc_start = jnp.sum(jnp.where(passed, lengths[:, None, :], 0), axis=2, dtype=jnp.int32)
    offset = (positions[None, :] - doc_start).astype(F32)
    allowed = (segment[:, :, None] == segment[:, None, :]) & (
        positions[None, :, None] >= positions[None, None, :]
    )
    half_dim = HEAD_DIM // 2
    inverse = jnp.exp(
        jnp.arange(half_dim, dtype=F32) * (-2.0 * math.log(10000.0) / HEAD_DIM)
    )
    angles = offset[:, :, None] * inverse
    cosine, sine = jnp.cos(angles), jnp.sin(angles)
    return (
        allowed.astype(BF),
        jnp.concatenate([cosine, cosine], axis=2),
        jnp.concatenate([-sine, sine], axis=2),
    )


def rms_scale(values):
    return lax.rsqrt(jnp.mean(values * values, axis=-1, keepdims=True) + EPS_NORM)


def norm_back(grad_normed, normed, scale):
    return scale * (
        grad_normed - normed * jnp.mean(grad_normed * normed, axis=-1, keepdims=True)
    )


def shards(
    tokens,
    norm1_gain,
    qkv_weight,
    out_weight,
    norm2_gain,
    gate_up_weight,
    down_weight,
    doc_lengths,
    cotangent,
):
    rows, width = tokens.shape
    place = lax.axis_index("dp")
    core = lax.axis_index("tensor")
    member = place % GROUP
    outer = lax.axis_size("dp") // GROUP
    row_count = 2 * rows
    shard_rows, _, local_width = qkv_weight.shape
    own_width = local_width // GROUP
    own_hidden = gate_up_weight.shape[2] // GROUP
    places = jnp.arange(GROUP, dtype=jnp.int32) ^ member
    order = ring()
    spot = sum(jnp.where(place // GROUP == one, i, 0) for i, one in enumerate(order))
    back = [order[-i % outer] for i in range(outer)]

    def turn(shaped, by):
        twice = jnp.concatenate([shaped, shaped], axis=1)
        return lax.dynamic_slice_in_dim(twice, by, outer, axis=1)

    def rolled(x):
        shaped = x.reshape(rows, outer, width // outer)
        shaped = jnp.stack([shaped[:, one] for one in back], axis=1)
        return turn(shaped, (outer - spot) % outer).reshape(x.shape)

    def unrolled(x):
        shaped = turn(x.reshape(rows, outer, width // outer), spot)
        return jnp.stack([shaped[:, back.index(one)] for one in range(outer)], axis=1).reshape(x.shape)

    gain_one = norm1_gain.astype(F32)[:, None]
    gain_two = norm2_gain.astype(F32)[:, None]

    residual = rolled(tokens).astype(F32)
    scale_one = rms_scale(residual)
    normed_one = residual * scale_one
    blocks_one = gather(normed_one.astype(BF))
    rows_one = part_of(with_other_core(blocks_one), 0, rows)
    qkv_flat = qkv_weight.reshape(shard_rows, 3 * local_width)
    docs = doc_lengths.shape[1]
    note = jnp.pad(doc_lengths.astype(BF), ((0, 15), (0, 4 * own_width - docs)))
    head_own = swap_members(
        plain_call(
            pack_heads_kernel,
            "pack_heads",
            [qkv_flat, out_weight, gain_one, note],
            jax.ShapeDtypeStruct((GROUP, shard_rows + 16, 4 * own_width), BF),
        )
    )
    head_mats = outer_gather(head_own)
    chosen = (jnp.arange(GROUP, dtype=jnp.int32)[None, :] == places[:, None])[:, :, None]
    lengths = jnp.sum(
        jnp.where(chosen, head_own[:, shard_rows, :docs].astype(F32)[None], 0.0), axis=1
    ).astype(jnp.int32)
    positions = (jnp.arange(row_count, dtype=jnp.int32) + rows * core) % row_count
    mask, cosine, sine = doc_layout(lengths, positions)

    gate_up_flat = gate_up_weight.reshape(shard_rows, 2 * GROUP * own_hidden)
    feed_packed = plain_call(
        pack_feed_kernel,
        "pack_feed",
        [gate_up_flat, down_weight, gain_two],
        jax.ShapeDtypeStruct((GROUP, shard_rows, up_to_lanes(3 * own_hidden)), BF),
    )
    feed_own = swap_members(after(feed_packed, blocks_one[1]))
    feed_mats = outer_gather(feed_own)
    cot_own = rolled(cotangent)
    blocks_cot = gather(after(cot_own, blocks_one[3]))
    rows_cot = part_of(with_other_core(blocks_cot), 0, rows)

    a_own, a_other, mixed, queries, keys, values = attend(
        places, rows_one, head_mats, shard_rows, cosine, sine, after(mask, feed_own)
    )
    attn_blocks = after_all(both_cores(a_own, a_other), *blocks_cot[1:3])
    attn = reduce_last(*reduce_first(attn_blocks))
    stream = residual + attn
    scale_two = rms_scale(stream)
    normed_two = stream * scale_two
    blocks_two = gather(after(normed_two.astype(BF), blocks_cot[3], feed_mats[1]))
    rows_two = part_of(with_other_core(blocks_two), 0, rows)

    m_own, m_other, hidden, grads = feed(
        places, feed_mats, rows_two, rows_cot, rows, own_hidden
    )
    down_part = weight_grads(places, rows_cot, hidden, shard_rows, hidden.shape[2])
    down_sums = outer_reduce(down_part)
    first = reduce_first(both_cores(m_own, m_other))
    pair_part = weight_grads(places, rows_two, grads, shard_rows, grads.shape[2])
    pair_sums = outer_reduce(pair_part)
    first = after_all(first, pair_part)
    back_two = reduce_last(*(block[:rows] for block in first))
    mlp_out = reduce_last(*after_all([block[rows:] for block in first], back_two))
    down_got, pair_got = swap_members(down_sums[-1]), swap_members(pair_sums[-1])
    grad_stream = cot_own.astype(F32) + norm_back(back_two, normed_two, scale_two)

    grad_low = grad_stream.astype(BF)
    rows_grad = part_of(with_other_core(gather(grad_low)), 0, rows)
    grad_qkv, m_own, m_other = attend_back(
        places,
        rows_grad,
        head_mats,
        shard_rows,
        cosine,
        sine,
        mask,
        queries,
        keys,
        values,
    )
    head_part = weight_grads(places, rows_grad, mixed, shard_rows, 4 * own_width, 3)
    head_part = weight_grads(
        places, rows_one, grad_qkv, shard_rows, 4 * own_width, 0, head_part
    )
    head_got = swap_members(outer_reduce(head_part)[-1])
    first = reduce_first(after_all(both_cores(m_own, m_other), head_part))
    gate_up_grad, down_grad, gain_two_part = plain_call(
        unpack_feed_kernel,
        "unpack_feed",
        [pair_got, down_got, gate_up_flat, gain_two],
        [
            jax.ShapeDtypeStruct(gate_up_flat.shape, F32),
            jax.ShapeDtypeStruct(down_weight.shape, F32),
            jax.ShapeDtypeStruct((shard_rows, 128), F32),
        ],
    )
    back_one = reduce_last(*first)

    output = unrolled((stream + mlp_out).astype(BF))
    input_grad = unrolled((grad_stream + norm_back(back_one, normed_one, scale_one)).astype(BF))
    qkv_grad, out_grad, gain_one_part = plain_call(
        unpack_heads_kernel,
        "unpack_heads",
        [head_got, qkv_flat, gain_one],
        [
            jax.ShapeDtypeStruct(qkv_flat.shape, F32),
            jax.ShapeDtypeStruct(out_weight.shape, F32),
            jax.ShapeDtypeStruct((shard_rows, 128), F32),
        ],
    )
    gain_two_part, gain_one_part = gain_two_part[:, 0], gain_one_part[:, 0]
    return (
        output,
        input_grad,
        gain_one_part + over_cores(gain_one_part),
        qkv_grad.reshape(qkv_weight.shape),
        out_grad,
        gain_two_part + over_cores(gain_two_part),
        gate_up_grad.reshape(gate_up_weight.shape),
        down_grad,
    )


def solution(mesh):
    placed = (
        P(("dp", "tensor"), None),
        P("dp"),
        P("dp", None, "tensor"),
        P("dp", "tensor"),
        P("dp"),
        P("dp", None, "tensor"),
        P("dp", "tensor"),
        P("dp", None),
        P(("dp", "tensor"), None),
    )
    return jax.shard_map(
        shards,
        mesh=mesh,
        in_specs=placed,
        out_specs=(
            P(("dp", "tensor"), None),
            P(("dp", "tensor"), None),
            P("dp"),
            P("dp", None, "tensor"),
            P("dp", "tensor"),
            P("dp"),
            P("dp", None, "tensor"),
            P("dp", "tensor"),
        ),
        check_vma=False,
    )
```

```python
import functools
import math

import jax
import jax.numpy as jnp
from jax import lax
from jax.experimental import pallas as pl
from jax.experimental.pallas import tpu as pltpu
from jax.sharding import PartitionSpec as P

HEAD_DIM = 128
EPS_NORM = 1e-05
MASKED_SCORE = -1e30
GROUP = 4
X, Y = 1, 2
BF = jnp.bfloat16
F32 = jnp.float32
VMEM_LIMIT = 60 * 2**20


def over_dp(x, bit):
    size = lax.axis_size("dp")
    return lax.ppermute(x, "dp", [(i, i ^ bit) for i in range(size)])


def over_cores(x):
    return lax.ppermute(x, "tensor", [(0, 1), (1, 0)])


def groups():
    size = lax.axis_size("dp")
    return [list(range(first, first + GROUP)) for first in range(0, size, GROUP)]


def ring():
    count = lax.axis_size("dp") // GROUP
    return [*range(0, count, 2)][:1] + [*range(1, count, 2)] + [*range(2, count, 2)][::-1]


def over_ring(x):
    order = ring()
    pairs = zip(order, order[1:] + order[:1])
    return lax.ppermute(
        x, "dp", [(GROUP * a + i, GROUP * b + i) for a, b in pairs for i in range(GROUP)]
    )


def after(x, *others):
    return lax.optimization_barrier((x, *others))[0]


def after_all(arrays, *others):
    return list(lax.optimization_barrier((*arrays, *others)))[: len(arrays)]


def with_other_core(blocks):
    return [array for block in blocks for array in (block, over_cores(block))]


def part_of(pieces, first, rows):
    moves = [(i, first, i // 2, (i % 2) * rows, rows) for i in range(len(pieces))]
    return pieces, tuple(moves)


def gather(own):
    x, y = over_dp(own, X), over_dp(own, Y)
    return [own, x, y, over_dp(x, Y)]


def plus(base, more):
    return (base.astype(F32) + more.astype(F32)).astype(BF)


def both_cores(own, other):
    other = over_cores(other)
    return [plus(own[step], other[step]) for step in range(GROUP)]


def reduce_first(blocks):
    own, x, y, xy = blocks
    return [own, plus(x, over_dp(xy, Y)), y]


def reduce_last(own, x, y):
    terms = [own, over_dp(x, X), over_dp(y, Y)]
    return sum(term.astype(F32) for term in terms)


def swap_members(blocks):
    return lax.all_to_all(
        blocks, "dp", split_axis=0, concat_axis=0, tiled=True, axis_index_groups=groups()
    )


def outer_gather(block):
    blocks = [block]
    for _ in ring()[1:]:
        blocks.append(over_ring(blocks[-1]))
    return blocks


def outer_reduce(part):
    chunks = part.reshape(-1, GROUP, *part.shape[1:])
    got = [over_ring(chunks[1])]
    for k in range(2, chunks.shape[0]):
        got.append(over_ring(plus(got[-1], chunks[k])))
    return got, plus(got[-1], chunks[0])


def dot(left, right, left_dim, right_dim):
    return lax.dot_general(
        left, right, (((left_dim,), (right_dim,)), ((), ())), preferred_element_type=F32
    )


def moves_of(moves, piece_refs, held, sems):
    return [
        (
            step,
            pltpu.make_async_copy(
                piece_refs[index].at[pl.ds(source, rows)],
                held.at[step, pl.ds(row, rows)],
                sems.at[index],
            ),
        )
        for index, source, step, row, rows in moves
    ]


def fetch(moves, piece_refs, held, sems, step):
    copies = moves_of(moves, piece_refs, held, sems)

    @pl.when(step == 0)
    def _():
        for _, copy in copies:
            copy.start()

    for index in range(GROUP):

        @pl.when(step == index)
        def _():
            for at, copy in copies:
                if at == index:
                    copy.wait()


def turned(values, cosine, sine):
    return values * cosine + pltpu.roll(values, HEAD_DIM // 2, 1) * sine


def probabilities(queries, keys, mask):
    scores = dot(queries, keys, 1, 1) * (HEAD_DIM**-0.5)
    scores = jnp.where(mask > 0, scores, MASKED_SCORE)
    exps = jnp.exp(scores - jnp.max(scores, axis=1, keepdims=True))
    return exps / jnp.sum(exps, axis=1, keepdims=True)


def params():
    return pltpu.CompilerParams(
        dimension_semantics=("arbitrary",), vmem_limit_bytes=VMEM_LIMIT
    )


def whole(array):
    return pl.BlockSpec(array.shape, lambda step, places: (0,) * array.ndim)


def stepped(*block):
    return pl.BlockSpec((1, *block), lambda step, places: (step,) + (0,) * len(block))


ANYWHERE = pl.BlockSpec(memory_space=pl.ANY)


def up_to_lanes(columns):
    return -(-columns // 128) * 128


def fetch_weights(refs, held, sems, step):
    blocks = refs[0].shape[0]
    copies = [
        pltpu.make_async_copy(ref, held.at[pl.ds(i * blocks, blocks)], sems.at[i])
        for i, ref in enumerate(refs)
    ]

    @pl.when(step == 0)
    def _():
        for copy in copies:
            copy.start()

    def wait():
        @pl.when(step == 0)
        def _():
            for copy in copies:
                copy.wait()

    return wait


def head_weights(held, rows):
    owners, _, columns = held.shape
    cut = columns // 4 * 3
    return (
        held[:, :rows, :cut].reshape(owners * rows, cut),
        held[:, :rows, cut:].reshape(owners * rows, columns - cut),
    )


def heads_of(width):
    return [(i, i + HEAD_DIM) for i in range(0, width, HEAD_DIM)]


def attend_kernel(moves, shard_rows, outer, places, cosine, sine, mask, *refs):
    weights, refs = refs[:outer], refs[outer:]
    count = len(moves)
    pieces, refs = refs[:count], refs[count:]
    a_own, a_other, mixed_ref, q_ref, k_ref, v_ref, held, weight, sems, weight_sems = refs
    step = pl.program_id(0)
    wait = fetch_weights(weights, weight, weight_sems, step)
    fetch(moves, pieces, held, sems, step)
    wait()
    qkv_w, out_w = head_weights(weight, shard_rows)
    projected = dot(held[step], qkv_w, 1, 0)
    width = out_w.shape[1]
    for low, high in heads_of(width):
        queries = turned(projected[:, low:high], cosine[0], sine[0]).astype(BF)
        keys = turned(projected[:, width + low : width + high], cosine[0], sine[0]).astype(BF)
        values = projected[:, 2 * width + low : 2 * width + high].astype(BF)
        q_ref[0, :, low:high], k_ref[0, :, low:high], v_ref[0, :, low:high] = queries, keys, values
        probs = probabilities(queries, keys, mask[0]).astype(BF)
        mixed_ref[0, :, low:high] = dot(probs, values, 1, 0).astype(BF)
    mixed = mixed_ref[0]
    attn = dot(mixed, out_w, 1, 1).astype(BF)
    half = attn.shape[0] // 2
    a_own[0], a_other[0] = attn[:half], attn[half:]


def row_specs(tokens):
    return [stepped(tokens, HEAD_DIM), stepped(tokens, HEAD_DIM), stepped(tokens, tokens)]


def attend(places, rows_one, weights, shard_rows, cosine, sine, mask):
    arrays, moves = rows_one
    tokens, width = mask.shape[1], arrays[0].shape[1]
    half = tokens // 2
    outer = len(weights)
    made = [jax.ShapeDtypeStruct((GROUP, half, width), BF)] * 2
    own = weights[0].shape[2] // 4
    made += [jax.ShapeDtypeStruct((GROUP, tokens, own), BF)] * 4
    return pl.pallas_call(
        functools.partial(attend_kernel, moves, shard_rows, outer),
        grid_spec=pltpu.PrefetchScalarGridSpec(
            num_scalar_prefetch=1,
            grid=(GROUP,),
            in_specs=row_specs(tokens) + [ANYWHERE] * (outer + len(arrays)),
            out_specs=[stepped(half, width)] * 2 + [stepped(tokens, own)] * 4,
            scratch_shapes=[
                pltpu.VMEM((GROUP, tokens, width), BF),
                pltpu.VMEM((outer * GROUP, *weights[0].shape[1:]), BF),
                pltpu.SemaphoreType.DMA((len(arrays),)),
                pltpu.SemaphoreType.DMA((outer,)),
            ],
        ),
        out_shape=made,
        compiler_params=params(),
        cost_estimate=pl.CostEstimate(
            flops=2 * GROUP * tokens * (width * 4 + 2 * tokens) * own,
            bytes_accessed=4 * GROUP * tokens * width,
            transcendentals=GROUP * tokens * tokens,
        ),
        name="attend",
    )(places, cosine, sine, mask, *weights, *arrays)


def feed_kernel(moves, cot_moves, outer, places, *refs):
    weights, refs = refs[:outer], refs[outer:]
    count, cot_count = len(moves), len(cot_moves)
    pieces, cots, refs = refs[:count], refs[count : count + cot_count], refs[count + cot_count :]
    m_own, m_other, y_own, y_other, hidden_ref, grads_ref, *refs = refs
    held, held_cot, weight, sems, cot_sems, weight_sems = refs
    step = pl.program_id(0)
    wait = fetch_weights(weights, weight, weight_sems, step)
    fetch(moves, pieces, held, sems, step)
    fetch(cot_moves, cots, held_cot, cot_sems, step)
    wait()
    width = held.shape[2]
    own = grads_ref.shape[2] // 2
    pair_w = weight[:, :, : 2 * own].reshape(width, 2 * own)
    down_w = weight[:, :, 2 * own : 3 * own].reshape(width, own)
    rows = held[step]
    half = rows.shape[0] // 2
    both = dot(rows, pair_w, 1, 0)
    gate, upper = both[:, :own], both[:, own:]
    grad_hidden = dot(held_cot[step], down_w, 1, 0)
    sigma = 1.0 / (1.0 + jnp.exp(-gate))
    silu = gate * sigma
    hidden = (silu * upper).astype(BF)
    grad_gate = grad_hidden * upper * (sigma * (1.0 + gate * (1.0 - sigma)))
    grads = jnp.concatenate([grad_gate, grad_hidden * silu], axis=1).astype(BF)
    hidden_ref[0, :, :own], grads_ref[0] = hidden, grads
    hidden_ref[0, :, own:] = jnp.zeros((2 * half, hidden_ref.shape[2] - own), BF)
    back = dot(grads, pair_w, 1, 1).astype(BF)
    m_own[0], m_other[0] = back[:half], back[half:]
    out = dot(hidden, down_w, 1, 1).astype(BF)
    y_own[0], y_other[0] = out[:half], out[half:]


def feed(places, weights, rows_two, rows_cot, rows, own):
    (arrays, moves), (cot_arrays, cot_moves) = rows_two, rows_cot
    half, width = rows, arrays[0].shape[1]
    outer = len(weights)
    tokens = 2 * half
    made = [jax.ShapeDtypeStruct((GROUP, half, width), BF)] * 4
    kept = [up_to_lanes(own), 2 * own]
    made += [jax.ShapeDtypeStruct((GROUP, tokens, one), BF) for one in kept]
    return pl.pallas_call(
        functools.partial(feed_kernel, moves, cot_moves, outer),
        grid_spec=pltpu.PrefetchScalarGridSpec(
            num_scalar_prefetch=1,
            grid=(GROUP,),
            in_specs=[ANYWHERE] * (outer + len(arrays) + len(cot_arrays)),
            out_specs=[stepped(half, width)] * 4 + [stepped(tokens, one) for one in kept],
            scratch_shapes=[
                pltpu.VMEM((GROUP, tokens, width), BF),
                pltpu.VMEM((GROUP, tokens, width), BF),
                pltpu.VMEM((outer * GROUP, *weights[0].shape[1:]), BF),
                pltpu.SemaphoreType.DMA((len(arrays),)),
                pltpu.SemaphoreType.DMA((len(cot_arrays),)),
                pltpu.SemaphoreType.DMA((outer,)),
            ],
        ),
        out_shape=made,
        compiler_params=params(),
        cost_estimate=pl.CostEstimate(
            flops=12 * GROUP * tokens * width * own,
            bytes_accessed=8 * GROUP * tokens * width,
            transcendentals=GROUP * tokens * own,
        ),
        name="feed",
    )(places, *weights, *arrays, *cot_arrays)


def grads_kernel(layout, places, *refs):
    count = len(layout)
    pieces, (right, *_, out, held, sems) = refs[:count], refs[count:]
    step = pl.program_id(0)

    @pl.when(step == 0)
    def _():
        copies = moves_of(layout, pieces, held, sems)
        for _, copy in copies:
            copy.start()
        for _, copy in copies:
            copy.wait()

    shards, rows, own = out.shape
    tile = shards * rows
    tokens = held.shape[0] * held.shape[1]
    left = held[:, :, pl.ds(pl.multiple_of(step * tile, 128), tile)].reshape(tokens, tile)
    product = dot(left, right[...].reshape(tokens, own), 0, 0)
    out[...] = product.astype(BF).reshape(shards, rows, own)


def weight_grads(places, pieces, right, shard_rows, columns, at=0, into=None):
    arrays, layout = pieces
    _, tokens, own = right.shape
    width = arrays[0].shape[1]
    tile = 512
    kept = [] if into is None else [into]
    return pl.pallas_call(
        functools.partial(grads_kernel, layout),
        grid_spec=pltpu.PrefetchScalarGridSpec(
            num_scalar_prefetch=1,
            grid=(width // tile,),
            in_specs=[ANYWHERE] * len(arrays) + [whole(right)] + [ANYWHERE] * len(kept),
            out_specs=pl.BlockSpec(
                (tile // shard_rows, shard_rows, own), lambda step, places: (step, 0, at)
            ),
            scratch_shapes=[
                pltpu.VMEM((GROUP, tokens, width), BF),
                pltpu.SemaphoreType.DMA((len(arrays),)),
            ],
        ),
        out_shape=jax.ShapeDtypeStruct((width // shard_rows, shard_rows, columns), BF),
        input_output_aliases={2 + len(arrays): 0} if kept else {},
        compiler_params=params(),
        cost_estimate=pl.CostEstimate(
            flops=2 * GROUP * tokens * width * own,
            bytes_accessed=2 * GROUP * tokens * width,
            transcendentals=0,
        ),
        name="weight_grads",
    )(places, *arrays, right, *kept)


def pack_heads_kernel(qkv, out_weight, gain, note, packed):
    rows, columns = out_weight.shape
    own = columns // GROUP
    for member in range(GROUP):
        for which in range(3):
            first = which * columns + member * own
            part = qkv[:, first : first + own].astype(F32) * gain[...]
            packed[member, :rows, which * own : (which + 1) * own] = part.astype(BF)
        packed[member, :rows, 3 * own :] = out_weight[:, member * own : (member + 1) * own]
        packed[member, rows:, :] = note[...]


def pack_feed_kernel(gate_up, down, gain, packed):
    rows, columns = down.shape
    own = columns // GROUP
    for member in range(GROUP):
        for which in range(2):
            first = which * columns + member * own
            part = (gate_up[:, first : first + own].astype(F32) * gain[...]).astype(BF)
            packed[member, :, which * own : (which + 1) * own] = part
        packed[member, :, 2 * own : 3 * own] = down[:, member * own : (member + 1) * own]
        packed[member, :, 3 * own :] = jnp.zeros((rows, packed.shape[2] - 3 * own), BF)


def gained(gain_ref, sums):
    gain_ref[...] = jnp.broadcast_to(sum(sums), gain_ref.shape)


def unpack_heads_kernel(got, qkv, gain, qkv_ref, out_ref, gain_ref):
    columns = out_ref.shape[1]
    own = columns // GROUP
    sums = []
    for member in range(GROUP):
        total = got[member].astype(F32)
        for which in range(3):
            first = which * columns + member * own
            part = total[:, which * own : (which + 1) * own]
            sums.append(jnp.sum(qkv[:, first : first + own].astype(F32) * part, axis=1, keepdims=True))
            qkv_ref[:, first : first + own] = part * gain[...]
        out_ref[:, member * own : (member + 1) * own] = total[:, 3 * own :]
    gained(gain_ref, sums)


def unpack_feed_kernel(got, got_down, gate_up, gain, gate_up_ref, down_ref, gain_ref):
    columns = down_ref.shape[1]
    own = columns // GROUP
    sums = []
    for member in range(GROUP):
        total = got[member].astype(F32)
        for which in range(2):
            first = which * columns + member * own
            part = total[:, which * own : (which + 1) * own]
            old = gate_up[:, first : first + own].astype(F32)
            sums.append(jnp.sum(old * part, axis=1, keepdims=True))
            gate_up_ref[:, first : first + own] = part * gain[...]
        down_ref[:, member * own : (member + 1) * own] = got_down[member, :, :own].astype(F32)
    gained(gain_ref, sums)


def plain_call(kernel, name, arrays, made):
    in_vmem = pl.BlockSpec(memory_space=pltpu.VMEM)
    return pl.pallas_call(
        kernel,
        in_specs=[in_vmem] * len(arrays),
        out_specs=jax.tree.map(lambda _: in_vmem, made),
        out_shape=made,
        compiler_params=pltpu.CompilerParams(vmem_limit_bytes=VMEM_LIMIT),
        name=name,
    )(*arrays)


def attend_back_kernel(
    moves, shard_rows, outer, places, cosine, sine, mask, q_ref, k_ref, v_ref, *refs
):
    weights, refs = refs[:outer], refs[outer:]
    count = len(moves)
    pieces, refs = refs[:count], refs[count:]
    grad_ref, m_own, m_other, held, weight, sems, weight_sems = refs
    step = pl.program_id(0)
    wait = fetch_weights(weights, weight, weight_sems, step)
    fetch(moves, pieces, held, sems, step)
    wait()
    qkv_w, out_w = head_weights(weight, shard_rows)
    width = out_w.shape[1]
    all_mixed = dot(held[step], out_w, 1, 0).astype(BF)
    made = [[], [], []]
    for low, high in heads_of(width):
        queries, keys, values = (ref[0, :, low:high] for ref in (q_ref, k_ref, v_ref))
        grad_mixed = all_mixed[:, low:high]
        probs = probabilities(queries, keys, mask[0])
        made[2].append(dot(probs.astype(BF), grad_mixed, 0, 0))
        grad_probs = dot(grad_mixed, values, 1, 1)
        delta = jnp.sum(probs * grad_probs, axis=1, keepdims=True)
        grad_scores = (probs * (grad_probs - delta) * (HEAD_DIM**-0.5)).astype(BF)
        made[0].append(turned(dot(grad_scores, keys, 1, 0), cosine[0], -sine[0]))
        made[1].append(turned(dot(grad_scores, queries, 0, 0), cosine[0], -sine[0]))
    grads = jnp.concatenate([part for parts in made for part in parts], axis=1).astype(BF)
    grad_ref[0] = grads
    back = dot(grads, qkv_w, 1, 1).astype(BF)
    half = back.shape[0] // 2
    m_own[0], m_other[0] = back[:half], back[half:]


def attend_back(places, rows_grad, weights, shard_rows, cosine, sine, mask, queries, keys, values):
    arrays, moves = rows_grad
    tokens, width = mask.shape[1], arrays[0].shape[1]
    half = tokens // 2
    outer = len(weights)
    own = weights[0].shape[2] // 4
    made = [jax.ShapeDtypeStruct((GROUP, tokens, 3 * own), BF)]
    made += [jax.ShapeDtypeStruct((GROUP, half, width), BF)] * 2
    return pl.pallas_call(
        functools.partial(attend_back_kernel, moves, shard_rows, outer),
        grid_spec=pltpu.PrefetchScalarGridSpec(
            num_scalar_prefetch=1,
            grid=(GROUP,),
            in_specs=row_specs(tokens)
            + [stepped(tokens, own)] * 3
            + [ANYWHERE] * (outer + len(arrays)),
            out_specs=[stepped(tokens, 3 * own)] + [stepped(half, width)] * 2,
            scratch_shapes=[
                pltpu.VMEM((GROUP, tokens, width), BF),
                pltpu.VMEM((outer * GROUP, *weights[0].shape[1:]), BF),
                pltpu.SemaphoreType.DMA((len(arrays),)),
                pltpu.SemaphoreType.DMA((outer,)),
            ],
        ),
        out_shape=made,
        compiler_params=params(),
        cost_estimate=pl.CostEstimate(
            flops=2 * GROUP * tokens * (width * 4 + 5 * tokens) * own,
            bytes_accessed=4 * GROUP * tokens * width,
            transcendentals=GROUP * tokens * tokens,
        ),
        name="attend_back",
    )(places, cosine, sine, mask, queries, keys, values, *weights, *arrays)


def doc_layout(lengths, positions):
    docs = jnp.arange(lengths.shape[1], dtype=jnp.int32)
    ends_at = jnp.sum(
        jnp.where(docs[None, None, :] <= docs[None, :, None], lengths[:, None, :], 0),
        axis=2,
        dtype=jnp.int32,
    )
    passed = positions[None, :, None] >= ends_at[:, None, :]
    segment = jnp.sum(passed.astype(jnp.int32), axis=2, dtype=jnp.int32)
    doc_start = jnp.sum(jnp.where(passed, lengths[:, None, :], 0), axis=2, dtype=jnp.int32)
    offset = (positions[None, :] - doc_start).astype(F32)
    allowed = (segment[:, :, None] == segment[:, None, :]) & (
        positions[None, :, None] >= positions[None, None, :]
    )
    half_dim = HEAD_DIM // 2
    inverse = jnp.exp(
        jnp.arange(half_dim, dtype=F32) * (-2.0 * math.log(10000.0) / HEAD_DIM)
    )
    angles = offset[:, :, None] * inverse
    cosine, sine = jnp.cos(angles), jnp.sin(angles)
    return (
        allowed.astype(BF),
        jnp.concatenate([cosine, cosine], axis=2),
        jnp.concatenate([-sine, sine], axis=2),
    )


def rms_scale(values):
    return lax.rsqrt(jnp.mean(values * values, axis=-1, keepdims=True) + EPS_NORM)


def norm_back(grad_normed, normed, scale):
    return scale * (
        grad_normed - normed * jnp.mean(grad_normed * normed, axis=-1, keepdims=True)
    )


def shards(
    tokens,
    norm1_gain,
    qkv_weight,
    out_weight,
    norm2_gain,
    gate_up_weight,
    down_weight,
    doc_lengths,
    cotangent,
):
    rows, width = tokens.shape
    place = lax.axis_index("dp")
    core = lax.axis_index("tensor")
    member = place % GROUP
    outer = lax.axis_size("dp") // GROUP
    row_count = 2 * rows
    shard_rows, _, local_width = qkv_weight.shape
    own_width = local_width // GROUP
    own_hidden = gate_up_weight.shape[2] // GROUP
    places = jnp.arange(GROUP, dtype=jnp.int32) ^ member
    order = ring()
    spot = sum(jnp.where(place // GROUP == one, i, 0) for i, one in enumerate(order))
    back = [order[-i % outer] for i in range(outer)]

    def turn(shaped, by):
        twice = jnp.concatenate([shaped, shaped], axis=1)
        return lax.dynamic_slice_in_dim(twice, by, outer, axis=1)

    def rolled(x):
        shaped = x.reshape(rows, outer, width // outer)
        shaped = jnp.stack([shaped[:, one] for one in back], axis=1)
        return turn(shaped, (outer - spot) % outer).reshape(x.shape)

    def unrolled(x):
        shaped = turn(x.reshape(rows, outer, width // outer), spot)
        return jnp.stack([shaped[:, back.index(one)] for one in range(outer)], axis=1).reshape(x.shape)

    gain_one = norm1_gain.astype(F32)[:, None]
    gain_two = norm2_gain.astype(F32)[:, None]

    residual = rolled(tokens).astype(F32)
    scale_one = rms_scale(residual)
    normed_one = residual * scale_one
    blocks_one = gather(normed_one.astype(BF))
    rows_one = part_of(with_other_core(blocks_one), 0, rows)
    qkv_flat = qkv_weight.reshape(shard_rows, 3 * local_width)
    docs = doc_lengths.shape[1]
    note = jnp.pad(doc_lengths.astype(BF), ((0, 15), (0, 4 * own_width - docs)))
    head_own = swap_members(
        plain_call(
            pack_heads_kernel,
            "pack_heads",
            [qkv_flat, out_weight, gain_one, note],
            jax.ShapeDtypeStruct((GROUP, shard_rows + 16, 4 * own_width), BF),
        )
    )
    head_mats = outer_gather(head_own)
    chosen = (jnp.arange(GROUP, dtype=jnp.int32)[None, :] == places[:, None])[:, :, None]
    lengths = jnp.sum(
        jnp.where(chosen, head_own[:, shard_rows, :docs].astype(F32)[None], 0.0), axis=1
    ).astype(jnp.int32)
    positions = (jnp.arange(row_count, dtype=jnp.int32) + rows * core) % row_count
    mask, cosine, sine = doc_layout(lengths, positions)

    gate_up_flat = gate_up_weight.reshape(shard_rows, 2 * GROUP * own_hidden)
    feed_packed = plain_call(
        pack_feed_kernel,
        "pack_feed",
        [gate_up_flat, down_weight, gain_two],
        jax.ShapeDtypeStruct((GROUP, shard_rows, up_to_lanes(3 * own_hidden)), BF),
    )
    feed_own = swap_members(after(feed_packed, blocks_one[1]))
    feed_mats = outer_gather(feed_own)
    cot_own = rolled(cotangent)
    blocks_cot = gather(after(cot_own, blocks_one[3]))
    rows_cot = part_of(with_other_core(blocks_cot), 0, rows)

    a_own, a_other, mixed, queries, keys, values = attend(
        places, rows_one, head_mats, shard_rows, cosine, sine, after(mask, feed_own)
    )
    attn_blocks = after_all(both_cores(a_own, a_other), *blocks_cot[1:3])
    attn = reduce_last(*reduce_first(attn_blocks))
    stream = residual + attn
    scale_two = rms_scale(stream)
    normed_two = stream * scale_two
    blocks_two = gather(after(normed_two.astype(BF), blocks_cot[3], feed_mats[1]))
    rows_two = part_of(with_other_core(blocks_two), 0, rows)

    m_own, m_other, y_own, y_other, hidden, grads = feed(
        places, feed_mats, rows_two, rows_cot, rows, own_hidden
    )
    down_part = weight_grads(places, rows_cot, hidden, shard_rows, hidden.shape[2])
    down_got, down_sum = outer_reduce(down_part)
    terms = reduce_first(after_all(both_cores(m_own, m_other), down_part))
    pair_part = weight_grads(places, rows_two, grads, shard_rows, grads.shape[2])
    pair_got, pair_sum = outer_reduce(pair_part)
    back_two = reduce_last(*after_all(terms, pair_part, down_got[0]))
    grad_stream = cot_own.astype(F32) + norm_back(back_two, normed_two, scale_two)

    grad_low = after(grad_stream.astype(BF), pair_got[0])
    blocks_grad = gather(grad_low)
    rows_grad = part_of(with_other_core(blocks_grad), 0, rows)
    y_terms = reduce_first(after_all(both_cores(y_own, y_other), blocks_grad[1]))
    grad_qkv, m_own, m_other = attend_back(
        places,
        rows_grad,
        head_mats,
        shard_rows,
        cosine,
        sine,
        after(mask, down_got[1]),
        queries,
        keys,
        values,
    )
    head_part = weight_grads(places, rows_grad, mixed, shard_rows, 4 * own_width, 3)
    head_part = weight_grads(
        places, rows_one, grad_qkv, shard_rows, 4 * own_width, 0, head_part
    )
    _, head_sum = outer_reduce(head_part)
    terms = reduce_first(after_all(both_cores(m_own, m_other), head_part, pair_got[1]))
    down_got, pair_got = swap_members(down_sum), swap_members(pair_sum)
    head_got = swap_members(head_sum)
    mlp_out = reduce_last(*after_all(y_terms, terms[1]))
    gate_up_grad, down_grad, gain_two_part = plain_call(
        unpack_feed_kernel,
        "unpack_feed",
        [pair_got, down_got, gate_up_flat, gain_two],
        [
            jax.ShapeDtypeStruct(gate_up_flat.shape, F32),
            jax.ShapeDtypeStruct(down_weight.shape, F32),
            jax.ShapeDtypeStruct((shard_rows, 128), F32),
        ],
    )
    back_one = reduce_last(*terms)

    output = unrolled((stream + mlp_out).astype(BF))
    input_grad = unrolled((grad_stream + norm_back(back_one, normed_one, scale_one)).astype(BF))
    qkv_grad, out_grad, gain_one_part = plain_call(
        unpack_heads_kernel,
        "unpack_heads",
        [head_got, qkv_flat, gain_one],
        [
            jax.ShapeDtypeStruct(qkv_flat.shape, F32),
            jax.ShapeDtypeStruct(out_weight.shape, F32),
            jax.ShapeDtypeStruct((shard_rows, 128), F32),
        ],
    )
    gain_two_part, gain_one_part = gain_two_part[:, 0], gain_one_part[:, 0]
    return (
        output,
        input_grad,
        gain_one_part + over_cores(gain_one_part),
        qkv_grad.reshape(qkv_weight.shape),
        out_grad,
        gain_two_part + over_cores(gain_two_part),
        gate_up_grad.reshape(gate_up_weight.shape),
        down_grad,
    )


def solution(mesh):
    placed = (
        P(("dp", "tensor"), None),
        P("dp"),
        P("dp", None, "tensor"),
        P("dp", "tensor"),
        P("dp"),
        P("dp", None, "tensor"),
        P("dp", "tensor"),
        P("dp", None),
        P(("dp", "tensor"), None),
    )
    return jax.shard_map(
        shards,
        mesh=mesh,
        in_specs=placed,
        out_specs=(
            P(("dp", "tensor"), None),
            P(("dp", "tensor"), None),
            P("dp"),
            P("dp", None, "tensor"),
            P("dp", "tensor"),
            P("dp"),
            P("dp", None, "tensor"),
            P("dp", "tensor"),
        ),
        check_vma=False,
    )
```

```python
import functools
import math

import jax
import jax.numpy as jnp
from jax import lax
from jax.experimental import pallas as pl
from jax.experimental.pallas import tpu as pltpu
from jax.sharding import PartitionSpec as P

HEAD_DIM = 128
EPS_NORM = 1e-05
MASKED_SCORE = -1e30
GROUP = 4
X, Y = 1, 2
BF = jnp.bfloat16
F32 = jnp.float32
VMEM_LIMIT = 60 * 2**20


def over_dp(x, bit):
    size = lax.axis_size("dp")
    return lax.ppermute(x, "dp", [(i, i ^ bit) for i in range(size)])


def over_cores(x):
    return lax.ppermute(x, "tensor", [(0, 1), (1, 0)])


def groups():
    size = lax.axis_size("dp")
    return [list(range(first, first + GROUP)) for first in range(0, size, GROUP)]


def ring():
    count = lax.axis_size("dp") // GROUP
    return [*range(0, count, 2)][:1] + [*range(1, count, 2)] + [*range(2, count, 2)][::-1]


def over_ring(x):
    order = ring()
    pairs = zip(order, order[1:] + order[:1])
    return lax.ppermute(
        x, "dp", [(GROUP * a + i, GROUP * b + i) for a, b in pairs for i in range(GROUP)]
    )


def after(x, *others):
    return lax.optimization_barrier((x, *others))[0]


def after_all(arrays, *others):
    return list(lax.optimization_barrier((*arrays, *others)))[: len(arrays)]


def with_other_core(blocks):
    return [array for block in blocks for array in (block, over_cores(block))]


def part_of(pieces, first, rows):
    moves = [(i, first, i // 2, (i % 2) * rows, rows) for i in range(len(pieces))]
    return pieces, tuple(moves)


def gather(own):
    x, y = over_dp(own, X), over_dp(own, Y)
    return [own, x, y, over_dp(x, Y)]


def plus(base, more):
    return (base.astype(F32) + more.astype(F32)).astype(BF)


def both_cores(own, other):
    other = over_cores(other)
    return [plus(own[step], other[step]) for step in range(GROUP)]


def reduce_first(blocks):
    own, x, y, xy = blocks
    return [own, plus(x, over_dp(xy, Y)), y]


def reduce_last(own, x, y):
    terms = [own, over_dp(x, X), over_dp(y, Y)]
    return sum(term.astype(F32) for term in terms)


def swap_members(blocks):
    return lax.all_to_all(
        blocks, "dp", split_axis=0, concat_axis=0, tiled=True, axis_index_groups=groups()
    )


def outer_gather(block):
    blocks = [block]
    for _ in ring()[1:]:
        blocks.append(over_ring(blocks[-1]))
    return blocks


def outer_reduce(first, others, waits=()):
    got, sums = [over_ring(first)], []
    for i, chunk in enumerate(others[:-1]):
        sums.append(plus(got[-1], chunk))
        got.append(over_ring(after(sums[-1], waits[i]) if i < len(waits) else sums[-1]))
    return got, [*sums, plus(got[-1], others[-1])]


def dot(left, right, left_dim, right_dim):
    return lax.dot_general(
        left, right, (((left_dim,), (right_dim,)), ((), ())), preferred_element_type=F32
    )


def moves_of(moves, piece_refs, held, sems):
    return [
        (
            step,
            pltpu.make_async_copy(
                piece_refs[index].at[pl.ds(source, rows)],
                held.at[step, pl.ds(row, rows)],
                sems.at[index],
            ),
        )
        for index, source, step, row, rows in moves
    ]


def fetch(moves, piece_refs, held, sems, step):
    copies = moves_of(moves, piece_refs, held, sems)

    @pl.when(step == 0)
    def _():
        for _, copy in copies:
            copy.start()

    for index in range(GROUP):

        @pl.when(step == index)
        def _():
            for at, copy in copies:
                if at == index:
                    copy.wait()


def turned(values, cosine, sine):
    return values * cosine + pltpu.roll(values, HEAD_DIM // 2, 1) * sine


def probabilities(queries, keys, mask):
    scores = dot(queries, keys, 1, 1) * (HEAD_DIM**-0.5)
    scores = jnp.where(mask > 0, scores, MASKED_SCORE)
    exps = jnp.exp(scores - jnp.max(scores, axis=1, keepdims=True))
    return exps / jnp.sum(exps, axis=1, keepdims=True)


def params():
    return pltpu.CompilerParams(
        dimension_semantics=("arbitrary",), vmem_limit_bytes=VMEM_LIMIT
    )


def whole(array):
    return pl.BlockSpec(array.shape, lambda step, places: (0,) * array.ndim)


def stepped(*block):
    return pl.BlockSpec((1, *block), lambda step, places: (step,) + (0,) * len(block))


ANYWHERE = pl.BlockSpec(memory_space=pl.ANY)


def up_to_lanes(columns):
    return -(-columns // 128) * 128


def fetch_weights(refs, held, sems, step):
    blocks = refs[0].shape[0]
    copies = [
        pltpu.make_async_copy(ref, held.at[pl.ds(i * blocks, blocks)], sems.at[i])
        for i, ref in enumerate(refs)
    ]

    @pl.when(step == 0)
    def _():
        for copy in copies:
            copy.start()

    def wait():
        @pl.when(step == 0)
        def _():
            for copy in copies:
                copy.wait()

    return wait


def head_weights(held, rows):
    owners, _, columns = held.shape
    cut = columns // 4 * 3
    return (
        held[:, :rows, :cut].reshape(owners * rows, cut),
        held[:, :rows, cut:].reshape(owners * rows, columns - cut),
    )


def heads_of(width):
    return [(i, i + HEAD_DIM) for i in range(0, width, HEAD_DIM)]


def attend_kernel(moves, shard_rows, outer, places, cosine, sine, mask, *refs):
    weights, refs = refs[:outer], refs[outer:]
    count = len(moves)
    pieces, refs = refs[:count], refs[count:]
    a_own, a_other, mixed_ref, q_ref, k_ref, v_ref, held, weight, sems, weight_sems = refs
    step = pl.program_id(0)
    wait = fetch_weights(weights, weight, weight_sems, step)
    fetch(moves, pieces, held, sems, step)
    wait()
    qkv_w, out_w = head_weights(weight, shard_rows)
    projected = dot(held[step], qkv_w, 1, 0)
    width = out_w.shape[1]
    for low, high in heads_of(width):
        queries = turned(projected[:, low:high], cosine[0], sine[0]).astype(BF)
        keys = turned(projected[:, width + low : width + high], cosine[0], sine[0]).astype(BF)
        values = projected[:, 2 * width + low : 2 * width + high].astype(BF)
        q_ref[0, :, low:high], k_ref[0, :, low:high], v_ref[0, :, low:high] = queries, keys, values
        probs = probabilities(queries, keys, mask[0]).astype(BF)
        mixed_ref[0, :, low:high] = dot(probs, values, 1, 0).astype(BF)
    mixed = mixed_ref[0]
    attn = dot(mixed, out_w, 1, 1).astype(BF)
    half = attn.shape[0] // 2
    a_own[0], a_other[0] = attn[:half], attn[half:]


def row_specs(tokens):
    return [stepped(tokens, HEAD_DIM), stepped(tokens, HEAD_DIM), stepped(tokens, tokens)]


def attend(places, rows_one, weights, shard_rows, cosine, sine, mask):
    arrays, moves = rows_one
    tokens, width = mask.shape[1], arrays[0].shape[1]
    half = tokens // 2
    outer = len(weights)
    made = [jax.ShapeDtypeStruct((GROUP, half, width), BF)] * 2
    own = weights[0].shape[2] // 4
    made += [jax.ShapeDtypeStruct((GROUP, tokens, own), BF)] * 4
    return pl.pallas_call(
        functools.partial(attend_kernel, moves, shard_rows, outer),
        grid_spec=pltpu.PrefetchScalarGridSpec(
            num_scalar_prefetch=1,
            grid=(GROUP,),
            in_specs=row_specs(tokens) + [ANYWHERE] * (outer + len(arrays)),
            out_specs=[stepped(half, width)] * 2 + [stepped(tokens, own)] * 4,
            scratch_shapes=[
                pltpu.VMEM((GROUP, tokens, width), BF),
                pltpu.VMEM((outer * GROUP, *weights[0].shape[1:]), BF),
                pltpu.SemaphoreType.DMA((len(arrays),)),
                pltpu.SemaphoreType.DMA((outer,)),
            ],
        ),
        out_shape=made,
        compiler_params=params(),
        cost_estimate=pl.CostEstimate(
            flops=2 * GROUP * tokens * (width * 4 + 2 * tokens) * own,
            bytes_accessed=4 * GROUP * tokens * width,
            transcendentals=GROUP * tokens * tokens,
        ),
        name="attend",
    )(places, cosine, sine, mask, *weights, *arrays)


def feed_kernel(moves, cot_moves, outer, places, *refs):
    weights, refs = refs[:outer], refs[outer:]
    count, cot_count = len(moves), len(cot_moves)
    pieces, cots, refs = refs[:count], refs[count : count + cot_count], refs[count + cot_count :]
    m_own, m_other, hidden_ref, grads_ref, first_ref, *refs = refs
    held, held_cot, hidden_held, grads_held, weight, sems, cot_sems, weight_sems = refs
    step = pl.program_id(0)
    wait = fetch_weights(weights, weight, weight_sems, step)
    fetch(moves, pieces, held, sems, step)
    fetch(cot_moves, cots, held_cot, cot_sems, step)
    wait()
    width = held.shape[2]
    own = grads_ref.shape[2] // 2
    pair_w = weight[:, :, : 2 * own].reshape(width, 2 * own)
    down_w = weight[:, :, 2 * own : 3 * own].reshape(width, own)
    rows = held[step]
    half = rows.shape[0] // 2
    both = dot(rows, pair_w, 1, 0)
    gate, upper = both[:, :own], both[:, own:]
    grad_hidden = dot(held_cot[step], down_w, 1, 0)
    sigma = 1.0 / (1.0 + jnp.exp(-gate))
    silu = gate * sigma
    hidden = (silu * upper).astype(BF)
    grad_gate = grad_hidden * upper * (sigma * (1.0 + gate * (1.0 - sigma)))
    grads = jnp.concatenate([grad_gate, grad_hidden * silu], axis=1).astype(BF)
    hidden_held[step, :, :own] = hidden
    hidden_held[step, :, own:] = jnp.zeros((2 * half, hidden_ref.shape[2] - own), BF)
    grads_held[step] = grads
    hidden_ref[0], grads_ref[0] = hidden_held[step], grads
    back = dot(grads, pair_w, 1, 1).astype(BF)
    m_own[0], m_other[0] = back[:half], back[half:]

    @pl.when(step == GROUP - 1)
    def _():
        members, shard_rows, _ = first_ref.shape
        wide, tokens = members * shard_rows, GROUP * 2 * half
        column = 0
        for left, right in ((held, grads_held), (held_cot, hidden_held)):
            columns = right.shape[2]
            product = dot(
                left[:, :, wide : 2 * wide].reshape(tokens, wide),
                right[...].reshape(tokens, columns),
                0,
                0,
            )
            first_ref[:, :, column : column + columns] = product.astype(BF).reshape(
                members, shard_rows, columns
            )
            column += columns


def feed(places, weights, rows_two, rows_cot, rows, own):
    (arrays, moves), (cot_arrays, cot_moves) = rows_two, rows_cot
    half, width = rows, arrays[0].shape[1]
    outer = len(weights)
    tokens = 2 * half
    kept = [up_to_lanes(own), 2 * own]
    first = (GROUP, weights[0].shape[1], sum(kept))
    made = [jax.ShapeDtypeStruct((GROUP, half, width), BF)] * 2
    made += [jax.ShapeDtypeStruct((GROUP, tokens, one), BF) for one in kept]
    made += [jax.ShapeDtypeStruct(first, BF)]
    return pl.pallas_call(
        functools.partial(feed_kernel, moves, cot_moves, outer),
        grid_spec=pltpu.PrefetchScalarGridSpec(
            num_scalar_prefetch=1,
            grid=(GROUP,),
            in_specs=[ANYWHERE] * (outer + len(arrays) + len(cot_arrays)),
            out_specs=[stepped(half, width)] * 2
            + [stepped(tokens, one) for one in kept]
            + [pl.BlockSpec(first, lambda step, places: (0, 0, 0))],
            scratch_shapes=[
                pltpu.VMEM((GROUP, tokens, width), BF),
                pltpu.VMEM((GROUP, tokens, width), BF),
                pltpu.VMEM((GROUP, tokens, kept[0]), BF),
                pltpu.VMEM((GROUP, tokens, kept[1]), BF),
                pltpu.VMEM((outer * GROUP, *weights[0].shape[1:]), BF),
                pltpu.SemaphoreType.DMA((len(arrays),)),
                pltpu.SemaphoreType.DMA((len(cot_arrays),)),
                pltpu.SemaphoreType.DMA((outer,)),
            ],
        ),
        out_shape=made,
        compiler_params=params(),
        cost_estimate=pl.CostEstimate(
            flops=10 * GROUP * tokens * width * own,
            bytes_accessed=6 * GROUP * tokens * width,
            transcendentals=GROUP * tokens * own,
        ),
        name="feed",
    )(places, *weights, *arrays, *cot_arrays)


def feed_out_kernel(first, outer, places, hidden, *refs):
    weights, (y_own, y_other, weight, sems) = refs[:outer], refs[outer:]
    step = pl.program_id(0)
    own = weight.shape[2]
    parts = [ref.at[:, :, pl.ds(first, own)] for ref in weights]
    fetch_weights(parts, weight, sems, step)()
    down_w = weight[...].reshape(y_own.shape[2], own)
    out = dot(hidden[0], down_w, 1, 1).astype(BF)
    half = out.shape[0] // 2
    y_own[0], y_other[0] = out[:half], out[half:]


def feed_out(places, weights, hidden, rows, width, own):
    outer, tokens = len(weights), 2 * rows
    columns = hidden.shape[2]
    return pl.pallas_call(
        functools.partial(feed_out_kernel, 2 * own, outer),
        grid_spec=pltpu.PrefetchScalarGridSpec(
            num_scalar_prefetch=1,
            grid=(GROUP,),
            in_specs=[stepped(tokens, columns)] + [ANYWHERE] * outer,
            out_specs=[stepped(rows, width)] * 2,
            scratch_shapes=[
                pltpu.VMEM((outer * GROUP, weights[0].shape[1], columns), BF),
                pltpu.SemaphoreType.DMA((outer,)),
            ],
        ),
        out_shape=[jax.ShapeDtypeStruct((GROUP, rows, width), BF)] * 2,
        compiler_params=params(),
        cost_estimate=pl.CostEstimate(
            flops=2 * GROUP * tokens * width * own,
            bytes_accessed=4 * GROUP * tokens * width,
            transcendentals=0,
        ),
        name="feed_out",
    )(places, hidden, *weights)


def grads_kernel(all_moves, chunks, count_outs, *refs):
    counts = [1 + max(move[0] for move in moves) for moves in all_moves]
    lefts = []
    for count in counts:
        lefts.append(refs[:count])
        refs = refs[count:]
    rights, refs = refs[: len(lefts)], refs[len(lefts) :]
    outs, (held, sems) = refs[: len(chunks) * count_outs], refs[len(chunks) * count_outs :]
    wide = held.shape[4]
    waits = []
    for i, chunk in enumerate(chunks):
        for part, (pieces, moves) in enumerate(zip(lefts, all_moves)):
            for index, source, step, row, rows in moves:
                copy = pltpu.make_async_copy(
                    pieces[index].at[pl.ds(source, rows), pl.ds(chunk * wide, wide)],
                    held.at[i, part, step, pl.ds(row, rows)],
                    sems.at[i, part, index],
                )
                copy.start()
                waits.append((i, copy))
    for i in range(len(chunks)):
        for at, copy in waits:
            if at == i:
                copy.wait()
        products = []
        for part, right in enumerate(rights):
            tokens, own = right.shape[0] * right.shape[1], right.shape[2]
            product = dot(held[i, part].reshape(tokens, wide), right[...].reshape(tokens, own), 0, 0)
            products.append(product.astype(BF))
        product = products[0] if len(products) == 1 else jnp.concatenate(products, axis=1)
        column = 0
        for out in outs[i * count_outs : (i + 1) * count_outs]:
            members, rows, own = out.shape
            out[...] = product[:, column : column + own].reshape(members, rows, own)
            column += own


def weight_grads(lefts, rights, shard_rows, chunks, widths):
    tokens = rights[0].shape[1]
    wide = GROUP * shard_rows
    in_vmem = pl.BlockSpec(memory_space=pltpu.VMEM)
    pieces = [array for arrays, _ in lefts for array in arrays]
    made = [jax.ShapeDtypeStruct((GROUP, shard_rows, width), BF) for width in widths]
    results = pl.pallas_call(
        functools.partial(grads_kernel, [moves for _, moves in lefts], chunks, len(widths)),
        in_specs=[ANYWHERE] * len(pieces) + [in_vmem] * len(rights),
        out_specs=[in_vmem] * (len(made) * len(chunks)),
        scratch_shapes=[
            pltpu.VMEM((len(chunks), len(lefts), GROUP, tokens, wide), BF),
            pltpu.SemaphoreType.DMA((len(chunks), len(lefts), len(lefts[0][0]))),
        ],
        out_shape=made * len(chunks),
        compiler_params=pltpu.CompilerParams(vmem_limit_bytes=VMEM_LIMIT),
        cost_estimate=pl.CostEstimate(
            flops=2 * GROUP * tokens * wide * len(chunks) * sum(r.shape[2] for r in rights),
            bytes_accessed=2 * GROUP * tokens * wide * len(chunks),
            transcendentals=0,
        ),
        name="weight_grads",
    )(*pieces, *rights)
    return [results[i : i + len(made)] for i in range(0, len(results), len(made))]


def pack_heads_kernel(qkv, out_weight, gain, packed):
    columns = out_weight.shape[1]
    own = columns // GROUP
    for member in range(GROUP):
        for which in range(3):
            first = which * columns + member * own
            part = qkv[:, first : first + own].astype(F32) * gain[...]
            packed[member, :, which * own : (which + 1) * own] = part.astype(BF)
        packed[member, :, 3 * own :] = out_weight[:, member * own : (member + 1) * own]


def pack_feed_kernel(gate_up, down, gain, lengths, packed):
    rows, columns = down.shape
    own = columns // GROUP
    for member in range(GROUP):
        for which in range(2):
            first = which * columns + member * own
            part = (gate_up[:, first : first + own].astype(F32) * gain[...]).astype(BF)
            packed[member, :, which * own : (which + 1) * own] = part
        packed[member, :, 2 * own : 3 * own] = down[:, member * own : (member + 1) * own]
        packed[member, :, 3 * own :] = jnp.broadcast_to(
            lengths[:, : packed.shape[2] - 3 * own], (rows, packed.shape[2] - 3 * own)
        )


def gained(gain_ref, sums):
    gain_ref[...] = jnp.broadcast_to(sum(sums), gain_ref.shape)


def unpack_heads_kernel(got, got_more, qkv, gain, qkv_ref, out_ref, gain_ref):
    columns = out_ref.shape[1]
    own = columns // GROUP
    sums = []
    for member in range(GROUP):
        total = jnp.concatenate([got[member], got_more[member]], axis=1).astype(F32)
        for which in range(3):
            first = which * columns + member * own
            part = total[:, which * own : (which + 1) * own]
            sums.append(jnp.sum(qkv[:, first : first + own].astype(F32) * part, axis=1, keepdims=True))
            qkv_ref[:, first : first + own] = part * gain[...]
        out_ref[:, member * own : (member + 1) * own] = total[:, 3 * own :]
    gained(gain_ref, sums)


def unpack_feed_kernel(got, gate_up, gain, gate_up_ref, down_ref, gain_ref):
    columns = down_ref.shape[1]
    own = columns // GROUP
    sums = []
    for member in range(GROUP):
        total = got[member].astype(F32)
        for which in range(2):
            first = which * columns + member * own
            part = total[:, which * own : (which + 1) * own]
            old = gate_up[:, first : first + own].astype(F32)
            sums.append(jnp.sum(old * part, axis=1, keepdims=True))
            gate_up_ref[:, first : first + own] = part * gain[...]
        down_ref[:, member * own : (member + 1) * own] = total[:, 2 * own : 3 * own]
    gained(gain_ref, sums)


def plain_call(kernel, name, arrays, made):
    in_vmem = pl.BlockSpec(memory_space=pltpu.VMEM)
    return pl.pallas_call(
        kernel,
        in_specs=[in_vmem] * len(arrays),
        out_specs=jax.tree.map(lambda _: in_vmem, made),
        out_shape=made,
        compiler_params=pltpu.CompilerParams(vmem_limit_bytes=VMEM_LIMIT),
        name=name,
    )(*arrays)


def attend_back_kernel(
    moves, shard_rows, outer, places, cosine, sine, mask, q_ref, k_ref, v_ref, *refs
):
    weights, refs = refs[:outer], refs[outer:]
    count = len(moves)
    pieces, refs = refs[:count], refs[count:]
    grad_ref, m_own, m_other, held, weight, sems, weight_sems = refs
    step = pl.program_id(0)
    wait = fetch_weights(weights, weight, weight_sems, step)
    fetch(moves, pieces, held, sems, step)
    wait()
    qkv_w, out_w = head_weights(weight, shard_rows)
    width = out_w.shape[1]
    all_mixed = dot(held[step], out_w, 1, 0).astype(BF)
    made = [[], [], []]
    for low, high in heads_of(width):
        queries, keys, values = (ref[0, :, low:high] for ref in (q_ref, k_ref, v_ref))
        grad_mixed = all_mixed[:, low:high]
        probs = probabilities(queries, keys, mask[0])
        made[2].append(dot(probs.astype(BF), grad_mixed, 0, 0))
        grad_probs = dot(grad_mixed, values, 1, 1)
        delta = jnp.sum(probs * grad_probs, axis=1, keepdims=True)
        grad_scores = (probs * (grad_probs - delta) * (HEAD_DIM**-0.5)).astype(BF)
        made[0].append(turned(dot(grad_scores, keys, 1, 0), cosine[0], -sine[0]))
        made[1].append(turned(dot(grad_scores, queries, 0, 0), cosine[0], -sine[0]))
    grads = jnp.concatenate([part for parts in made for part in parts], axis=1).astype(BF)
    grad_ref[0] = grads
    back = dot(grads, qkv_w, 1, 1).astype(BF)
    half = back.shape[0] // 2
    m_own[0], m_other[0] = back[:half], back[half:]


def attend_back(places, rows_grad, weights, shard_rows, cosine, sine, mask, queries, keys, values):
    arrays, moves = rows_grad
    tokens, width = mask.shape[1], arrays[0].shape[1]
    half = tokens // 2
    outer = len(weights)
    own = weights[0].shape[2] // 4
    made = [jax.ShapeDtypeStruct((GROUP, tokens, 3 * own), BF)]
    made += [jax.ShapeDtypeStruct((GROUP, half, width), BF)] * 2
    return pl.pallas_call(
        functools.partial(attend_back_kernel, moves, shard_rows, outer),
        grid_spec=pltpu.PrefetchScalarGridSpec(
            num_scalar_prefetch=1,
            grid=(GROUP,),
            in_specs=row_specs(tokens)
            + [stepped(tokens, own)] * 3
            + [ANYWHERE] * (outer + len(arrays)),
            out_specs=[stepped(tokens, 3 * own)] + [stepped(half, width)] * 2,
            scratch_shapes=[
                pltpu.VMEM((GROUP, tokens, width), BF),
                pltpu.VMEM((outer * GROUP, *weights[0].shape[1:]), BF),
                pltpu.SemaphoreType.DMA((len(arrays),)),
                pltpu.SemaphoreType.DMA((outer,)),
            ],
        ),
        out_shape=made,
        compiler_params=params(),
        cost_estimate=pl.CostEstimate(
            flops=2 * GROUP * tokens * (width * 4 + 5 * tokens) * own,
            bytes_accessed=4 * GROUP * tokens * width,
            transcendentals=GROUP * tokens * tokens,
        ),
        name="attend_back",
    )(places, cosine, sine, mask, queries, keys, values, *weights, *arrays)


def doc_layout(lengths, positions):
    docs = jnp.arange(lengths.shape[1], dtype=jnp.int32)
    ends_at = jnp.sum(
        jnp.where(docs[None, None, :] <= docs[None, :, None], lengths[:, None, :], 0),
        axis=2,
        dtype=jnp.int32,
    )
    passed = positions[None, :, None] >= ends_at[:, None, :]
    segment = jnp.sum(passed.astype(jnp.int32), axis=2, dtype=jnp.int32)
    doc_start = jnp.sum(jnp.where(passed, lengths[:, None, :], 0), axis=2, dtype=jnp.int32)
    offset = (positions[None, :] - doc_start).astype(F32)
    allowed = (segment[:, :, None] == segment[:, None, :]) & (
        positions[None, :, None] >= positions[None, None, :]
    )
    half_dim = HEAD_DIM // 2
    inverse = jnp.exp(
        jnp.arange(half_dim, dtype=F32) * (-2.0 * math.log(10000.0) / HEAD_DIM)
    )
    angles = offset[:, :, None] * inverse
    cosine, sine = jnp.cos(angles), jnp.sin(angles)
    return (
        allowed.astype(BF),
        jnp.concatenate([cosine, cosine], axis=2),
        jnp.concatenate([-sine, sine], axis=2),
    )


def rms_scale(values):
    return lax.rsqrt(jnp.mean(values * values, axis=-1, keepdims=True) + EPS_NORM)


def norm_back(grad_normed, normed, scale):
    return scale * (
        grad_normed - normed * jnp.mean(grad_normed * normed, axis=-1, keepdims=True)
    )


def shards(
    tokens,
    norm1_gain,
    qkv_weight,
    out_weight,
    norm2_gain,
    gate_up_weight,
    down_weight,
    doc_lengths,
    cotangent,
):
    rows, width = tokens.shape
    place = lax.axis_index("dp")
    core = lax.axis_index("tensor")
    member = place % GROUP
    outer = lax.axis_size("dp") // GROUP
    row_count = 2 * rows
    shard_rows, _, local_width = qkv_weight.shape
    own_width = local_width // GROUP
    own_hidden = gate_up_weight.shape[2] // GROUP
    places = jnp.arange(GROUP, dtype=jnp.int32) ^ member
    order = ring()
    spot = sum(jnp.where(place // GROUP == one, i, 0) for i, one in enumerate(order))
    back = [order[-i % outer] for i in range(outer)]

    def turn(shaped, by):
        twice = jnp.concatenate([shaped, shaped], axis=1)
        return lax.dynamic_slice_in_dim(twice, by, outer, axis=1)

    def rolled(x):
        shaped = x.reshape(rows, outer, width // outer)
        shaped = jnp.stack([shaped[:, one] for one in back], axis=1)
        return turn(shaped, (outer - spot) % outer).reshape(x.shape)

    def unrolled(x):
        shaped = turn(x.reshape(rows, outer, width // outer), spot)
        return jnp.stack([shaped[:, back.index(one)] for one in range(outer)], axis=1).reshape(x.shape)

    gain_one = norm1_gain.astype(F32)[:, None]
    gain_two = norm2_gain.astype(F32)[:, None]

    residual = rolled(tokens).astype(F32)
    scale_one = rms_scale(residual)
    normed_one = residual * scale_one
    qkv_flat = qkv_weight.reshape(shard_rows, 3 * local_width)
    head_packed = plain_call(
        pack_heads_kernel,
        "pack_heads",
        [qkv_flat, out_weight, gain_one],
        jax.ShapeDtypeStruct((GROUP, shard_rows, 4 * own_width), BF),
    )
    head_own = swap_members(head_packed)
    blocks_one = gather(after(normed_one.astype(BF), head_packed))
    rows_one = part_of(with_other_core(blocks_one), 0, rows)
    head_mats = outer_gather(head_own)
    gate_up_flat = gate_up_weight.reshape(shard_rows, 2 * GROUP * own_hidden)
    spare = up_to_lanes(3 * own_hidden) - 3 * own_hidden
    docs = doc_lengths.shape[1]
    assert docs <= spare
    feed_packed = plain_call(
        pack_feed_kernel,
        "pack_feed",
        [
            gate_up_flat,
            down_weight,
            gain_two,
            jnp.pad(doc_lengths.astype(BF), ((0, 0), (0, 128 - docs))),
        ],
        jax.ShapeDtypeStruct((GROUP, shard_rows, 3 * own_hidden + spare), BF),
    )
    feed_own = swap_members(after(feed_packed, blocks_one[3]))
    notes = feed_own[:, 0, 3 * own_hidden : 3 * own_hidden + docs].astype(F32)
    chosen = (jnp.arange(GROUP, dtype=jnp.int32)[None, :] == places[:, None])[:, :, None]
    lengths = jnp.sum(jnp.where(chosen, notes[None], 0.0), axis=1).astype(jnp.int32)
    positions = (jnp.arange(row_count, dtype=jnp.int32) + rows * core) % row_count
    mask, cosine, sine = doc_layout(lengths, positions)
    feed_mats = outer_gather(feed_own)
    cot_own = rolled(cotangent)
    blocks_cot = gather(after(cot_own, blocks_one[3]))
    rows_cot = part_of(with_other_core(blocks_cot), 0, rows)

    a_own, a_other, mixed, queries, keys, values = attend(
        places, rows_one, head_mats, shard_rows, cosine, sine, after(mask, feed_own)
    )
    attn_blocks = after_all(both_cores(a_own, a_other), *blocks_cot[1:3])
    attn = reduce_last(*reduce_first(attn_blocks))
    stream = residual + attn
    scale_two = rms_scale(stream)
    normed_two = stream * scale_two
    blocks_two = gather(after(normed_two.astype(BF), blocks_cot[3], feed_mats[1]))
    rows_two = part_of(with_other_core(blocks_two), 0, rows)

    m_own, m_other, hidden, grads, feed_first = feed(
        places, feed_mats, rows_two, rows_cot, rows, own_hidden
    )
    ones, rest = [1], [*range(2, outer), 0]
    feed_args = [rows_two, rows_cot], [grads, hidden], shard_rows
    widths = [grads.shape[2] + hidden.shape[2]]
    terms = reduce_first(both_cores(m_own, m_other))
    feed_rest = [one for [one] in weight_grads(*feed_args, rest, widths)]
    y_own, y_other = feed_out(
        places, feed_mats, after(hidden, terms[1]), rows, width, own_hidden
    )
    back_two = reduce_last(*after_all(terms, feed_rest[0]))
    feed_got, feed_sums = outer_reduce(feed_first, feed_rest)
    grad_stream = cot_own.astype(F32) + norm_back(back_two, normed_two, scale_two)

    blocks_grad = gather(after(grad_stream.astype(BF), feed_sums[0]))
    rows_grad = part_of(with_other_core(blocks_grad), 0, rows)
    y_terms = reduce_first(after_all(both_cores(y_own, y_other), blocks_grad[1]))
    grad_qkv, m_own, m_other = attend_back(
        places,
        rows_grad,
        head_mats,
        shard_rows,
        cosine,
        sine,
        after(mask, y_terms[1], feed_sums[1]),
        queries,
        keys,
        values,
    )
    head_args = [rows_one, rows_grad], [grad_qkv, mixed], shard_rows
    widths = [2 * own_width] * 2
    [head_first] = weight_grads(*head_args, ones, widths)
    head_args = head_args[0], [after(grad_qkv, *head_first), mixed], shard_rows
    head_rest = weight_grads(*head_args, rest, widths)
    terms = reduce_first(after_all(both_cores(m_own, m_other), *head_first))
    back_one = reduce_last(*terms)
    mlp_out = reduce_last(*after_all(y_terms, terms[1]))
    head_first = after_all(head_first, feed_got[-1])
    head_sums = [
        outer_reduce(one, [chunk[i] for chunk in head_rest], (terms[1], back_one))[1][-1] for i, one in enumerate(head_first)
    ]
    feed_back = swap_members(after(feed_sums[-1], back_one))
    gate_up_grad, down_grad, gain_two_part = plain_call(
        unpack_feed_kernel,
        "unpack_feed",
        [feed_back, gate_up_flat, gain_two],
        [
            jax.ShapeDtypeStruct(gate_up_flat.shape, F32),
            jax.ShapeDtypeStruct(down_weight.shape, F32),
            jax.ShapeDtypeStruct((shard_rows, 128), F32),
        ],
    )

    output = unrolled((stream + mlp_out).astype(BF))
    input_grad = unrolled((grad_stream + norm_back(back_one, normed_one, scale_one)).astype(BF))
    gate_up_grad = gate_up_grad.reshape(gate_up_weight.shape)
    head_got = [swap_members(after(one, feed_back)) for one in head_sums[:1]]
    head_got.append(swap_members(after(head_sums[1], gate_up_grad)))
    qkv_grad, out_grad, gain_one_part = plain_call(
        unpack_heads_kernel,
        "unpack_heads",
        [*head_got, qkv_flat, gain_one],
        [
            jax.ShapeDtypeStruct(qkv_flat.shape, F32),
            jax.ShapeDtypeStruct(out_weight.shape, F32),
            jax.ShapeDtypeStruct((shard_rows, 128), F32),
        ],
    )
    gain_two_part, gain_one_part = gain_two_part[:, 0], gain_one_part[:, 0]
    return (
        output,
        input_grad,
        gain_one_part + over_cores(gain_one_part),
        qkv_grad.reshape(qkv_weight.shape),
        out_grad,
        gain_two_part + over_cores(gain_two_part),
        gate_up_grad,
        down_grad,
    )


def solution(mesh):
    placed = (
        P(("dp", "tensor"), None),
        P("dp"),
        P("dp", None, "tensor"),
        P("dp", "tensor"),
        P("dp"),
        P("dp", None, "tensor"),
        P("dp", "tensor"),
        P("dp", None),
        P(("dp", "tensor"), None),
    )
    return jax.shard_map(
        shards,
        mesh=mesh,
        in_specs=placed,
        out_specs=(
            P(("dp", "tensor"), None),
            P(("dp", "tensor"), None),
            P("dp"),
            P("dp", None, "tensor"),
            P("dp", "tensor"),
            P("dp"),
            P("dp", None, "tensor"),
            P("dp", "tensor"),
        ),
        check_vma=False,
    )
```

```python
import functools
import math

import jax
import jax.numpy as jnp
from jax import lax
from jax.experimental import pallas as pl
from jax.experimental.pallas import tpu as pltpu
from jax.sharding import PartitionSpec as P

HEAD_DIM = 128
EPS_NORM = 1e-05
MASKED_SCORE = -1e30
GROUP = 4
X, Y = 1, 2
BF = jnp.bfloat16
F32 = jnp.float32
VMEM_LIMIT = 60 * 2**20


def over_dp(x, bit):
    size = lax.axis_size("dp")
    return lax.ppermute(x, "dp", [(i, i ^ bit) for i in range(size)])


def over_cores(x):
    return lax.ppermute(x, "tensor", [(0, 1), (1, 0)])


def groups():
    size = lax.axis_size("dp")
    return [list(range(first, first + GROUP)) for first in range(0, size, GROUP)]


def ring():
    count = lax.axis_size("dp") // GROUP
    return [*range(0, count, 2)][:1] + [*range(1, count, 2)] + [*range(2, count, 2)][::-1]


def over_ring(x):
    order = ring()
    pairs = zip(order, order[1:] + order[:1])
    return lax.ppermute(
        x, "dp", [(GROUP * a + i, GROUP * b + i) for a, b in pairs for i in range(GROUP)]
    )


def after(x, *others):
    return lax.optimization_barrier((x, *others))[0]


def after_all(arrays, *others):
    return list(lax.optimization_barrier((*arrays, *others)))[: len(arrays)]


def with_other_core(blocks):
    return [array for block in blocks for array in (block, over_cores(block))]


def part_of(pieces, first, rows):
    moves = [(i, first, i // 2, (i % 2) * rows, rows) for i in range(len(pieces))]
    return pieces, tuple(moves)


def gather(own, *before):
    x, y = over_dp(own, X), over_dp(own, Y)
    return [own, x, y, over_dp(after(x, *before), Y)]


def plus(base, more):
    return (base.astype(F32) + more.astype(F32)).astype(BF)


def both_cores(own, other):
    other = over_cores(other)
    return [plus(own[step], other[step]) for step in range(GROUP)]


def reduce_first(blocks):
    own, x, y, xy = blocks
    return [own, plus(x, over_dp(xy, Y)), y]


def reduce_last(own, x, y):
    terms = [own, over_dp(x, X), over_dp(y, Y)]
    return sum(term.astype(F32) for term in terms)


def swap_members(blocks):
    return lax.all_to_all(
        blocks, "dp", split_axis=0, concat_axis=0, tiled=True, axis_index_groups=groups()
    )


def outer_gather(block):
    blocks = [block]
    for _ in ring()[1:]:
        blocks.append(over_ring(blocks[-1]))
    return blocks


def outer_reduce(first, others, waits=()):
    got, sums = [over_ring(first)], []
    for i, chunk in enumerate(others[:-1]):
        sums.append(plus(got[-1], chunk))
        got.append(over_ring(after(sums[-1], waits[i]) if i < len(waits) else sums[-1]))
    return got, [*sums, plus(got[-1], others[-1])]


def dot(left, right, left_dim, right_dim):
    return lax.dot_general(
        left, right, (((left_dim,), (right_dim,)), ((), ())), preferred_element_type=F32
    )


def moves_of(moves, piece_refs, held, sems):
    return [
        (
            step,
            pltpu.make_async_copy(
                piece_refs[index].at[pl.ds(source, rows)],
                held.at[step, pl.ds(row, rows)],
                sems.at[index],
            ),
        )
        for index, source, step, row, rows in moves
    ]


def fetch(moves, piece_refs, held, sems, step):
    copies = moves_of(moves, piece_refs, held, sems)

    @pl.when(step == 0)
    def _():
        for _, copy in copies:
            copy.start()

    for index in range(GROUP):

        @pl.when(step == index)
        def _():
            for at, copy in copies:
                if at == index:
                    copy.wait()


def turned(values, cosine, sine):
    return values * cosine + pltpu.roll(values, HEAD_DIM // 2, 1) * sine


def probabilities(queries, keys, mask):
    scores = dot(queries, keys, 1, 1) * (HEAD_DIM**-0.5)
    scores = jnp.where(mask > 0, scores, MASKED_SCORE)
    exps = jnp.exp(scores - jnp.max(scores, axis=1, keepdims=True))
    return exps / jnp.sum(exps, axis=1, keepdims=True)


def params():
    return pltpu.CompilerParams(
        dimension_semantics=("arbitrary",), vmem_limit_bytes=VMEM_LIMIT
    )


def whole(array):
    return pl.BlockSpec(array.shape, lambda step, places: (0,) * array.ndim)


def stepped(*block):
    return pl.BlockSpec((1, *block), lambda step, places: (step,) + (0,) * len(block))


ANYWHERE = pl.BlockSpec(memory_space=pl.ANY)


def up_to_lanes(columns):
    return -(-columns // 128) * 128


def fetch_weights(refs, held, sems, step):
    blocks = refs[0].shape[0]
    copies = [
        pltpu.make_async_copy(ref, held.at[pl.ds(i * blocks, blocks)], sems.at[i])
        for i, ref in enumerate(refs)
    ]

    @pl.when(step == 0)
    def _():
        for copy in copies:
            copy.start()

    def wait():
        @pl.when(step == 0)
        def _():
            for copy in copies:
                copy.wait()

    return wait


def head_weights(held, rows):
    owners, _, columns = held.shape
    cut = columns // 4 * 3
    return (
        held[:, :rows, :cut].reshape(owners * rows, cut),
        held[:, :rows, cut:].reshape(owners * rows, columns - cut),
    )


def heads_of(width):
    return [(i, i + HEAD_DIM) for i in range(0, width, HEAD_DIM)]


def attend_kernel(moves, shard_rows, outer, places, cosine, sine, mask, *refs):
    weights, refs = refs[:outer], refs[outer:]
    count = len(moves)
    pieces, refs = refs[:count], refs[count:]
    a_own, a_other, mixed_ref, q_ref, k_ref, v_ref, held, weight, sems, weight_sems = refs
    step = pl.program_id(0)
    wait = fetch_weights(weights, weight, weight_sems, step)
    fetch(moves, pieces, held, sems, step)
    wait()
    qkv_w, out_w = head_weights(weight, shard_rows)
    projected = dot(held[step], qkv_w, 1, 0)
    width = out_w.shape[1]
    for low, high in heads_of(width):
        queries = turned(projected[:, low:high], cosine[0], sine[0]).astype(BF)
        keys = turned(projected[:, width + low : width + high], cosine[0], sine[0]).astype(BF)
        values = projected[:, 2 * width + low : 2 * width + high].astype(BF)
        q_ref[0, :, low:high], k_ref[0, :, low:high], v_ref[0, :, low:high] = queries, keys, values
        probs = probabilities(queries, keys, mask[0]).astype(BF)
        mixed_ref[0, :, low:high] = dot(probs, values, 1, 0).astype(BF)
    mixed = mixed_ref[0]
    attn = dot(mixed, out_w, 1, 1).astype(BF)
    half = attn.shape[0] // 2
    a_own[0], a_other[0] = attn[:half], attn[half:]


def row_specs(tokens):
    return [stepped(tokens, HEAD_DIM), stepped(tokens, HEAD_DIM), stepped(tokens, tokens)]


def attend(places, rows_one, weights, shard_rows, cosine, sine, mask):
    arrays, moves = rows_one
    tokens, width = mask.shape[1], arrays[0].shape[1]
    half = tokens // 2
    outer = len(weights)
    made = [jax.ShapeDtypeStruct((GROUP, half, width), BF)] * 2
    own = weights[0].shape[2] // 4
    made += [jax.ShapeDtypeStruct((GROUP, tokens, own), BF)] * 4
    return pl.pallas_call(
        functools.partial(attend_kernel, moves, shard_rows, outer),
        grid_spec=pltpu.PrefetchScalarGridSpec(
            num_scalar_prefetch=1,
            grid=(GROUP,),
            in_specs=row_specs(tokens) + [ANYWHERE] * (outer + len(arrays)),
            out_specs=[stepped(half, width)] * 2 + [stepped(tokens, own)] * 4,
            scratch_shapes=[
                pltpu.VMEM((GROUP, tokens, width), BF),
                pltpu.VMEM((outer * GROUP, *weights[0].shape[1:]), BF),
                pltpu.SemaphoreType.DMA((len(arrays),)),
                pltpu.SemaphoreType.DMA((outer,)),
            ],
        ),
        out_shape=made,
        compiler_params=params(),
        cost_estimate=pl.CostEstimate(
            flops=2 * GROUP * tokens * (width * 4 + 2 * tokens) * own,
            bytes_accessed=4 * GROUP * tokens * width,
            transcendentals=GROUP * tokens * tokens,
        ),
        name="attend",
    )(places, cosine, sine, mask, *weights, *arrays)


def feed_kernel(moves, cot_moves, outer, places, *refs):
    weights, refs = refs[:outer], refs[outer:]
    count, cot_count = len(moves), len(cot_moves)
    pieces, cots, refs = refs[:count], refs[count : count + cot_count], refs[count + cot_count :]
    m_own, m_other, hidden_ref, grads_ref, first_ref, *refs = refs
    held, held_cot, hidden_held, grads_held, weight, sems, cot_sems, weight_sems = refs
    step = pl.program_id(0)
    wait = fetch_weights(weights, weight, weight_sems, step)
    fetch(moves, pieces, held, sems, step)
    fetch(cot_moves, cots, held_cot, cot_sems, step)
    wait()
    width = held.shape[2]
    own = grads_ref.shape[2] // 2
    pair_w = weight[:, :, : 2 * own].reshape(width, 2 * own)
    down_w = weight[:, :, 2 * own : 3 * own].reshape(width, own)
    rows = held[step]
    half = rows.shape[0] // 2
    both = dot(rows, pair_w, 1, 0)
    gate, upper = both[:, :own], both[:, own:]
    grad_hidden = dot(held_cot[step], down_w, 1, 0)
    sigma = 1.0 / (1.0 + jnp.exp(-gate))
    silu = gate * sigma
    hidden = (silu * upper).astype(BF)
    grad_gate = grad_hidden * upper * (sigma * (1.0 + gate * (1.0 - sigma)))
    grads = jnp.concatenate([grad_gate, grad_hidden * silu], axis=1).astype(BF)
    hidden_held[step, :, :own] = hidden
    hidden_held[step, :, own:] = jnp.zeros((2 * half, hidden_ref.shape[2] - own), BF)
    grads_held[step] = grads
    hidden_ref[0], grads_ref[0] = hidden_held[step], grads
    back = dot(grads, pair_w, 1, 1).astype(BF)
    m_own[0], m_other[0] = back[:half], back[half:]

    @pl.when(step == GROUP - 1)
    def _():
        members, shard_rows, _ = first_ref.shape
        wide, tokens = members * shard_rows, GROUP * 2 * half
        column = 0
        for left, right in ((held, grads_held), (held_cot, hidden_held)):
            columns = right.shape[2]
            product = dot(
                left[:, :, wide : 2 * wide].reshape(tokens, wide),
                right[...].reshape(tokens, columns),
                0,
                0,
            )
            first_ref[:, :, column : column + columns] = product.astype(BF).reshape(
                members, shard_rows, columns
            )
            column += columns


def feed(places, weights, rows_two, rows_cot, rows, own):
    (arrays, moves), (cot_arrays, cot_moves) = rows_two, rows_cot
    half, width = rows, arrays[0].shape[1]
    outer = len(weights)
    tokens = 2 * half
    kept = [up_to_lanes(own), 2 * own]
    first = (GROUP, weights[0].shape[1], sum(kept))
    made = [jax.ShapeDtypeStruct((GROUP, half, width), BF)] * 2
    made += [jax.ShapeDtypeStruct((GROUP, tokens, one), BF) for one in kept]
    made += [jax.ShapeDtypeStruct(first, BF)]
    return pl.pallas_call(
        functools.partial(feed_kernel, moves, cot_moves, outer),
        grid_spec=pltpu.PrefetchScalarGridSpec(
            num_scalar_prefetch=1,
            grid=(GROUP,),
            in_specs=[ANYWHERE] * (outer + len(arrays) + len(cot_arrays)),
            out_specs=[stepped(half, width)] * 2
            + [stepped(tokens, one) for one in kept]
            + [pl.BlockSpec(first, lambda step, places: (0, 0, 0))],
            scratch_shapes=[
                pltpu.VMEM((GROUP, tokens, width), BF),
                pltpu.VMEM((GROUP, tokens, width), BF),
                pltpu.VMEM((GROUP, tokens, kept[0]), BF),
                pltpu.VMEM((GROUP, tokens, kept[1]), BF),
                pltpu.VMEM((outer * GROUP, *weights[0].shape[1:]), BF),
                pltpu.SemaphoreType.DMA((len(arrays),)),
                pltpu.SemaphoreType.DMA((len(cot_arrays),)),
                pltpu.SemaphoreType.DMA((outer,)),
            ],
        ),
        out_shape=made,
        compiler_params=params(),
        cost_estimate=pl.CostEstimate(
            flops=10 * GROUP * tokens * width * own,
            bytes_accessed=6 * GROUP * tokens * width,
            transcendentals=GROUP * tokens * own,
        ),
        name="feed",
    )(places, *weights, *arrays, *cot_arrays)


def feed_out_kernel(first, outer, places, hidden, *refs):
    weights, (y_own, y_other, weight, sems) = refs[:outer], refs[outer:]
    step = pl.program_id(0)
    own = weight.shape[2]
    parts = [ref.at[:, :, pl.ds(first, own)] for ref in weights]
    fetch_weights(parts, weight, sems, step)()
    down_w = weight[...].reshape(y_own.shape[2], own)
    out = dot(hidden[0], down_w, 1, 1).astype(BF)
    half = out.shape[0] // 2
    y_own[0], y_other[0] = out[:half], out[half:]


def feed_out(places, weights, hidden, rows, width, own):
    outer, tokens = len(weights), 2 * rows
    columns = hidden.shape[2]
    return pl.pallas_call(
        functools.partial(feed_out_kernel, 2 * own, outer),
        grid_spec=pltpu.PrefetchScalarGridSpec(
            num_scalar_prefetch=1,
            grid=(GROUP,),
            in_specs=[stepped(tokens, columns)] + [ANYWHERE] * outer,
            out_specs=[stepped(rows, width)] * 2,
            scratch_shapes=[
                pltpu.VMEM((outer * GROUP, weights[0].shape[1], columns), BF),
                pltpu.SemaphoreType.DMA((outer,)),
            ],
        ),
        out_shape=[jax.ShapeDtypeStruct((GROUP, rows, width), BF)] * 2,
        compiler_params=params(),
        cost_estimate=pl.CostEstimate(
            flops=2 * GROUP * tokens * width * own,
            bytes_accessed=4 * GROUP * tokens * width,
            transcendentals=0,
        ),
        name="feed_out",
    )(places, hidden, *weights)


def grads_kernel(all_moves, chunks, count_outs, *refs):
    counts = [1 + max(move[0] for move in moves) for moves in all_moves]
    lefts = []
    for count in counts:
        lefts.append(refs[:count])
        refs = refs[count:]
    rights, refs = refs[: len(lefts)], refs[len(lefts) :]
    outs, (held, sems) = refs[: len(chunks) * count_outs], refs[len(chunks) * count_outs :]
    wide = held.shape[4]
    waits = []
    for i, chunk in enumerate(chunks):
        for part, (pieces, moves) in enumerate(zip(lefts, all_moves)):
            for index, source, step, row, rows in moves:
                copy = pltpu.make_async_copy(
                    pieces[index].at[pl.ds(source, rows), pl.ds(chunk * wide, wide)],
                    held.at[i, part, step, pl.ds(row, rows)],
                    sems.at[i, part, index],
                )
                copy.start()
                waits.append((i, copy))
    for i in range(len(chunks)):
        for at, copy in waits:
            if at == i:
                copy.wait()
        products = []
        for part, right in enumerate(rights):
            tokens, own = right.shape[0] * right.shape[1], right.shape[2]
            product = dot(held[i, part].reshape(tokens, wide), right[...].reshape(tokens, own), 0, 0)
            products.append(product.astype(BF))
        product = products[0] if len(products) == 1 else jnp.concatenate(products, axis=1)
        column = 0
        for out in outs[i * count_outs : (i + 1) * count_outs]:
            members, rows, own = out.shape
            out[...] = product[:, column : column + own].reshape(members, rows, own)
            column += own


def weight_grads(lefts, rights, shard_rows, chunks, widths):
    tokens = rights[0].shape[1]
    wide = GROUP * shard_rows
    in_vmem = pl.BlockSpec(memory_space=pltpu.VMEM)
    pieces = [array for arrays, _ in lefts for array in arrays]
    made = [jax.ShapeDtypeStruct((GROUP, shard_rows, width), BF) for width in widths]
    results = pl.pallas_call(
        functools.partial(grads_kernel, [moves for _, moves in lefts], chunks, len(widths)),
        in_specs=[ANYWHERE] * len(pieces) + [in_vmem] * len(rights),
        out_specs=[in_vmem] * (len(made) * len(chunks)),
        scratch_shapes=[
            pltpu.VMEM((len(chunks), len(lefts), GROUP, tokens, wide), BF),
            pltpu.SemaphoreType.DMA((len(chunks), len(lefts), len(lefts[0][0]))),
        ],
        out_shape=made * len(chunks),
        compiler_params=pltpu.CompilerParams(vmem_limit_bytes=VMEM_LIMIT),
        cost_estimate=pl.CostEstimate(
            flops=2 * GROUP * tokens * wide * len(chunks) * sum(r.shape[2] for r in rights),
            bytes_accessed=2 * GROUP * tokens * wide * len(chunks),
            transcendentals=0,
        ),
        name="weight_grads",
    )(*pieces, *rights)
    return [results[i : i + len(made)] for i in range(0, len(results), len(made))]


def pack_heads_kernel(qkv, out_weight, gain, packed):
    columns = out_weight.shape[1]
    own = columns // GROUP
    for member in range(GROUP):
        for which in range(3):
            first = which * columns + member * own
            part = qkv[:, first : first + own].astype(F32) * gain[...]
            packed[member, :, which * own : (which + 1) * own] = part.astype(BF)
        packed[member, :, 3 * own :] = out_weight[:, member * own : (member + 1) * own]


def pack_feed_kernel(gate_up, down, gain, lengths, packed):
    rows, columns = down.shape
    own = columns // GROUP
    for member in range(GROUP):
        for which in range(2):
            first = which * columns + member * own
            part = (gate_up[:, first : first + own].astype(F32) * gain[...]).astype(BF)
            packed[member, :, which * own : (which + 1) * own] = part
        packed[member, :, 2 * own : 3 * own] = down[:, member * own : (member + 1) * own]
        packed[member, :, 3 * own :] = jnp.broadcast_to(
            lengths[:, : packed.shape[2] - 3 * own], (rows, packed.shape[2] - 3 * own)
        )


def gained(gain_ref, sums):
    gain_ref[...] = jnp.broadcast_to(sum(sums), gain_ref.shape)


def unpack_heads_kernel(got, got_more, qkv, gain, qkv_ref, out_ref, gain_ref):
    columns = out_ref.shape[1]
    own = columns // GROUP
    sums = []
    for member in range(GROUP):
        total = jnp.concatenate([got[member], got_more[member]], axis=1).astype(F32)
        for which in range(3):
            first = which * columns + member * own
            part = total[:, which * own : (which + 1) * own]
            sums.append(jnp.sum(qkv[:, first : first + own].astype(F32) * part, axis=1, keepdims=True))
            qkv_ref[:, first : first + own] = part * gain[...]
        out_ref[:, member * own : (member + 1) * own] = total[:, 3 * own :]
    gained(gain_ref, sums)


def unpack_feed_kernel(got, gate_up, gain, gate_up_ref, down_ref, gain_ref):
    columns = down_ref.shape[1]
    own = columns // GROUP
    sums = []
    for member in range(GROUP):
        total = got[member].astype(F32)
        for which in range(2):
            first = which * columns + member * own
            part = total[:, which * own : (which + 1) * own]
            old = gate_up[:, first : first + own].astype(F32)
            sums.append(jnp.sum(old * part, axis=1, keepdims=True))
            gate_up_ref[:, first : first + own] = part * gain[...]
        down_ref[:, member * own : (member + 1) * own] = total[:, 2 * own : 3 * own]
    gained(gain_ref, sums)


def plain_call(kernel, name, arrays, made):
    in_vmem = pl.BlockSpec(memory_space=pltpu.VMEM)
    return pl.pallas_call(
        kernel,
        in_specs=[in_vmem] * len(arrays),
        out_specs=jax.tree.map(lambda _: in_vmem, made),
        out_shape=made,
        compiler_params=pltpu.CompilerParams(vmem_limit_bytes=VMEM_LIMIT),
        name=name,
    )(*arrays)


def attend_back_kernel(
    moves, shard_rows, outer, places, cosine, sine, mask, q_ref, k_ref, v_ref, *refs
):
    weights, refs = refs[:outer], refs[outer:]
    count = len(moves)
    pieces, refs = refs[:count], refs[count:]
    grad_ref, m_own, m_other, held, weight, sems, weight_sems = refs
    step = pl.program_id(0)
    wait = fetch_weights(weights, weight, weight_sems, step)
    fetch(moves, pieces, held, sems, step)
    wait()
    qkv_w, out_w = head_weights(weight, shard_rows)
    width = out_w.shape[1]
    all_mixed = dot(held[step], out_w, 1, 0).astype(BF)
    made = [[], [], []]
    for low, high in heads_of(width):
        queries, keys, values = (ref[0, :, low:high] for ref in (q_ref, k_ref, v_ref))
        grad_mixed = all_mixed[:, low:high]
        probs = probabilities(queries, keys, mask[0])
        made[2].append(dot(probs.astype(BF), grad_mixed, 0, 0))
        grad_probs = dot(grad_mixed, values, 1, 1)
        delta = jnp.sum(probs * grad_probs, axis=1, keepdims=True)
        grad_scores = (probs * (grad_probs - delta) * (HEAD_DIM**-0.5)).astype(BF)
        made[0].append(turned(dot(grad_scores, keys, 1, 0), cosine[0], -sine[0]))
        made[1].append(turned(dot(grad_scores, queries, 0, 0), cosine[0], -sine[0]))
    grads = jnp.concatenate([part for parts in made for part in parts], axis=1).astype(BF)
    grad_ref[0] = grads
    back = dot(grads, qkv_w, 1, 1).astype(BF)
    half = back.shape[0] // 2
    m_own[0], m_other[0] = back[:half], back[half:]


def attend_back(places, rows_grad, weights, shard_rows, cosine, sine, mask, queries, keys, values):
    arrays, moves = rows_grad
    tokens, width = mask.shape[1], arrays[0].shape[1]
    half = tokens // 2
    outer = len(weights)
    own = weights[0].shape[2] // 4
    made = [jax.ShapeDtypeStruct((GROUP, tokens, 3 * own), BF)]
    made += [jax.ShapeDtypeStruct((GROUP, half, width), BF)] * 2
    return pl.pallas_call(
        functools.partial(attend_back_kernel, moves, shard_rows, outer),
        grid_spec=pltpu.PrefetchScalarGridSpec(
            num_scalar_prefetch=1,
            grid=(GROUP,),
            in_specs=row_specs(tokens)
            + [stepped(tokens, own)] * 3
            + [ANYWHERE] * (outer + len(arrays)),
            out_specs=[stepped(tokens, 3 * own)] + [stepped(half, width)] * 2,
            scratch_shapes=[
                pltpu.VMEM((GROUP, tokens, width), BF),
                pltpu.VMEM((outer * GROUP, *weights[0].shape[1:]), BF),
                pltpu.SemaphoreType.DMA((len(arrays),)),
                pltpu.SemaphoreType.DMA((outer,)),
            ],
        ),
        out_shape=made,
        compiler_params=params(),
        cost_estimate=pl.CostEstimate(
            flops=2 * GROUP * tokens * (width * 4 + 5 * tokens) * own,
            bytes_accessed=4 * GROUP * tokens * width,
            transcendentals=GROUP * tokens * tokens,
        ),
        name="attend_back",
    )(places, cosine, sine, mask, queries, keys, values, *weights, *arrays)


def doc_layout(lengths, positions):
    docs = jnp.arange(lengths.shape[1], dtype=jnp.int32)
    ends_at = jnp.sum(
        jnp.where(docs[None, None, :] <= docs[None, :, None], lengths[:, None, :], 0),
        axis=2,
        dtype=jnp.int32,
    )
    passed = positions[None, :, None] >= ends_at[:, None, :]
    segment = jnp.sum(passed.astype(jnp.int32), axis=2, dtype=jnp.int32)
    doc_start = jnp.sum(jnp.where(passed, lengths[:, None, :], 0), axis=2, dtype=jnp.int32)
    offset = (positions[None, :] - doc_start).astype(F32)
    allowed = (segment[:, :, None] == segment[:, None, :]) & (
        positions[None, :, None] >= positions[None, None, :]
    )
    half_dim = HEAD_DIM // 2
    inverse = jnp.exp(
        jnp.arange(half_dim, dtype=F32) * (-2.0 * math.log(10000.0) / HEAD_DIM)
    )
    angles = offset[:, :, None] * inverse
    cosine, sine = jnp.cos(angles), jnp.sin(angles)
    return (
        allowed.astype(BF),
        jnp.concatenate([cosine, cosine], axis=2),
        jnp.concatenate([-sine, sine], axis=2),
    )


def rms_scale(values):
    return lax.rsqrt(jnp.mean(values * values, axis=-1, keepdims=True) + EPS_NORM)


def norm_back(grad_normed, normed, scale):
    return scale * (
        grad_normed - normed * jnp.mean(grad_normed * normed, axis=-1, keepdims=True)
    )


def shards(
    tokens,
    norm1_gain,
    qkv_weight,
    out_weight,
    norm2_gain,
    gate_up_weight,
    down_weight,
    doc_lengths,
    cotangent,
):
    rows, width = tokens.shape
    place = lax.axis_index("dp")
    core = lax.axis_index("tensor")
    member = place % GROUP
    outer = lax.axis_size("dp") // GROUP
    row_count = 2 * rows
    shard_rows, _, local_width = qkv_weight.shape
    own_width = local_width // GROUP
    own_hidden = gate_up_weight.shape[2] // GROUP
    places = jnp.arange(GROUP, dtype=jnp.int32) ^ member
    order = ring()
    spot = sum(jnp.where(place // GROUP == one, i, 0) for i, one in enumerate(order))
    back = [order[-i % outer] for i in range(outer)]

    def turn(shaped, by):
        twice = jnp.concatenate([shaped, shaped], axis=1)
        return lax.dynamic_slice_in_dim(twice, by, outer, axis=1)

    def rolled(x):
        shaped = x.reshape(rows, outer, width // outer)
        shaped = jnp.stack([shaped[:, one] for one in back], axis=1)
        return turn(shaped, (outer - spot) % outer).reshape(x.shape)

    def unrolled(x):
        shaped = turn(x.reshape(rows, outer, width // outer), spot)
        return jnp.stack([shaped[:, back.index(one)] for one in range(outer)], axis=1).reshape(x.shape)

    gain_one = norm1_gain.astype(F32)[:, None]
    gain_two = norm2_gain.astype(F32)[:, None]

    residual = rolled(tokens).astype(F32)
    scale_one = rms_scale(residual)
    normed_one = residual * scale_one
    qkv_flat = qkv_weight.reshape(shard_rows, 3 * local_width)
    head_packed = plain_call(
        pack_heads_kernel,
        "pack_heads",
        [qkv_flat, out_weight, gain_one],
        jax.ShapeDtypeStruct((GROUP, shard_rows, 4 * own_width), BF),
    )
    head_own = swap_members(head_packed)
    head_mats = outer_gather(head_own)
    blocks_one = gather(normed_one.astype(BF), head_mats[1])
    rows_one = part_of(with_other_core(blocks_one), 0, rows)
    gate_up_flat = gate_up_weight.reshape(shard_rows, 2 * GROUP * own_hidden)
    spare = up_to_lanes(3 * own_hidden) - 3 * own_hidden
    docs = doc_lengths.shape[1]
    assert docs <= spare
    feed_packed = plain_call(
        pack_feed_kernel,
        "pack_feed",
        [
            gate_up_flat,
            down_weight,
            gain_two,
            jnp.pad(doc_lengths.astype(BF), ((0, 0), (0, 128 - docs))),
        ],
        jax.ShapeDtypeStruct((GROUP, shard_rows, 3 * own_hidden + spare), BF),
    )
    feed_own = swap_members(after(feed_packed, blocks_one[1]))
    notes = feed_own[:, 0, 3 * own_hidden : 3 * own_hidden + docs].astype(F32)
    chosen = (jnp.arange(GROUP, dtype=jnp.int32)[None, :] == places[:, None])[:, :, None]
    lengths = jnp.sum(jnp.where(chosen, notes[None], 0.0), axis=1).astype(jnp.int32)
    positions = (jnp.arange(row_count, dtype=jnp.int32) + rows * core) % row_count
    mask, cosine, sine = doc_layout(lengths, positions)
    feed_mats = outer_gather(feed_own)
    cot_own = rolled(cotangent)
    blocks_cot = gather(after(cot_own, blocks_one[3]))
    rows_cot = part_of(with_other_core(blocks_cot), 0, rows)

    a_own, a_other, mixed, queries, keys, values = attend(
        places, rows_one, head_mats, shard_rows, cosine, sine, after(mask, feed_own)
    )
    attn_blocks = after_all(both_cores(a_own, a_other), *blocks_cot[1:3])
    attn = reduce_last(*reduce_first(attn_blocks))
    stream = residual + attn
    scale_two = rms_scale(stream)
    normed_two = stream * scale_two
    blocks_two = gather(after(normed_two.astype(BF), blocks_cot[3], feed_mats[1]))
    rows_two = part_of(with_other_core(blocks_two), 0, rows)

    m_own, m_other, hidden, grads, feed_first = feed(
        places, feed_mats, rows_two, rows_cot, rows, own_hidden
    )
    ones, rest = [1], [*range(2, outer), 0]
    feed_args = [rows_two, rows_cot], [grads, hidden], shard_rows
    widths = [grads.shape[2] + hidden.shape[2]]
    terms = reduce_first(both_cores(m_own, m_other))
    feed_rest = [one for [one] in weight_grads(*feed_args, rest, widths)]
    y_own, y_other = feed_out(
        places, feed_mats, after(hidden, terms[1]), rows, width, own_hidden
    )
    back_two = reduce_last(*after_all(terms, feed_rest[0]))
    feed_got, feed_sums = outer_reduce(feed_first, feed_rest)
    grad_stream = cot_own.astype(F32) + norm_back(back_two, normed_two, scale_two)

    blocks_grad = gather(after(grad_stream.astype(BF), feed_sums[0]))
    rows_grad = part_of(with_other_core(blocks_grad), 0, rows)
    y_terms = reduce_first(after_all(both_cores(y_own, y_other), blocks_grad[1]))
    grad_qkv, m_own, m_other = attend_back(
        places,
        rows_grad,
        head_mats,
        shard_rows,
        cosine,
        sine,
        after(mask, y_terms[1], feed_sums[1]),
        queries,
        keys,
        values,
    )
    head_args = [rows_one, rows_grad], [grad_qkv, mixed], shard_rows
    widths = [2 * own_width] * 2
    [head_first] = weight_grads(*head_args, ones, widths)
    head_args = head_args[0], [after(grad_qkv, *head_first), mixed], shard_rows
    head_rest = weight_grads(*head_args, rest, widths)
    terms = reduce_first(after_all(both_cores(m_own, m_other), *head_first))
    back_one = reduce_last(*terms)
    mlp_out = reduce_last(*after_all(y_terms, terms[1]))
    head_first = after_all(head_first, feed_got[-1])
    head_sums = [
        outer_reduce(one, [chunk[i] for chunk in head_rest], (terms[1], back_one))[1][-1] for i, one in enumerate(head_first)
    ]
    feed_back = swap_members(after(feed_sums[-1], back_one))
    gate_up_grad, down_grad, gain_two_part = plain_call(
        unpack_feed_kernel,
        "unpack_feed",
        [feed_back, gate_up_flat, gain_two],
        [
            jax.ShapeDtypeStruct(gate_up_flat.shape, F32),
            jax.ShapeDtypeStruct(down_weight.shape, F32),
            jax.ShapeDtypeStruct((shard_rows, 128), F32),
        ],
    )

    output = unrolled((stream + mlp_out).astype(BF))
    input_grad = unrolled((grad_stream + norm_back(back_one, normed_one, scale_one)).astype(BF))
    gate_up_grad = gate_up_grad.reshape(gate_up_weight.shape)
    head_got = [swap_members(after(one, feed_back)) for one in head_sums[:1]]
    head_got.append(swap_members(after(head_sums[1], gate_up_grad)))
    qkv_grad, out_grad, gain_one_part = plain_call(
        unpack_heads_kernel,
        "unpack_heads",
        [*head_got, qkv_flat, gain_one],
        [
            jax.ShapeDtypeStruct(qkv_flat.shape, F32),
            jax.ShapeDtypeStruct(out_weight.shape, F32),
            jax.ShapeDtypeStruct((shard_rows, 128), F32),
        ],
    )
    gain_two_part, gain_one_part = gain_two_part[:, 0], gain_one_part[:, 0]
    return (
        output,
        input_grad,
        gain_one_part + over_cores(gain_one_part),
        qkv_grad.reshape(qkv_weight.shape),
        out_grad,
        gain_two_part + over_cores(gain_two_part),
        gate_up_grad,
        down_grad,
    )


def solution(mesh):
    placed = (
        P(("dp", "tensor"), None),
        P("dp"),
        P("dp", None, "tensor"),
        P("dp", "tensor"),
        P("dp"),
        P("dp", None, "tensor"),
        P("dp", "tensor"),
        P("dp", None),
        P(("dp", "tensor"), None),
    )
    return jax.shard_map(
        shards,
        mesh=mesh,
        in_specs=placed,
        out_specs=(
            P(("dp", "tensor"), None),
            P(("dp", "tensor"), None),
            P("dp"),
            P("dp", None, "tensor"),
            P("dp", "tensor"),
            P("dp"),
            P("dp", None, "tensor"),
            P("dp", "tensor"),
        ),
        check_vma=False,
    )
```

```python
import functools
import math

import jax
import jax.numpy as jnp
from jax import lax
from jax.experimental import pallas as pl
from jax.experimental.pallas import tpu as pltpu
from jax.sharding import PartitionSpec as P

HEAD_DIM = 128
EPS_NORM = 1e-05
MASKED_SCORE = -1e30
GROUP = 4
X, Y = 1, 2
BF = jnp.bfloat16
F32 = jnp.float32
VMEM_LIMIT = 60 * 2**20


def over_dp(x, bit):
    size = lax.axis_size("dp")
    return lax.ppermute(x, "dp", [(i, i ^ bit) for i in range(size)])


def over_cores(x):
    return lax.ppermute(x, "tensor", [(0, 1), (1, 0)])


def groups():
    size = lax.axis_size("dp")
    return [list(range(first, first + GROUP)) for first in range(0, size, GROUP)]


def ring():
    count = lax.axis_size("dp") // GROUP
    return [*range(0, count, 2)][:1] + [*range(1, count, 2)] + [*range(2, count, 2)][::-1]


def over_ring(x):
    order = ring()
    pairs = zip(order, order[1:] + order[:1])
    return lax.ppermute(
        x, "dp", [(GROUP * a + i, GROUP * b + i) for a, b in pairs for i in range(GROUP)]
    )


def after(x, *others):
    return lax.optimization_barrier((x, *others))[0]


def after_all(arrays, *others):
    return list(lax.optimization_barrier((*arrays, *others)))[: len(arrays)]


def with_other_core(blocks):
    return [array for block in blocks for array in (block, over_cores(block))]


def part_of(pieces, first, rows):
    moves = [(i, first, i // 2, (i % 2) * rows, rows) for i in range(len(pieces))]
    return pieces, tuple(moves)


def gather(own, *before):
    x, y = over_dp(own, X), over_dp(own, Y)
    return [own, x, y, over_dp(after(x, *before), Y)]


def plus(base, more):
    return (base.astype(F32) + more.astype(F32)).astype(BF)


def both_cores(own, other):
    other = over_cores(other)
    return [plus(own[step], other[step]) for step in range(GROUP)]


def reduce_first(blocks):
    own, x, y, xy = blocks
    return [own, plus(x, over_dp(xy, Y)), y]


def reduce_last(own, x, y):
    terms = [own, over_dp(x, X), over_dp(y, Y)]
    return sum(term.astype(F32) for term in terms)


def swap_members(blocks):
    return lax.all_to_all(
        blocks, "dp", split_axis=0, concat_axis=0, tiled=True, axis_index_groups=groups()
    )


def outer_gather(block):
    blocks = [block]
    for _ in ring()[1:]:
        blocks.append(over_ring(blocks[-1]))
    return blocks


def outer_reduce(first, others, waits=()):
    got, sums = [over_ring(first)], []
    for i, chunk in enumerate(others[:-1]):
        sums.append(plus(got[-1], chunk))
        got.append(over_ring(after(sums[-1], waits[i]) if i < len(waits) else sums[-1]))
    return got, [*sums, plus(got[-1], others[-1])]


def dot(left, right, left_dim, right_dim):
    return lax.dot_general(
        left, right, (((left_dim,), (right_dim,)), ((), ())), preferred_element_type=F32
    )


def moves_of(moves, piece_refs, held, sems):
    return [
        (
            step,
            pltpu.make_async_copy(
                piece_refs[index].at[pl.ds(source, rows)],
                held.at[step, pl.ds(row, rows)],
                sems.at[index],
            ),
        )
        for index, source, step, row, rows in moves
    ]


def fetch(moves, piece_refs, held, sems, step):
    copies = moves_of(moves, piece_refs, held, sems)

    @pl.when(step == 0)
    def _():
        for _, copy in copies:
            copy.start()

    for index in range(GROUP):

        @pl.when(step == index)
        def _():
            for at, copy in copies:
                if at == index:
                    copy.wait()


def turned(values, cosine, sine):
    return values * cosine + pltpu.roll(values, HEAD_DIM // 2, 1) * sine


def probabilities(queries, keys, mask):
    scores = dot(queries, keys, 1, 1) * (HEAD_DIM**-0.5)
    scores = jnp.where(mask > 0, scores, MASKED_SCORE)
    exps = jnp.exp(scores - jnp.max(scores, axis=1, keepdims=True))
    return exps / jnp.sum(exps, axis=1, keepdims=True)


def params():
    return pltpu.CompilerParams(
        dimension_semantics=("arbitrary",), vmem_limit_bytes=VMEM_LIMIT
    )


def whole(array):
    return pl.BlockSpec(array.shape, lambda step, places: (0,) * array.ndim)


def stepped(*block):
    return pl.BlockSpec((1, *block), lambda step, places: (step,) + (0,) * len(block))


ANYWHERE = pl.BlockSpec(memory_space=pl.ANY)


def up_to_lanes(columns):
    return -(-columns // 128) * 128


def fetch_weights(refs, held, sems, step):
    blocks = refs[0].shape[0]
    copies = [
        pltpu.make_async_copy(ref, held.at[pl.ds(i * blocks, blocks)], sems.at[i])
        for i, ref in enumerate(refs)
    ]

    @pl.when(step == 0)
    def _():
        for copy in copies:
            copy.start()

    def wait():
        @pl.when(step == 0)
        def _():
            for copy in copies:
                copy.wait()

    return wait


def head_weights(held, rows):
    owners, _, columns = held.shape
    cut = columns // 4 * 3
    return (
        held[:, :rows, :cut].reshape(owners * rows, cut),
        held[:, :rows, cut:].reshape(owners * rows, columns - cut),
    )


def heads_of(width):
    return [(i, i + HEAD_DIM) for i in range(0, width, HEAD_DIM)]


def attend_kernel(moves, shard_rows, outer, places, cosine, sine, mask, *refs):
    weights, refs = refs[:outer], refs[outer:]
    count = len(moves)
    pieces, refs = refs[:count], refs[count:]
    a_own, a_other, mixed_ref, q_ref, k_ref, v_ref, held, weight, sems, weight_sems = refs
    step = pl.program_id(0)
    wait = fetch_weights(weights, weight, weight_sems, step)
    fetch(moves, pieces, held, sems, step)
    wait()
    qkv_w, out_w = head_weights(weight, shard_rows)
    projected = dot(held[step], qkv_w, 1, 0)
    width = out_w.shape[1]
    for low, high in heads_of(width):
        queries = turned(projected[:, low:high], cosine[0], sine[0]).astype(BF)
        keys = turned(projected[:, width + low : width + high], cosine[0], sine[0]).astype(BF)
        values = projected[:, 2 * width + low : 2 * width + high].astype(BF)
        q_ref[0, :, low:high], k_ref[0, :, low:high], v_ref[0, :, low:high] = queries, keys, values
        probs = probabilities(queries, keys, mask[0]).astype(BF)
        mixed_ref[0, :, low:high] = dot(probs, values, 1, 0).astype(BF)
    mixed = mixed_ref[0]
    attn = dot(mixed, out_w, 1, 1).astype(BF)
    half = attn.shape[0] // 2
    a_own[0], a_other[0] = attn[:half], attn[half:]


def row_specs(tokens):
    return [stepped(tokens, HEAD_DIM), stepped(tokens, HEAD_DIM), stepped(tokens, tokens)]


def attend(places, rows_one, weights, shard_rows, cosine, sine, mask):
    arrays, moves = rows_one
    tokens, width = mask.shape[1], arrays[0].shape[1]
    half = tokens // 2
    outer = len(weights)
    made = [jax.ShapeDtypeStruct((GROUP, half, width), BF)] * 2
    own = weights[0].shape[2] // 4
    made += [jax.ShapeDtypeStruct((GROUP, tokens, own), BF)] * 4
    return pl.pallas_call(
        functools.partial(attend_kernel, moves, shard_rows, outer),
        grid_spec=pltpu.PrefetchScalarGridSpec(
            num_scalar_prefetch=1,
            grid=(GROUP,),
            in_specs=row_specs(tokens) + [ANYWHERE] * (outer + len(arrays)),
            out_specs=[stepped(half, width)] * 2 + [stepped(tokens, own)] * 4,
            scratch_shapes=[
                pltpu.VMEM((GROUP, tokens, width), BF),
                pltpu.VMEM((outer * GROUP, *weights[0].shape[1:]), BF),
                pltpu.SemaphoreType.DMA((len(arrays),)),
                pltpu.SemaphoreType.DMA((outer,)),
            ],
        ),
        out_shape=made,
        compiler_params=params(),
        cost_estimate=pl.CostEstimate(
            flops=2 * GROUP * tokens * (width * 4 + 2 * tokens) * own,
            bytes_accessed=4 * GROUP * tokens * width,
            transcendentals=GROUP * tokens * tokens,
        ),
        name="attend",
    )(places, cosine, sine, mask, *weights, *arrays)


def feed_kernel(moves, cot_moves, outer, places, *refs):
    weights, refs = refs[:outer], refs[outer:]
    count, cot_count = len(moves), len(cot_moves)
    pieces, cots, refs = refs[:count], refs[count : count + cot_count], refs[count + cot_count :]
    m_own, m_other, hidden_ref, grads_ref, first_ref, *refs = refs
    held, held_cot, hidden_held, grads_held, weight, sems, cot_sems, weight_sems = refs
    step = pl.program_id(0)
    wait = fetch_weights(weights, weight, weight_sems, step)
    fetch(moves, pieces, held, sems, step)
    fetch(cot_moves, cots, held_cot, cot_sems, step)
    wait()
    width = held.shape[2]
    own = grads_ref.shape[2] // 2
    pair_w = weight[:, :, : 2 * own].reshape(width, 2 * own)
    down_w = weight[:, :, 2 * own : 3 * own].reshape(width, own)
    rows = held[step]
    half = rows.shape[0] // 2
    both = dot(rows, pair_w, 1, 0)
    gate, upper = both[:, :own], both[:, own:]
    grad_hidden = dot(held_cot[step], down_w, 1, 0)
    sigma = 1.0 / (1.0 + jnp.exp(-gate))
    silu = gate * sigma
    hidden = (silu * upper).astype(BF)
    grad_gate = grad_hidden * upper * (sigma * (1.0 + gate * (1.0 - sigma)))
    grads = jnp.concatenate([grad_gate, grad_hidden * silu], axis=1).astype(BF)
    hidden_held[step, :, :own] = hidden
    hidden_held[step, :, own:] = jnp.zeros((2 * half, hidden_ref.shape[2] - own), BF)
    grads_held[step] = grads
    hidden_ref[0], grads_ref[0] = hidden_held[step], grads
    back = dot(grads, pair_w, 1, 1).astype(BF)
    m_own[0], m_other[0] = back[:half], back[half:]

    @pl.when(step == GROUP - 1)
    def _():
        members, shard_rows, _ = first_ref.shape
        wide, tokens = members * shard_rows, GROUP * 2 * half
        column = 0
        for left, right in ((held, grads_held), (held_cot, hidden_held)):
            columns = right.shape[2]
            product = dot(
                left[:, :, wide : 2 * wide].reshape(tokens, wide),
                right[...].reshape(tokens, columns),
                0,
                0,
            )
            first_ref[:, :, column : column + columns] = product.astype(BF).reshape(
                members, shard_rows, columns
            )
            column += columns


def feed(places, weights, rows_two, rows_cot, rows, own):
    (arrays, moves), (cot_arrays, cot_moves) = rows_two, rows_cot
    half, width = rows, arrays[0].shape[1]
    outer = len(weights)
    tokens = 2 * half
    kept = [up_to_lanes(own), 2 * own]
    first = (GROUP, weights[0].shape[1], sum(kept))
    made = [jax.ShapeDtypeStruct((GROUP, half, width), BF)] * 2
    made += [jax.ShapeDtypeStruct((GROUP, tokens, one), BF) for one in kept]
    made += [jax.ShapeDtypeStruct(first, BF)]
    return pl.pallas_call(
        functools.partial(feed_kernel, moves, cot_moves, outer),
        grid_spec=pltpu.PrefetchScalarGridSpec(
            num_scalar_prefetch=1,
            grid=(GROUP,),
            in_specs=[ANYWHERE] * (outer + len(arrays) + len(cot_arrays)),
            out_specs=[stepped(half, width)] * 2
            + [stepped(tokens, one) for one in kept]
            + [pl.BlockSpec(first, lambda step, places: (0, 0, 0))],
            scratch_shapes=[
                pltpu.VMEM((GROUP, tokens, width), BF),
                pltpu.VMEM((GROUP, tokens, width), BF),
                pltpu.VMEM((GROUP, tokens, kept[0]), BF),
                pltpu.VMEM((GROUP, tokens, kept[1]), BF),
                pltpu.VMEM((outer * GROUP, *weights[0].shape[1:]), BF),
                pltpu.SemaphoreType.DMA((len(arrays),)),
                pltpu.SemaphoreType.DMA((len(cot_arrays),)),
                pltpu.SemaphoreType.DMA((outer,)),
            ],
        ),
        out_shape=made,
        compiler_params=params(),
        cost_estimate=pl.CostEstimate(
            flops=10 * GROUP * tokens * width * own,
            bytes_accessed=6 * GROUP * tokens * width,
            transcendentals=GROUP * tokens * own,
        ),
        name="feed",
    )(places, *weights, *arrays, *cot_arrays)


def feed_out_kernel(first, outer, places, hidden, *refs):
    weights, (y_own, y_other, weight, sems) = refs[:outer], refs[outer:]
    step = pl.program_id(0)
    own = weight.shape[2]
    parts = [ref.at[:, :, pl.ds(first, own)] for ref in weights]
    fetch_weights(parts, weight, sems, step)()
    down_w = weight[...].reshape(y_own.shape[2], own)
    out = dot(hidden[0], down_w, 1, 1).astype(BF)
    half = out.shape[0] // 2
    y_own[0], y_other[0] = out[:half], out[half:]


def feed_out(places, weights, hidden, rows, width, own):
    outer, tokens = len(weights), 2 * rows
    columns = hidden.shape[2]
    return pl.pallas_call(
        functools.partial(feed_out_kernel, 2 * own, outer),
        grid_spec=pltpu.PrefetchScalarGridSpec(
            num_scalar_prefetch=1,
            grid=(GROUP,),
            in_specs=[stepped(tokens, columns)] + [ANYWHERE] * outer,
            out_specs=[stepped(rows, width)] * 2,
            scratch_shapes=[
                pltpu.VMEM((outer * GROUP, weights[0].shape[1], columns), BF),
                pltpu.SemaphoreType.DMA((outer,)),
            ],
        ),
        out_shape=[jax.ShapeDtypeStruct((GROUP, rows, width), BF)] * 2,
        compiler_params=params(),
        cost_estimate=pl.CostEstimate(
            flops=2 * GROUP * tokens * width * own,
            bytes_accessed=4 * GROUP * tokens * width,
            transcendentals=0,
        ),
        name="feed_out",
    )(places, hidden, *weights)


def grads_kernel(all_moves, chunks, count_outs, *refs):
    counts = [1 + max(move[0] for move in moves) for moves in all_moves]
    lefts = []
    for count in counts:
        lefts.append(refs[:count])
        refs = refs[count:]
    rights, refs = refs[: len(lefts)], refs[len(lefts) :]
    outs, (held, sems) = refs[: len(chunks) * count_outs], refs[len(chunks) * count_outs :]
    wide = held.shape[4]
    waits = []
    for i, chunk in enumerate(chunks):
        for part, (pieces, moves) in enumerate(zip(lefts, all_moves)):
            for index, source, step, row, rows in moves:
                copy = pltpu.make_async_copy(
                    pieces[index].at[pl.ds(source, rows), pl.ds(chunk * wide, wide)],
                    held.at[i, part, step, pl.ds(row, rows)],
                    sems.at[i, part, index],
                )
                copy.start()
                waits.append((i, copy))
    for i in range(len(chunks)):
        for at, copy in waits:
            if at == i:
                copy.wait()
        products = []
        for part, right in enumerate(rights):
            tokens, own = right.shape[0] * right.shape[1], right.shape[2]
            product = dot(held[i, part].reshape(tokens, wide), right[...].reshape(tokens, own), 0, 0)
            products.append(product.astype(BF))
        product = products[0] if len(products) == 1 else jnp.concatenate(products, axis=1)
        column = 0
        for out in outs[i * count_outs : (i + 1) * count_outs]:
            members, rows, own = out.shape
            out[...] = product[:, column : column + own].reshape(members, rows, own)
            column += own


def weight_grads(lefts, rights, shard_rows, chunks, widths):
    tokens = rights[0].shape[1]
    wide = GROUP * shard_rows
    in_vmem = pl.BlockSpec(memory_space=pltpu.VMEM)
    pieces = [array for arrays, _ in lefts for array in arrays]
    made = [jax.ShapeDtypeStruct((GROUP, shard_rows, width), BF) for width in widths]
    results = pl.pallas_call(
        functools.partial(grads_kernel, [moves for _, moves in lefts], chunks, len(widths)),
        in_specs=[ANYWHERE] * len(pieces) + [in_vmem] * len(rights),
        out_specs=[in_vmem] * (len(made) * len(chunks)),
        scratch_shapes=[
            pltpu.VMEM((len(chunks), len(lefts), GROUP, tokens, wide), BF),
            pltpu.SemaphoreType.DMA((len(chunks), len(lefts), len(lefts[0][0]))),
        ],
        out_shape=made * len(chunks),
        compiler_params=pltpu.CompilerParams(vmem_limit_bytes=VMEM_LIMIT),
        cost_estimate=pl.CostEstimate(
            flops=2 * GROUP * tokens * wide * len(chunks) * sum(r.shape[2] for r in rights),
            bytes_accessed=2 * GROUP * tokens * wide * len(chunks),
            transcendentals=0,
        ),
        name="weight_grads",
    )(*pieces, *rights)
    return [results[i : i + len(made)] for i in range(0, len(results), len(made))]


def pack_heads_kernel(qkv, out_weight, gain, packed):
    columns = out_weight.shape[1]
    own = columns // GROUP
    for member in range(GROUP):
        for which in range(3):
            first = which * columns + member * own
            part = qkv[:, first : first + own].astype(F32) * gain[...]
            packed[member, :, which * own : (which + 1) * own] = part.astype(BF)
        packed[member, :, 3 * own :] = out_weight[:, member * own : (member + 1) * own]


def pack_feed_kernel(gate_up, down, gain, lengths, packed):
    rows, columns = down.shape
    own = columns // GROUP
    for member in range(GROUP):
        for which in range(2):
            first = which * columns + member * own
            part = (gate_up[:, first : first + own].astype(F32) * gain[...]).astype(BF)
            packed[member, :, which * own : (which + 1) * own] = part
        packed[member, :, 2 * own : 3 * own] = down[:, member * own : (member + 1) * own]
        packed[member, :, 3 * own :] = jnp.broadcast_to(
            lengths[:, : packed.shape[2] - 3 * own], (rows, packed.shape[2] - 3 * own)
        )


def gained(gain_ref, sums):
    gain_ref[...] = jnp.broadcast_to(sum(sums), gain_ref.shape)


def unpack_heads_kernel(got, got_more, qkv, gain, qkv_ref, out_ref, gain_ref):
    columns = out_ref.shape[1]
    own = columns // GROUP
    sums = []
    for member in range(GROUP):
        total = jnp.concatenate([got[member], got_more[member]], axis=1).astype(F32)
        for which in range(3):
            first = which * columns + member * own
            part = total[:, which * own : (which + 1) * own]
            sums.append(jnp.sum(qkv[:, first : first + own].astype(F32) * part, axis=1, keepdims=True))
            qkv_ref[:, first : first + own] = part * gain[...]
        out_ref[:, member * own : (member + 1) * own] = total[:, 3 * own :]
    gained(gain_ref, sums)


def unpack_feed_kernel(got, gate_up, gain, gate_up_ref, down_ref, gain_ref):
    columns = down_ref.shape[1]
    own = columns // GROUP
    sums = []
    for member in range(GROUP):
        total = got[member].astype(F32)
        for which in range(2):
            first = which * columns + member * own
            part = total[:, which * own : (which + 1) * own]
            old = gate_up[:, first : first + own].astype(F32)
            sums.append(jnp.sum(old * part, axis=1, keepdims=True))
            gate_up_ref[:, first : first + own] = part * gain[...]
        down_ref[:, member * own : (member + 1) * own] = total[:, 2 * own : 3 * own]
    gained(gain_ref, sums)


def plain_call(kernel, name, arrays, made):
    in_vmem = pl.BlockSpec(memory_space=pltpu.VMEM)
    return pl.pallas_call(
        kernel,
        in_specs=[in_vmem] * len(arrays),
        out_specs=jax.tree.map(lambda _: in_vmem, made),
        out_shape=made,
        compiler_params=pltpu.CompilerParams(vmem_limit_bytes=VMEM_LIMIT),
        name=name,
    )(*arrays)


def attend_back_kernel(
    moves, shard_rows, outer, places, cosine, sine, mask, q_ref, k_ref, v_ref, *refs
):
    weights, refs = refs[:outer], refs[outer:]
    count = len(moves)
    pieces, refs = refs[:count], refs[count:]
    grad_ref, m_own, m_other, held, weight, sems, weight_sems = refs
    step = pl.program_id(0)
    wait = fetch_weights(weights, weight, weight_sems, step)
    fetch(moves, pieces, held, sems, step)
    wait()
    qkv_w, out_w = head_weights(weight, shard_rows)
    width = out_w.shape[1]
    all_mixed = dot(held[step], out_w, 1, 0).astype(BF)
    made = [[], [], []]
    for low, high in heads_of(width):
        queries, keys, values = (ref[0, :, low:high] for ref in (q_ref, k_ref, v_ref))
        grad_mixed = all_mixed[:, low:high]
        probs = probabilities(queries, keys, mask[0])
        made[2].append(dot(probs.astype(BF), grad_mixed, 0, 0))
        grad_probs = dot(grad_mixed, values, 1, 1)
        delta = jnp.sum(probs * grad_probs, axis=1, keepdims=True)
        grad_scores = (probs * (grad_probs - delta) * (HEAD_DIM**-0.5)).astype(BF)
        made[0].append(turned(dot(grad_scores, keys, 1, 0), cosine[0], -sine[0]))
        made[1].append(turned(dot(grad_scores, queries, 0, 0), cosine[0], -sine[0]))
    grads = jnp.concatenate([part for parts in made for part in parts], axis=1).astype(BF)
    grad_ref[0] = grads
    back = dot(grads, qkv_w, 1, 1).astype(BF)
    half = back.shape[0] // 2
    m_own[0], m_other[0] = back[:half], back[half:]


def attend_back(places, rows_grad, weights, shard_rows, cosine, sine, mask, queries, keys, values):
    arrays, moves = rows_grad
    tokens, width = mask.shape[1], arrays[0].shape[1]
    half = tokens // 2
    outer = len(weights)
    own = weights[0].shape[2] // 4
    made = [jax.ShapeDtypeStruct((GROUP, tokens, 3 * own), BF)]
    made += [jax.ShapeDtypeStruct((GROUP, half, width), BF)] * 2
    return pl.pallas_call(
        functools.partial(attend_back_kernel, moves, shard_rows, outer),
        grid_spec=pltpu.PrefetchScalarGridSpec(
            num_scalar_prefetch=1,
            grid=(GROUP,),
            in_specs=row_specs(tokens)
            + [stepped(tokens, own)] * 3
            + [ANYWHERE] * (outer + len(arrays)),
            out_specs=[stepped(tokens, 3 * own)] + [stepped(half, width)] * 2,
            scratch_shapes=[
                pltpu.VMEM((GROUP, tokens, width), BF),
                pltpu.VMEM((outer * GROUP, *weights[0].shape[1:]), BF),
                pltpu.SemaphoreType.DMA((len(arrays),)),
                pltpu.SemaphoreType.DMA((outer,)),
            ],
        ),
        out_shape=made,
        compiler_params=params(),
        cost_estimate=pl.CostEstimate(
            flops=2 * GROUP * tokens * (width * 4 + 5 * tokens) * own,
            bytes_accessed=4 * GROUP * tokens * width,
            transcendentals=GROUP * tokens * tokens,
        ),
        name="attend_back",
    )(places, cosine, sine, mask, queries, keys, values, *weights, *arrays)


def doc_layout(lengths, positions):
    docs = jnp.arange(lengths.shape[1], dtype=jnp.int32)
    ends_at = jnp.sum(
        jnp.where(docs[None, None, :] <= docs[None, :, None], lengths[:, None, :], 0),
        axis=2,
        dtype=jnp.int32,
    )
    passed = positions[None, :, None] >= ends_at[:, None, :]
    segment = jnp.sum(passed.astype(jnp.int32), axis=2, dtype=jnp.int32)
    doc_start = jnp.sum(jnp.where(passed, lengths[:, None, :], 0), axis=2, dtype=jnp.int32)
    offset = (positions[None, :] - doc_start).astype(F32)
    allowed = (segment[:, :, None] == segment[:, None, :]) & (
        positions[None, :, None] >= positions[None, None, :]
    )
    half_dim = HEAD_DIM // 2
    inverse = jnp.exp(
        jnp.arange(half_dim, dtype=F32) * (-2.0 * math.log(10000.0) / HEAD_DIM)
    )
    angles = offset[:, :, None] * inverse
    cosine, sine = jnp.cos(angles), jnp.sin(angles)
    return (
        allowed.astype(BF),
        jnp.concatenate([cosine, cosine], axis=2),
        jnp.concatenate([-sine, sine], axis=2),
    )


def rms_scale(values):
    return lax.rsqrt(jnp.mean(values * values, axis=-1, keepdims=True) + EPS_NORM)


def norm_back(grad_normed, normed, scale):
    return scale * (
        grad_normed - normed * jnp.mean(grad_normed * normed, axis=-1, keepdims=True)
    )


def shards(
    tokens,
    norm1_gain,
    qkv_weight,
    out_weight,
    norm2_gain,
    gate_up_weight,
    down_weight,
    doc_lengths,
    cotangent,
):
    rows, width = tokens.shape
    place = lax.axis_index("dp")
    core = lax.axis_index("tensor")
    member = place % GROUP
    outer = lax.axis_size("dp") // GROUP
    row_count = 2 * rows
    shard_rows, _, local_width = qkv_weight.shape
    own_width = local_width // GROUP
    own_hidden = gate_up_weight.shape[2] // GROUP
    places = jnp.arange(GROUP, dtype=jnp.int32) ^ member
    order = ring()
    spot = sum(jnp.where(place // GROUP == one, i, 0) for i, one in enumerate(order))
    back = [order[-i % outer] for i in range(outer)]

    def turn(shaped, by):
        twice = jnp.concatenate([shaped, shaped], axis=1)
        return lax.dynamic_slice_in_dim(twice, by, outer, axis=1)

    def rolled(x):
        shaped = x.reshape(rows, outer, width // outer)
        shaped = jnp.stack([shaped[:, one] for one in back], axis=1)
        return turn(shaped, (outer - spot) % outer).reshape(x.shape)

    def unrolled(x):
        shaped = turn(x.reshape(rows, outer, width // outer), spot)
        return jnp.stack([shaped[:, back.index(one)] for one in range(outer)], axis=1).reshape(x.shape)

    gain_one = norm1_gain.astype(F32)[:, None]
    gain_two = norm2_gain.astype(F32)[:, None]

    residual = rolled(tokens).astype(F32)
    scale_one = rms_scale(residual)
    normed_one = residual * scale_one
    qkv_flat = qkv_weight.reshape(shard_rows, 3 * local_width)
    head_packed = plain_call(
        pack_heads_kernel,
        "pack_heads",
        [qkv_flat, out_weight, gain_one],
        jax.ShapeDtypeStruct((GROUP, shard_rows, 4 * own_width), BF),
    )
    head_own = swap_members(head_packed)
    head_mats = outer_gather(head_own)
    blocks_one = gather(normed_one.astype(BF), head_mats[1])
    rows_one = part_of(with_other_core(blocks_one), 0, rows)
    gate_up_flat = gate_up_weight.reshape(shard_rows, 2 * GROUP * own_hidden)
    spare = up_to_lanes(3 * own_hidden) - 3 * own_hidden
    docs = doc_lengths.shape[1]
    assert docs <= spare
    feed_packed = plain_call(
        pack_feed_kernel,
        "pack_feed",
        [
            gate_up_flat,
            down_weight,
            gain_two,
            jnp.pad(doc_lengths.astype(BF), ((0, 0), (0, 128 - docs))),
        ],
        jax.ShapeDtypeStruct((GROUP, shard_rows, 3 * own_hidden + spare), BF),
    )
    feed_own = swap_members(after(feed_packed, blocks_one[1]))
    notes = feed_own[:, 0, 3 * own_hidden : 3 * own_hidden + docs].astype(F32)
    chosen = (jnp.arange(GROUP, dtype=jnp.int32)[None, :] == places[:, None])[:, :, None]
    lengths = jnp.sum(jnp.where(chosen, notes[None], 0.0), axis=1).astype(jnp.int32)
    positions = (jnp.arange(row_count, dtype=jnp.int32) + rows * core) % row_count
    mask, cosine, sine = doc_layout(lengths, positions)
    feed_mats = outer_gather(feed_own)
    cot_own = rolled(cotangent)
    blocks_cot = gather(after(cot_own, blocks_one[3]))
    rows_cot = part_of(with_other_core(blocks_cot), 0, rows)

    a_own, a_other, mixed, queries, keys, values = attend(
        places, rows_one, head_mats, shard_rows, cosine, sine, after(mask, feed_own)
    )
    attn_blocks = after_all(both_cores(a_own, a_other), *blocks_cot[1:3])
    attn = reduce_last(*reduce_first(attn_blocks))
    stream = residual + attn
    scale_two = rms_scale(stream)
    normed_two = stream * scale_two
    blocks_two = gather(after(normed_two.astype(BF), blocks_cot[3], feed_mats[1]))
    rows_two = part_of(with_other_core(blocks_two), 0, rows)

    m_own, m_other, hidden, grads, feed_first = feed(
        places, feed_mats, rows_two, rows_cot, rows, own_hidden
    )
    ones, rest = [1], [*range(2, outer), 0]
    feed_args = [rows_two, rows_cot], [grads, hidden], shard_rows
    widths = [grads.shape[2] + hidden.shape[2]]
    terms = reduce_first(both_cores(m_own, m_other))
    feed_rest = [one for [one] in weight_grads(*feed_args, rest, widths)]
    y_own, y_other = feed_out(
        places, feed_mats, after(hidden, terms[1]), rows, width, own_hidden
    )
    back_two = reduce_last(*after_all(terms, feed_rest[0]))
    feed_got, feed_sums = outer_reduce(feed_first, feed_rest)
    grad_stream = cot_own.astype(F32) + norm_back(back_two, normed_two, scale_two)

    blocks_grad = gather(after(grad_stream.astype(BF), feed_sums[0]))
    rows_grad = part_of(with_other_core(blocks_grad), 0, rows)
    y_terms = reduce_first(after_all(both_cores(y_own, y_other), blocks_grad[1]))
    grad_qkv, m_own, m_other = attend_back(
        places,
        rows_grad,
        head_mats,
        shard_rows,
        cosine,
        sine,
        after(mask, feed_sums[1]),
        queries,
        keys,
        values,
    )
    head_args = [rows_one, rows_grad], [grad_qkv, mixed], shard_rows
    widths = [2 * own_width] * 2
    [head_first] = weight_grads(*head_args, ones, widths)
    head_args = head_args[0], [after(grad_qkv, *head_first, y_terms[1]), mixed], shard_rows
    head_rest = weight_grads(*head_args, rest, widths)
    terms = reduce_first(after_all(both_cores(m_own, m_other), *head_first))
    back_one = reduce_last(*terms)
    mlp_out = reduce_last(*after_all(y_terms, terms[1]))
    head_first = after_all(head_first, feed_got[-1])
    head_sums = [
        outer_reduce(one, [chunk[i] for chunk in head_rest], (terms[1], back_one))[1][-1] for i, one in enumerate(head_first)
    ]
    feed_back = swap_members(after(feed_sums[-1], back_one))
    gate_up_grad, down_grad, gain_two_part = plain_call(
        unpack_feed_kernel,
        "unpack_feed",
        [feed_back, gate_up_flat, gain_two],
        [
            jax.ShapeDtypeStruct(gate_up_flat.shape, F32),
            jax.ShapeDtypeStruct(down_weight.shape, F32),
            jax.ShapeDtypeStruct((shard_rows, 128), F32),
        ],
    )

    output = unrolled((stream + mlp_out).astype(BF))
    input_grad = unrolled((grad_stream + norm_back(back_one, normed_one, scale_one)).astype(BF))
    gate_up_grad = gate_up_grad.reshape(gate_up_weight.shape)
    head_got = [swap_members(after(one, feed_back)) for one in head_sums[:1]]
    head_got.append(swap_members(after(head_sums[1], gate_up_grad)))
    qkv_grad, out_grad, gain_one_part = plain_call(
        unpack_heads_kernel,
        "unpack_heads",
        [*head_got, qkv_flat, gain_one],
        [
            jax.ShapeDtypeStruct(qkv_flat.shape, F32),
            jax.ShapeDtypeStruct(out_weight.shape, F32),
            jax.ShapeDtypeStruct((shard_rows, 128), F32),
        ],
    )
    gain_two_part, gain_one_part = gain_two_part[:, 0], gain_one_part[:, 0]
    return (
        output,
        input_grad,
        gain_one_part + over_cores(gain_one_part),
        qkv_grad.reshape(qkv_weight.shape),
        out_grad,
        gain_two_part + over_cores(gain_two_part),
        gate_up_grad,
        down_grad,
    )


def solution(mesh):
    placed = (
        P(("dp", "tensor"), None),
        P("dp"),
        P("dp", None, "tensor"),
        P("dp", "tensor"),
        P("dp"),
        P("dp", None, "tensor"),
        P("dp", "tensor"),
        P("dp", None),
        P(("dp", "tensor"), None),
    )
    return jax.shard_map(
        shards,
        mesh=mesh,
        in_specs=placed,
        out_specs=(
            P(("dp", "tensor"), None),
            P(("dp", "tensor"), None),
            P("dp"),
            P("dp", None, "tensor"),
            P("dp", "tensor"),
            P("dp"),
            P("dp", None, "tensor"),
            P("dp", "tensor"),
        ),
        check_vma=False,
    )
```
